32 devices in a mesh: dp: 8 (over z, x), seq: 4 (over y, core).
Axes of the slice: x: 2, y: 2, z: 4, core: 2. Of those that a mesh axis runs over, the one named last changes fastest.
Arguments:
- tokens: bfloat16 [16, 1024, 1024], P('dp', 'seq'), may hold values from -6 to 6
- captions: bfloat16 [16, 128, 1024], P('dp'), may hold values from -6 to 6
- caption_lengths: int32 [16], P('dp'), may hold values from 1 to 128, as said below
- cotangent: bfloat16 [16, 1024, 1024], P('dp', 'seq'), may hold values from -6 to 6
- self_gain: bfloat16 [1024], P(('dp', 'seq')), may hold values from 0.5 to 1.5
- self_shift: bfloat16 [1024], P(('dp', 'seq')), may hold values from -3 to 3
- self_in_weight: bfloat16 [1024, 3072], P(('dp', 'seq')), may hold values from -0.1875 to 0.1875
- self_out_weight: bfloat16 [1024, 1024], P(('dp', 'seq')), may hold values from -0.5 to 0.5
- cross_gain: bfloat16 [1024], P(('dp', 'seq')), may hold values from 0.5 to 1.5
- cross_shift: bfloat16 [1024], P(('dp', 'seq')), may hold values from -3 to 3
- cross_query_weight: bfloat16 [1024, 1024], P(('dp', 'seq')), may hold values from -0.1875 to 0.1875
- cross_memory_weight: bfloat16 [1024, 2048], P(('dp', 'seq')), may hold values from -0.1875 to 0.1875
- cross_out_weight: bfloat16 [1024, 1024], P(('dp', 'seq')), may hold values from -0.375 to 0.375
- feed_gain: bfloat16 [1024], P(('dp', 'seq')), may hold values from 0.5 to 1.5
- feed_shift: bfloat16 [1024], P(('dp', 'seq')), may hold values from -3 to 3
- up_weight: bfloat16 [1024, 4096], P(('dp', 'seq')), may hold values from -0.1875 to 0.1875
- up_bias: bfloat16 [4096], P(('dp', 'seq')), may hold values from -3 to 3
- down_weight: bfloat16 [4096, 1024], P(('dp', 'seq')), may hold values from -0.09375 to 0.09375
- down_bias: bfloat16 [1024], P(('dp', 'seq')), may hold values from -3 to 3
Outputs:
- output: bfloat16 [16, 1024, 1024], P('dp', 'seq')
- grad_tokens: float32 [16, 1024, 1024], P('dp', 'seq')
- grad_captions: float32 [16, 128, 1024], P('dp')
- grad_self_gain: float32 [1024], P(('dp', 'seq'))
- grad_self_shift: float32 [1024], P(('dp', 'seq'))
- grad_self_in_weight: float32 [1024, 3072], P(('dp', 'seq'))
- grad_self_out_weight: float32 [1024, 1024], P(('dp', 'seq'))
- grad_cross_gain: float32 [1024], P(('dp', 'seq'))
- grad_cross_shift: float32 [1024], P(('dp', 'seq'))
- grad_cross_query_weight: float32 [1024, 1024], P(('dp', 'seq'))
- grad_cross_memory_weight: float32 [1024, 2048], P(('dp', 'seq'))
- grad_cross_out_weight: float32 [1024, 1024], P(('dp', 'seq'))
- grad_feed_gain: float32 [1024], P(('dp', 'seq'))
- grad_feed_shift: float32 [1024], P(('dp', 'seq'))
- grad_up_weight: float32 [1024, 4096], P(('dp', 'seq'))
- grad_up_bias: float32 [4096], P(('dp', 'seq'))
- grad_down_weight: float32 [4096, 1024], P(('dp', 'seq'))
- grad_down_bias: float32 [1024], P(('dp', 'seq'))
The draws below stay inside these ranges and needn't reach their ends.
Inputs may be any that keep to these rules, and one draw needn't show every extreme that they name: `caption_lengths`: lengths are long-tailed, most of them short; in every draw some item has exactly 128.
All inputs are finite; a program needn't handle non-finite values.
Results may differ from the reference program's by a relative error of at most 0.017.
Values may be sent and summed in bfloat16 or wider, within the bound.
No kernel may reach another device: no remote copies, remote signals or barrier semaphores. Data moves between devices by JAX's collectives and lax.ppermute only.
A program may use at most 256 MiB of HBM per device.

```python
import jax
import jax.numpy as jnp
from jax import lax

D = 1024
HEADS = 16
FF = 4096
SLOTS = 128
SEQ_LEN = 1024
ITEMS = 16


def draw_caption_lengths(key, part):
    key = jax.random.fold_in(key, 7)
    key_power, key_length, key_pick = jax.random.split(key, 3)
    exponent = jax.random.randint(key_power, (ITEMS,), 2, 8)
    ceiling = jnp.minimum(jnp.left_shift(jnp.ones((ITEMS,), jnp.int32), exponent), SLOTS)
    lengths = 1 + jax.random.randint(key_length, (ITEMS,), 0, ceiling)
    chosen = jax.random.randint(key_pick, (), 0, ITEMS)
    return jnp.where(lax.iota(jnp.int32, ITEMS) == chosen, SLOTS, lengths).astype(jnp.int32)


def level_of(own_key, extent, pieces, least, top_value):
    def one(dim, blocks):
        draws = jax.random.uniform(jax.random.fold_in(jax.random.fold_in(own_key, 6), dim), (blocks,), jnp.float32, least / len(pieces), top_value / len(pieces))
        return jnp.repeat(jnp.exp(draws), extent[dim] // blocks).reshape((-1,) + (1,) * (len(extent) - dim - 1))

    gain = one(*pieces[0])
    for cut in pieces[1:]:
        gain = gain * one(*cut)
    return gain


def gaussian(rng, dims, deviation, limit, cuts=(), dtype=jnp.bfloat16):
    gain = level_of(rng, dims, cuts, -0.22, 0.18) if cuts else 1.0
    entries = jax.random.normal(rng, dims, jnp.float32) * deviation * gain
    return jnp.minimum(jnp.maximum(entries, -limit), limit).astype(dtype)


def setup_inputs(seed: int = 0) -> dict:
    streams_of = jax.random.split(jax.random.key(seed), 20)
    return {
        "tokens": gaussian(streams_of[0], (ITEMS, SEQ_LEN, D), 1.0, 6.0, ((0, 8), (1, 4))),
        "captions": gaussian(streams_of[1], (ITEMS, SLOTS, D), 1.0, 6.0, ((0, 8),)),
        "caption_lengths": draw_caption_lengths(jax.random.fold_in(streams_of[19], 71), 0),
        "cotangent": gaussian(streams_of[3], (ITEMS, SEQ_LEN, D), 1.0, 6.0, ((0, 8), (1, 4))),
        "self_gain": jnp.clip(1.0 + 0.1 * jax.random.normal(streams_of[4], (D,), jnp.float32), 0.5, 1.5).astype(jnp.bfloat16),
        "self_shift": gaussian(streams_of[5], (D,), 0.5, 3.0, ((0, 32),)),
        "self_in_weight": gaussian(streams_of[6], (D, 3 * D), D ** -0.5, 0.1875, ((0, 32),)),
        "self_out_weight": gaussian(streams_of[7], (D, D), (D // 8) ** -0.5, 0.5, ((0, 32),)),
        "cross_gain": jnp.clip(1.0 + 0.1 * jax.random.normal(streams_of[8], (D,), jnp.float32), 0.5, 1.5).astype(jnp.bfloat16),
        "cross_shift": gaussian(streams_of[9], (D,), 0.5, 3.0, ((0, 32),)),
        "cross_query_weight": gaussian(streams_of[10], (D, D), D ** -0.5, 0.1875, ((0, 32),)),
        "cross_memory_weight": gaussian(streams_of[11], (D, 2 * D), D ** -0.5, 0.1875, ((0, 32),)),
        "cross_out_weight": gaussian(streams_of[12], (D, D), (D // 4) ** -0.5, 0.375, ((0, 32),)),
        "feed_gain": jnp.clip(1.0 + 0.1 * jax.random.normal(streams_of[13], (D,), jnp.float32), 0.5, 1.5).astype(jnp.bfloat16),
        "feed_shift": gaussian(streams_of[14], (D,), 0.5, 3.0, ((0, 32),)),
        "up_weight": gaussian(streams_of[15], (D, FF), D ** -0.5, 0.1875, ((0, 32),)),
        "up_bias": gaussian(streams_of[16], (FF,), 0.5, 3.0, ((0, 32),)),
        "down_weight": gaussian(streams_of[17], (FF, D), FF ** -0.5, 0.09375, ((0, 32),)),
        "down_bias": gaussian(streams_of[18], (D,), 0.5, 3.0, ((0, 32),)),
    }


epsilon = 1e-05
masked_score = -1e+30
highest = lax.Precision.HIGHEST

@jax.custom_vjp
def low(v):
    return lax.optimization_barrier(v.astype(jnp.bfloat16)).astype(jnp.float32)

@jax.custom_vjp
def low_back(v):
    return v

def low_keep(v):
    return (low(v), None)

def low_pass(kept, grad):
    return (grad,)

def back_keep(v):
    return (v, None)

def back_low(kept, grad):
    return (low(grad),)
low.defvjp(low_keep, low_pass)
low_back.defvjp(back_keep, back_low)

def normalize(inputs, norm_gain, norm_shift):
    average = lax.optimization_barrier(jnp.mean(inputs, axis=-1, keepdims=True))
    centered = inputs - average
    inverse_spread = lax.rsqrt(lax.optimization_barrier(jnp.mean(centered * centered, axis=-1, keepdims=True)) + epsilon)
    return centered * inverse_spread * norm_gain + norm_shift

def product(left, right):
    return jnp.dot(left, right, preferred_element_type=jnp.float32, precision=highest)

def heads_attend(queries, key_rows, value_rows, allowed):
    row_count, features = queries.shape
    head_size = features // HEADS
    scaling = head_size ** (-0.5)
    query_heads = queries.reshape(row_count, HEADS, head_size)
    key_heads = key_rows.reshape(key_rows.shape[0], HEADS, head_size)
    value_heads = value_rows.reshape(value_rows.shape[0], HEADS, head_size)
    scores = low_back(jnp.einsum('qhd,khd->hqk', query_heads, key_heads, precision=highest) * scaling)
    scores = jnp.where(allowed[None], scores, masked_score)
    softened = low(jax.nn.softmax(scores, axis=-1))
    attended = jnp.einsum('hqk,khd->qhd', softened, value_heads, precision=highest)
    return low(low_back(attended.reshape(row_count, features)))

def layer_item(inputs, caption, length, params):
    self_gain, self_shift, self_in_weight, self_out_weight, cross_gain, cross_shift, cross_query_weight, cross_memory_weight, cross_out_weight, feed_gain, feed_shift, up_weight, up_bias, down_weight, down_bias = params
    features = inputs.shape[1]
    normed = low(normalize(inputs, self_gain, self_shift))
    projected = low(low_back(product(normed, self_in_weight)))
    positions = lax.iota(jnp.int32, inputs.shape[0])
    allowed = positions[None, :] <= positions[:, None]
    attended = heads_attend(projected[:, :features], projected[:, features:2 * features], projected[:, 2 * features:], allowed)
    residual = inputs + low_back(product(attended, self_out_weight))
    normed = low(normalize(residual, cross_gain, cross_shift))
    queries = low(low_back(product(normed, cross_query_weight)))
    memory = low(low_back(product(caption, cross_memory_weight)))
    slot_index = lax.iota(jnp.int32, caption.shape[0])
    visible = (slot_index < length)[None, :]
    attended = heads_attend(queries, memory[:, :features], memory[:, features:], visible)
    residual = residual + low_back(product(attended, cross_out_weight))
    normed = low(normalize(residual, feed_gain, feed_shift))
    before = low_back(product(normed, up_weight) + up_bias)
    activated = low(jax.nn.gelu(before, approximate=False))
    return residual + low_back(product(activated, down_weight) + down_bias)

def reference(tokens, captions, caption_lengths, cotangent, self_gain, self_shift, self_in_weight, self_out_weight, cross_gain, cross_shift, cross_query_weight, cross_memory_weight, cross_out_weight, feed_gain, feed_shift, up_weight, up_bias, down_weight, down_bias):
    params = tuple((tensor.astype(jnp.float32) for tensor in (self_gain, self_shift, self_in_weight, self_out_weight, cross_gain, cross_shift, cross_query_weight, cross_memory_weight, cross_out_weight, feed_gain, feed_shift, up_weight, up_bias, down_weight, down_bias)))

    def forward(inputs, memory_in, weights):

        def one_item(packed):
            item_tokens, item_caption, item_length = packed
            return jax.checkpoint(layer_item)(item_tokens, item_caption, item_length, weights)
        return lax.map(one_item, (inputs, memory_in, caption_lengths))
    final, pullback = jax.vjp(forward, tokens.astype(jnp.float32), captions.astype(jnp.float32), params)
    grad_tokens, grad_captions, grads = pullback(cotangent.astype(jnp.float32))
    return (final.astype(jnp.bfloat16), grad_tokens, grad_captions, grads[0], grads[1], grads[2], grads[3], grads[4], grads[5], grads[6], grads[7], grads[8], grads[9], grads[10], grads[11], grads[12], grads[13], grads[14])
```

```python
import functools

import jax
import jax.numpy as jnp
from jax import lax
from jax.experimental import pallas as pl
from jax.experimental.pallas import tpu as pltpu
from jax.sharding import PartitionSpec as P

HEADS = 16
AXES = ("dp", "seq")
BF = jnp.bfloat16
F32 = jnp.float32
epsilon = 1e-05
masked_score = -1e30
VMEM_LIMIT = 56 * 1024 * 1024


def device_count():
    return lax.axis_size("dp") * lax.axis_size("seq")


def place():
    index = lax.axis_index("dp") * lax.axis_size("seq") + lax.axis_index("seq")
    return index


def spots(core):
    index = place()
    c = index % 2
    half = c if core == "own" else 1 - c
    return jnp.stack(
        [half, (index // 4) % 2, (index // 2) % 2, (index // 8) % 2, index // 16]
    ).astype(jnp.int32)


def hop(values, change):
    count = device_count()
    pairs = [(i, change(i)) for i in range(count)]
    return lax.ppermute(values, AXES, pairs)


def hop_core(values):
    return hop(values, lambda i: i ^ 1)


def hop_first(values):
    return hop(values, lambda i: i ^ 4 if i % 2 == 0 else i ^ 2)


def hop_second(values):
    return hop(values, lambda i: i ^ 2 if i % 2 == 0 else i ^ 4)


def hop_z0(values):
    return hop(values, lambda i: i ^ 8)


def hop_z1(values, step):
    return hop(values, lambda i: i ^ (16 * step))


def far_count():
    return device_count() // 16


def column_half(values, half):
    width = values.shape[-1] // 2
    return lax.dynamic_slice_in_dim(values, half * width, width, values.ndim - 1)


def chip_rows(shards):
    c = place() % 2
    own = jnp.concatenate([column_half(s, c) for s in shards], axis=1)
    other = jnp.concatenate([column_half(s, 1 - c) for s in shards], axis=1)
    came = hop_core(other)
    return jnp.where(
        c == 0, jnp.concatenate([own, came], 0), jnp.concatenate([came, own], 0)
    )


def gather_chips(block):
    far = far_count()
    one = jnp.stack([block] + [hop_z1(block, k) for k in range(1, far)])
    two = jnp.stack([one, hop_first(one)])
    three = jnp.stack([two, hop_z0(two)])
    four = hop_second(three)
    return three, four, hop_core(three), hop_core(four)


def assemble_kernel(widths, far, rows, spot_ref, *refs):
    near_own, far_own, near_other, far_other = refs[:4]
    outs = refs[4 : 4 + len(widths)]
    sem = refs[-1]
    c, mx, my, mz0, mz1 = (spot_ref[i] for i in range(5))
    copies = []
    for side, pieces in (("own", (near_own, far_own)), ("other", (near_other, far_other))):
        half = c if side == "own" else 1 - c
        for d4 in range(2):
            for dz0 in range(2):
                for d2 in range(2):
                    for dz1 in range(far):
                        x = jnp.where(half == 0, d2, d4) ^ mx
                        y = jnp.where(half == 0, d4, d2) ^ my
                        z = (dz1 ^ mz1) * 2 + (dz0 ^ mz0)
                        row = pl.multiple_of(((z * 2 + x) * 2 + y) * rows, rows)
                        start = 0
                        for out, width in zip(outs, widths):
                            column = pl.multiple_of(half * width, 128)
                            copies.append(
                                pltpu.make_async_copy(
                                    pieces[d4].at[dz0, d2, dz1, :, pl.ds(start, width)],
                                    out.at[pl.ds(row, rows), pl.ds(column, width)],
                                    sem,
                                )
                            )
                            start += width
    for copy in copies:
        copy.start()
    for copy in copies:
        copy.wait()


def assemble(pieces, widths):
    far, rows = pieces[0].shape[2], pieces[0].shape[3]
    total = rows * 8 * far
    return pl.pallas_call(
        functools.partial(assemble_kernel, widths, far, rows),
        out_shape=[jax.ShapeDtypeStruct((total, 2 * w), BF) for w in widths],
        in_specs=[pl.BlockSpec(memory_space=pltpu.SMEM)]
        + [pl.BlockSpec(memory_space=pl.ANY)] * 4,
        out_specs=[pl.BlockSpec(memory_space=pltpu.VMEM)] * len(widths),
        scratch_shapes=[pltpu.SemaphoreType.DMA],
        compiler_params=pltpu.CompilerParams(vmem_limit_bytes=VMEM_LIMIT),
        name="assemble",
    )(spots("own"), *pieces)


def wgrad_kernel(kinds, rows, spot_ref, *refs):
    half, mx, my, mz0 = (spot_ref[i] for i in range(4))
    out = refs[-1]
    at, start = 0, 0
    for kind in kinds:
        if kind == "dot":
            left, right = refs[at], refs[at + 1]
            at += 2
            block = lax.dot_general(
                left[...], right[...], (((0,), (0,)), ((), ())), preferred_element_type=F32
            ).astype(BF)
        else:
            block = refs[at][...].astype(BF)
            at += 1
        width = block.shape[1]
        for j in range(8):
            z0 = (j // 4) ^ mz0
            x = (j // 2 % 2) ^ mx
            y = (j % 2) ^ my
            d4 = jnp.where(half == 0, y, x)
            d2 = jnp.where(half == 0, x, y)
            out[d4, z0, d2, 0, :, start : start + width] = block[j * rows : (j + 1) * rows]
        start += width


def wgrad(terms, core):
    far = far_count()
    kinds = tuple("dot" if len(t) == 2 else "raw" for t in terms)
    height = terms[0][0].shape[1] if kinds[0] == "dot" else terms[0][0].shape[0]
    rows = height // (8 * far)
    specs, args, total, flops, moved = [], [], 0, 0, 0
    for term in terms:
        right = term[-1]
        width = right.shape[1] // 2
        if len(term) == 2:
            left = term[0]
            specs.append(pl.BlockSpec((left.shape[0], 8 * rows), lambda z, s: (0, z)))
            specs.append(pl.BlockSpec((right.shape[0], width), lambda z, s: (0, s[0])))
            flops += 2 * left.shape[0] * height * width
            moved += left.size * 2 + right.size
        else:
            specs.append(pl.BlockSpec((8 * rows, width), lambda z, s: (z, s[0])))
        args += list(term)
        total += width
    return pl.pallas_call(
        functools.partial(wgrad_kernel, kinds, rows),
        out_shape=jax.ShapeDtypeStruct((2, 2, 2, far, rows, total), BF),
        grid_spec=pltpu.PrefetchScalarGridSpec(
            num_scalar_prefetch=1,
            grid=(far,),
            in_specs=specs,
            out_specs=pl.BlockSpec(
                (2, 2, 2, 1, rows, total),
                lambda z, s: (0, 0, 0, z ^ s[4], 0, 0),
            ),
        ),
        compiler_params=pltpu.CompilerParams(vmem_limit_bytes=VMEM_LIMIT),
        cost_estimate=pl.CostEstimate(
            flops=flops, bytes_accessed=moved + 2 * height * total, transcendentals=0
        ),
        name="wgrad",
    )(spots(core), *args)


def wide(values):
    return values.astype(F32)


def scatter_chips(terms):
    far = far_count()
    other = wgrad(terms, "other")
    came0 = hop_core(other)
    own = wgrad(terms, "own")
    came1 = hop_second((wide(own[1]) + wide(came0[1])).astype(BF))
    came2 = hop_z0((wide(own[0, 1]) + wide(came0[0, 1]) + wide(came1[1])).astype(BF))
    came3 = hop_first(
        (wide(own[0, 0, 1]) + wide(came0[0, 0, 1]) + wide(came1[0, 1]) + wide(came2[1])).astype(BF)
    )
    kept = (
        wide(own[0, 0, 0])
        + wide(came0[0, 0, 0])
        + wide(came1[0, 0])
        + wide(came2[0])
        + wide(came3)
    )
    low = kept.astype(BF)
    total = kept[0]
    for k in range(1, far):
        total = total + wide(hop_z1(low[k], k))
    c = place() % 2
    rows = total.shape[0] // 2
    mine = lax.dynamic_slice_in_dim(total, c * rows, rows, 0)
    came = hop_core(lax.dynamic_slice_in_dim(total, (1 - c) * rows, rows, 0))
    left = jnp.where(c == 0, mine, came)
    right = jnp.where(c == 0, came, mine)
    results, start = [], 0
    for term in terms:
        width = term[-1].shape[1] // 2
        results.append(
            jnp.concatenate(
                [left[:, start : start + width], right[:, start : start + width]], axis=1
            )
        )
        start += width
    return results


def pack_small(vectors, bias):
    r = vectors[0].shape[0]
    left = jnp.pad(jnp.stack(vectors, 1), ((0, 0), (0, 128 - len(vectors))))
    k = bias.shape[0] // r
    right = jnp.pad(bias.reshape(k, r).T, ((0, 0), (0, 128 - k)))
    return jnp.concatenate([left, right], axis=1)


def unpack_small(packed, count, k):
    n = device_count()
    d = packed.shape[0]
    flat = packed.T
    vectors = [flat[i] for i in range(count)]
    bias = flat[128 : 128 + k].reshape(k, n, d // n).transpose(1, 0, 2).reshape(k * d)
    return vectors, bias


def pack_small_grads(vectors, bias):
    n = device_count()
    d = vectors[0].shape[0]
    k = bias.shape[0] // d
    rows = bias.reshape(n, k, d // n).transpose(1, 0, 2).reshape(k, d)
    block = jnp.concatenate(
        [
            jnp.stack(vectors),
            jnp.zeros((128 - len(vectors), d), F32),
            rows,
            jnp.zeros((128 - k, d), F32),
        ]
    )
    return block.T


def normalize(inputs, norm_gain, norm_shift):
    average = jnp.mean(inputs, axis=-1, keepdims=True)
    centered = inputs - average
    inverse_spread = lax.rsqrt(jnp.mean(centered * centered, axis=-1, keepdims=True) + epsilon)
    return centered * inverse_spread * norm_gain + norm_shift


def norm_back(inputs, gain, grad_normed):
    average = jnp.mean(inputs, axis=-1, keepdims=True)
    centered = inputs - average
    inverse_spread = lax.rsqrt(jnp.mean(centered * centered, axis=-1, keepdims=True) + epsilon)
    unit = centered * inverse_spread
    grad_unit = grad_normed * gain
    grad_inputs = inverse_spread * (
        grad_unit
        - jnp.mean(grad_unit, axis=-1, keepdims=True)
        - unit * jnp.mean(grad_unit * unit, axis=-1, keepdims=True)
    )
    return grad_inputs, jnp.sum(grad_normed * unit, axis=(0, 1)), jnp.sum(grad_normed, axis=(0, 1))


def gelu_exact(inputs):
    return jax.nn.gelu(inputs, approximate=False)


def split_heads(tensor):
    return tensor.reshape(tensor.shape[0], tensor.shape[1], HEADS, tensor.shape[2] // HEADS)


def attend(queries, key_rows, value_rows, allowed):
    scaling = (queries.shape[2] // HEADS) ** (-0.5)
    scores = (
        jnp.einsum(
            "iqhd,ikhd->ihqk",
            split_heads(queries),
            split_heads(key_rows),
            preferred_element_type=F32,
        )
        * scaling
    )
    scores = jnp.where(allowed[:, None], scores, masked_score)
    softened = jax.nn.softmax(scores, axis=-1)
    attended = jnp.einsum(
        "ihqk,ikhd->iqhd",
        softened.astype(BF),
        split_heads(value_rows),
        preferred_element_type=F32,
    )
    return (attended.reshape(queries.shape).astype(BF), softened)


def attend_back(queries, key_rows, value_rows, softened, grad_attended):
    scaling = (queries.shape[2] // HEADS) ** (-0.5)
    grad_heads = split_heads(grad_attended)
    grad_soft = jnp.einsum(
        "iqhd,ikhd->ihqk", grad_heads, split_heads(value_rows), preferred_element_type=F32
    )
    grad_values = jnp.einsum(
        "ihqk,iqhd->ikhd", softened.astype(BF), grad_heads, preferred_element_type=F32
    ).reshape(value_rows.shape)
    grad_scores = (
        softened * (grad_soft - jnp.sum(softened * grad_soft, axis=-1, keepdims=True))
    ).astype(BF)
    grad_queries = (
        jnp.einsum(
            "ihqk,ikhd->iqhd", grad_scores, split_heads(key_rows), preferred_element_type=F32
        ).reshape(queries.shape)
        * scaling
    )
    grad_keys = (
        jnp.einsum(
            "ihqk,iqhd->ikhd", grad_scores, split_heads(queries), preferred_element_type=F32
        ).reshape(key_rows.shape)
        * scaling
    )
    return (grad_queries, grad_keys, grad_values)


def flat(tensor):
    return tensor.reshape(-1, tensor.shape[-1])


def dot(left, right):
    return jnp.dot(left, right, preferred_element_type=F32)


def dot_t(left, right):
    return lax.dot_general(
        left, right, (((left.ndim - 1,), (1,)), ((), ())), preferred_element_type=F32
    )


def sum_seq(values):
    size = lax.axis_size("seq")
    dp = lax.axis_size("dp")
    step = 1
    total = values.astype(BF)
    while step < size:
        pairs = [
            (d * size + s, d * size + (s ^ step)) for d in range(dp) for s in range(size)
        ]
        came = lax.ppermute(total, AXES, pairs)
        total = wide(total) + wide(came)
        step *= 2
        if step < size:
            total = total.astype(BF)
    return total


def body(
    tokens,
    captions,
    caption_lengths,
    cotangent,
    self_gain,
    self_shift,
    self_in_weight,
    self_out_weight,
    cross_gain,
    cross_shift,
    cross_query_weight,
    cross_memory_weight,
    cross_out_weight,
    feed_gain,
    feed_shift,
    up_weight,
    up_bias,
    down_weight,
    down_bias,
):
    features = tokens.shape[2]
    k_bias = up_weight.shape[1] // features
    small = pack_small(
        [self_gain, self_shift, cross_gain, cross_shift, feed_gain, feed_shift, down_bias], up_bias
    )
    groups = (
        (self_in_weight, self_out_weight, small),
        (cross_query_weight, cross_memory_weight, cross_out_weight),
        (up_weight,),
    )
    shards = [s for g in groups for s in g]
    rows = chip_rows(shards)
    blocks, start = [], 0
    for group in groups:
        widths = tuple(s.shape[1] // 2 for s in group)
        blocks.append((rows[:, start : start + sum(widths)], widths))
        start += sum(widths)
    blocks.append((chip_rows([down_weight]), (down_weight.shape[1] // 2,)))
    gathered = [assemble(gather_chips(b), w) for b, w in blocks]
    (self_in, self_out, small_full), (cross_query, cross_memory, cross_out), (up,), (down,) = (
        gathered
    )
    vectors, up_offset = unpack_small(small_full, 7, k_bias)
    self_gain, self_shift, cross_gain, cross_shift, feed_gain, feed_shift, down_offset = (
        wide(v) for v in vectors
    )
    up_offset = wide(up_offset)

    inputs = wide(tokens)
    normed1 = normalize(inputs, self_gain, self_shift).astype(BF)
    projected = dot(normed1, self_in).astype(BF)
    queries = projected[:, :, :features]
    key_rows = projected[:, :, features : 2 * features]
    value_rows = projected[:, :, 2 * features :]
    all_keys = lax.all_gather(key_rows, "seq", axis=1, tiled=True)
    all_values = lax.all_gather(value_rows, "seq", axis=1, tiled=True)
    row_count = inputs.shape[1]
    query_place = lax.axis_index("seq") * row_count + lax.iota(jnp.int32, row_count)
    key_place = lax.iota(jnp.int32, all_keys.shape[1])
    allowed = (key_place[None, :] <= query_place[:, None])[None]
    attended1, softened1 = attend(queries, all_keys, all_values, allowed)
    residual1 = inputs + dot(attended1, self_out)

    normed2 = normalize(residual1, cross_gain, cross_shift).astype(BF)
    cross_queries = dot(normed2, cross_query).astype(BF)
    memory = dot(captions, cross_memory).astype(BF)
    memory_keys, memory_values = memory[:, :, :features], memory[:, :, features:]
    slot_index = lax.iota(jnp.int32, captions.shape[1])
    visible = (slot_index[None, :] < caption_lengths[:, None])[:, None, :]
    attended2, softened2 = attend(cross_queries, memory_keys, memory_values, visible)
    residual2 = residual1 + dot(attended2, cross_out)

    normed3 = normalize(residual2, feed_gain, feed_shift).astype(BF)
    before = dot(normed3, up) + up_offset
    activated = gelu_exact(before).astype(BF)
    final = residual2 + dot(activated, down) + down_offset

    grad_final = wide(cotangent)
    grad_activated = dot_t(cotangent, down)
    _, pullback = jax.vjp(gelu_exact, before)
    grad_before = pullback(grad_activated)[0].astype(BF)
    grad_normed3 = dot_t(grad_before, up)
    grad_in3, grad_feed_gain, grad_feed_shift = norm_back(residual2, feed_gain, grad_normed3)
    grad_up_bias = jnp.sum(wide(grad_before), axis=(0, 1))
    grad_down_bias = jnp.sum(grad_final, axis=(0, 1))
    (grad_down,) = scatter_chips([(flat(activated), flat(cotangent))])
    (grad_up,) = scatter_chips([(flat(normed3), flat(grad_before))])
    grad_second = grad_final + grad_in3

    low2 = grad_second.astype(BF)
    grad_attended2 = dot_t(low2, cross_out).astype(BF)
    grad_cq, grad_mk, grad_mv = attend_back(
        cross_queries, memory_keys, memory_values, softened2, grad_attended2
    )
    grad_memory = jnp.concatenate([grad_mk, grad_mv], axis=-1).astype(BF)
    grad_captions = sum_seq(dot_t(grad_memory, cross_memory))
    low_cq = grad_cq.astype(BF)
    grad_normed2 = dot_t(low_cq, cross_query)
    grad_in2, grad_cross_gain, grad_cross_shift = norm_back(residual1, cross_gain, grad_normed2)
    grad_first = grad_second + grad_in2

    low1 = grad_first.astype(BF)
    grad_cross_query, grad_cross_memory, grad_cross_out, grad_self_out = scatter_chips(
        [
            (flat(normed2), flat(low_cq)),
            (flat(captions), flat(grad_memory)),
            (flat(attended2), flat(low2)),
            (flat(attended1), flat(low1)),
        ]
    )
    grad_attended1 = dot_t(low1, self_out).astype(BF)
    grad_q, grad_all_keys, grad_all_values = attend_back(
        queries, all_keys, all_values, softened1, grad_attended1
    )
    grad_keys = lax.psum_scatter(
        grad_all_keys.astype(BF), "seq", scatter_dimension=1, tiled=True
    ).astype(BF)
    grad_values = lax.psum_scatter(
        grad_all_values.astype(BF), "seq", scatter_dimension=1, tiled=True
    ).astype(BF)
    grad_projected = jnp.concatenate([grad_q.astype(BF), grad_keys, grad_values], axis=-1)
    grad_normed1 = dot_t(grad_projected, self_in)
    grad_in1, grad_self_gain, grad_self_shift = norm_back(inputs, self_gain, grad_normed1)
    small_grads = pack_small_grads(
        [
            grad_self_gain,
            grad_self_shift,
            grad_cross_gain,
            grad_cross_shift,
            grad_feed_gain,
            grad_feed_shift,
            grad_down_bias,
        ],
        grad_up_bias,
    )
    grad_self_in, small_out = scatter_chips(
        [(flat(normed1), flat(grad_projected)), (small_grads,)]
    )
    small_columns = small_out.T
    return (
        final.astype(BF),
        grad_first + grad_in1,
        grad_captions,
        small_columns[0],
        small_columns[1],
        grad_self_in,
        grad_self_out,
        small_columns[2],
        small_columns[3],
        grad_cross_query,
        grad_cross_memory,
        grad_cross_out,
        small_columns[4],
        small_columns[5],
        grad_up,
        small_columns[128 : 128 + k_bias].reshape(-1),
        grad_down,
        small_columns[6],
    )


def solution(mesh):
    tokens_spec = P("dp", "seq", None)
    rows1, rows2 = P(AXES), P(AXES, None)
    return jax.shard_map(
        body,
        mesh=mesh,
        in_specs=(
            tokens_spec, P("dp", None, None), P("dp"), tokens_spec,
            rows1, rows1, rows2, rows2, rows1, rows1, rows2, rows2, rows2,
            rows1, rows1, rows2, rows1, rows2, rows1,
        ),
        out_specs=(
            tokens_spec, tokens_spec, P("dp", None, None),
            rows1, rows1, rows2, rows2, rows1, rows1, rows2, rows2, rows2,
            rows1, rows1, rows2, rows1, rows2, rows1,
        ),
        check_vma=False,
    )
```

```python
import functools

import jax
import jax.numpy as jnp
from jax import lax
from jax.experimental import pallas as pl
from jax.experimental.pallas import tpu as pltpu
from jax.sharding import PartitionSpec as P

HEADS = 16
AXES = ("dp", "seq")
BF = jnp.bfloat16
F32 = jnp.float32
epsilon = 1e-05
masked_score = -1e30
VMEM_LIMIT = 56 * 1024 * 1024


def device_count():
    return lax.axis_size("dp") * lax.axis_size("seq")


def place():
    index = lax.axis_index("dp") * lax.axis_size("seq") + lax.axis_index("seq")
    return index


def spots(core):
    index = place()
    c = index % 2
    half = c if core == "own" else 1 - c
    return jnp.stack(
        [half, (index // 4) % 2, (index // 2) % 2, (index // 8) % 2, index // 16]
    ).astype(jnp.int32)


def hop(values, change):
    count = device_count()
    pairs = [(i, change(i)) for i in range(count)]
    return lax.ppermute(values, AXES, pairs)


def hop_core(values):
    return hop(values, lambda i: i ^ 1)


def hop_first(values):
    return hop(values, lambda i: i ^ 4 if i % 2 == 0 else i ^ 2)


def hop_second(values):
    return hop(values, lambda i: i ^ 2 if i % 2 == 0 else i ^ 4)


def hop_z0(values):
    return hop(values, lambda i: i ^ 8)


def hop_z1(values, step):
    return hop(values, lambda i: i ^ (16 * step))


def far_count():
    return device_count() // 16


def column_half(values, half):
    width = values.shape[-1] // 2
    return lax.dynamic_slice_in_dim(values, half * width, width, values.ndim - 1)


def chip_rows(shards):
    c = place() % 2
    own = jnp.concatenate([column_half(s, c) for s in shards], axis=1)
    other = jnp.concatenate([column_half(s, 1 - c) for s in shards], axis=1)
    came = hop_core(other)
    return jnp.where(
        c == 0, jnp.concatenate([own, came], 0), jnp.concatenate([came, own], 0)
    )


def after(value, *others):
    return lax.optimization_barrier((value, *others))[0]


class Line:
    def __init__(self):
        self.last = ()

    def __call__(self, function, first, *rest):
        if self.last:
            first = after(first, *self.last)
        result = function(first, *rest)
        self.last = jax.tree.leaves(result)[:1]
        return result


class Gather:
    def __init__(self, block):
        self.sent = block

    def far(self, line):
        self.sent = line(lambda v: v + 0 if line.last else v, self.sent)
        self.came = [hop_z1(self.sent, k) for k in range(1, far_count())]

    def first(self, line):
        self.sent = line(lambda c, s, *o: jnp.stack([s, *o, c]), self.came[-1], self.sent, *self.came[:-1])
        self.came = hop_first(self.sent)

    def near(self, line):
        self.sent = line(lambda c, s: jnp.stack([s, c]), self.came, self.sent)
        self.came = hop_z0(self.sent)

    def second(self, line):
        self.sent = line(lambda c, s: jnp.stack([s, c]), self.came, self.sent)
        self.came = hop_second(self.sent)
        self.sent_other = hop_core(self.sent)

    def pair(self, line):
        self.came = after(self.came, *line.last)
        self.came_other = hop_core(self.came)

    def pieces(self):
        return self.came_other, self.sent, self.came, self.sent_other


def assemble_kernel(widths, far, rows, spot_ref, *refs):
    far_other, near_own, far_own, near_other = refs[:4]
    outs = refs[4 : 4 + len(widths)]
    sem = refs[-1]
    c, mx, my, mz0, mz1 = (spot_ref[i] for i in range(5))
    copies = []
    for side, pieces in (("own", (near_own, far_own)), ("other", (near_other, far_other))):
        half = c if side == "own" else 1 - c
        for d4 in range(2):
            for dz0 in range(2):
                for d2 in range(2):
                    for dz1 in range(far):
                        x = jnp.where(half == 0, d2, d4) ^ mx
                        y = jnp.where(half == 0, d4, d2) ^ my
                        z = (dz1 ^ mz1) * 2 + (dz0 ^ mz0)
                        row = pl.multiple_of(((z * 2 + x) * 2 + y) * rows, rows)
                        start = 0
                        for out, width in zip(outs, widths):
                            column = pl.multiple_of(half * width, 128)
                            copies.append(
                                pltpu.make_async_copy(
                                    pieces[d4].at[dz0, d2, dz1, :, pl.ds(start, width)],
                                    out.at[pl.ds(row, rows), pl.ds(column, width)],
                                    sem,
                                )
                            )
                            start += width
    for copy in copies:
        copy.start()
    for copy in copies:
        copy.wait()


def assemble(pieces, widths):
    far, rows = pieces[0].shape[2], pieces[0].shape[3]
    total = rows * 8 * far
    return pl.pallas_call(
        functools.partial(assemble_kernel, widths, far, rows),
        out_shape=[jax.ShapeDtypeStruct((total, 2 * w), BF) for w in widths],
        in_specs=[pl.BlockSpec(memory_space=pltpu.SMEM)]
        + [pl.BlockSpec(memory_space=pl.ANY)] * 4,
        out_specs=[pl.BlockSpec(memory_space=pltpu.VMEM)] * len(widths),
        scratch_shapes=[pltpu.SemaphoreType.DMA],
        compiler_params=pltpu.CompilerParams(vmem_limit_bytes=VMEM_LIMIT),
        name="assemble",
    )(spots("own"), *pieces)


def wgrad_kernel(kinds, rows, spot_ref, *refs):
    half, mx, my, mz0 = (spot_ref[i] for i in range(4))
    out = refs[-1]
    at, start = 0, 0
    for kind in kinds:
        if kind == "dot":
            left, right = refs[at], refs[at + 1]
            at += 2
            block = lax.dot_general(
                left[...], right[...], (((0,), (0,)), ((), ())), preferred_element_type=F32
            ).astype(BF)
        else:
            block = refs[at][...].astype(BF)
            at += 1
        width = block.shape[1]
        for j in range(8):
            z0 = (j // 4) ^ mz0
            x = (j // 2 % 2) ^ mx
            y = (j % 2) ^ my
            d4 = jnp.where(half == 0, y, x)
            d2 = jnp.where(half == 0, x, y)
            out[d4, z0, d2, 0, :, start : start + width] = block[j * rows : (j + 1) * rows]
        start += width


def wgrad(terms, core):
    far = far_count()
    kinds = tuple("dot" if len(t) == 2 else "raw" for t in terms)
    height = terms[0][0].shape[1] if kinds[0] == "dot" else terms[0][0].shape[0]
    rows = height // (8 * far)
    specs, args, total, flops, moved = [], [], 0, 0, 0
    for term in terms:
        right = term[-1]
        width = right.shape[1] // 2
        if len(term) == 2:
            left = term[0]
            specs.append(pl.BlockSpec((left.shape[0], 8 * rows), lambda z, s: (0, z)))
            specs.append(pl.BlockSpec((right.shape[0], width), lambda z, s: (0, s[0])))
            flops += 2 * left.shape[0] * height * width
            moved += left.size * 2 + right.size
        else:
            specs.append(pl.BlockSpec((8 * rows, width), lambda z, s: (z, s[0])))
        args += list(term)
        total += width
    return pl.pallas_call(
        functools.partial(wgrad_kernel, kinds, rows),
        out_shape=jax.ShapeDtypeStruct((2, 2, 2, far, rows, total), BF),
        grid_spec=pltpu.PrefetchScalarGridSpec(
            num_scalar_prefetch=1,
            grid=(far,),
            in_specs=specs,
            out_specs=pl.BlockSpec(
                (2, 2, 2, 1, rows, total),
                lambda z, s: (0, 0, 0, z ^ s[4], 0, 0),
            ),
        ),
        compiler_params=pltpu.CompilerParams(vmem_limit_bytes=VMEM_LIMIT),
        cost_estimate=pl.CostEstimate(
            flops=flops, bytes_accessed=moved + 2 * height * total, transcendentals=0
        ),
        name="wgrad",
    )(spots(core), *args)


def wide(values):
    return values.astype(F32)


class Scatter:
    def __init__(self, line, terms):
        self.widths = [t[-1].shape[1] // 2 for t in terms]

        def run(core):
            return line(lambda f: wgrad([(f, *terms[0][1:]), *terms[1:]], core), terms[0][0])

        self.came0 = hop_core(run("other"))
        self.own = run("own")

    def second(self, line):
        sent = line(lambda c, o: (wide(o[1]) + wide(c[1])).astype(BF), self.came0, self.own)
        self.came1 = hop_second(sent)

    def near(self, line):
        def add(c1, c0, o):
            return (wide(o[0, 1]) + wide(c0[0, 1]) + wide(c1[1])).astype(BF)

        self.came2 = hop_z0(line(add, self.came1, self.came0, self.own))

    def first(self, line):
        def add(c2, c1, c0, o):
            return (wide(o[0, 0, 1]) + wide(c0[0, 0, 1]) + wide(c1[0, 1]) + wide(c2[1])).astype(BF)

        self.came3 = hop_first(line(add, self.came2, self.came1, self.came0, self.own))

    def far(self, line):
        def add(c3, c2, c1, c0, o):
            kept = wide(o[0, 0, 0]) + wide(c0[0, 0, 0]) + wide(c1[0, 0]) + wide(c2[0]) + wide(c3)
            return kept.astype(BF), kept[0]

        low, self.kept = line(add, self.came3, self.came2, self.came1, self.came0, self.own)
        self.came4 = [hop_z1(low[k], k) for k in range(1, far_count())]

    def close(self, line):
        total = line(lambda c, t, *o: sum(map(wide, o), t + wide(c)), self.came4[-1], self.kept, *self.came4[:-1])
        rows = total.shape[0] // 2
        c = place() % 2
        self.mine = lax.dynamic_slice_in_dim(total, c * rows, rows, 0)
        self.theirs = hop_core(lax.dynamic_slice_in_dim(total, (1 - c) * rows, rows, 0))

    def result(self, line):
        c = place() % 2

        def join(came, mine):
            left = jnp.where(c == 0, mine, came)
            right = jnp.where(c == 0, came, mine)
            results, start = [], 0
            for width in self.widths:
                at = slice(start, start + width)
                results.append(jnp.concatenate([left[:, at], right[:, at]], axis=1))
                start += width
            return results

        return line(join, self.theirs, self.mine)


def pack_small(vectors, bias):
    r = vectors[0].shape[0]
    left = jnp.pad(jnp.stack(vectors, 1), ((0, 0), (0, 128 - len(vectors))))
    k = bias.shape[0] // r
    right = jnp.pad(bias.reshape(k, r).T, ((0, 0), (0, 128 - k)))
    return jnp.concatenate([left, right], axis=1)


def unpack_small(packed, count, k):
    n = device_count()
    d = packed.shape[0]
    flat = packed.T
    vectors = [flat[i] for i in range(count)]
    bias = flat[128 : 128 + k].reshape(k, n, d // n).transpose(1, 0, 2).reshape(k * d)
    return vectors, bias


def pack_small_grads(vectors, bias):
    n = device_count()
    d = vectors[0].shape[0]
    k = bias.shape[0] // d
    rows = bias.reshape(n, k, d // n).transpose(1, 0, 2).reshape(k, d)
    block = jnp.concatenate(
        [
            jnp.stack(vectors),
            jnp.zeros((128 - len(vectors), d), F32),
            rows,
            jnp.zeros((128 - k, d), F32),
        ]
    )
    return block.T


def normalize(inputs, norm_gain, norm_shift):
    average = jnp.mean(inputs, axis=-1, keepdims=True)
    centered = inputs - average
    inverse_spread = lax.rsqrt(jnp.mean(centered * centered, axis=-1, keepdims=True) + epsilon)
    return centered * inverse_spread * norm_gain + norm_shift


def norm_back(inputs, gain, grad_normed):
    average = jnp.mean(inputs, axis=-1, keepdims=True)
    centered = inputs - average
    inverse_spread = lax.rsqrt(jnp.mean(centered * centered, axis=-1, keepdims=True) + epsilon)
    unit = centered * inverse_spread
    grad_unit = grad_normed * gain
    grad_inputs = inverse_spread * (
        grad_unit
        - jnp.mean(grad_unit, axis=-1, keepdims=True)
        - unit * jnp.mean(grad_unit * unit, axis=-1, keepdims=True)
    )
    return grad_inputs, jnp.sum(grad_normed * unit, axis=(0, 1)), jnp.sum(grad_normed, axis=(0, 1))


def shifts(info_ref, kind, block):
    if kind == "length" or block == 0:
        return None
    me = info_ref[0]
    return jnp.where((me ^ block) < me, 0.0, -masked_score).astype(F32)

def allowed_keys(info_ref, kind, item, span, count):
    shape = (span, count)
    row = lax.broadcasted_iota(jnp.int32, shape, 0)
    if kind == "length":
        return row < info_ref[item]
    return row <= lax.broadcasted_iota(jnp.int32, shape, 1)

def attend_kernel(kind, info_ref, q_ref, k_ref, v_ref, o_ref, lse_ref):
    blocks, _, span, wide_lanes = k_ref.shape
    count = q_ref.shape[2]
    lanes = 128
    head = lanes // 2
    low_lane = lax.broadcasted_iota(jnp.int32, (count, lanes), 1) < head
    allowed = allowed_keys(info_ref, kind, pl.program_id(0), span, count)
    outside = [shifts(info_ref, kind, j) for j in range(blocks)]
    for pair in range(wide_lanes // lanes):
        at = slice(pair * lanes, (pair + 1) * lanes)
        values_t = v_ref[:, :, :, at].reshape(blocks * span, lanes).T
        queries = q_ref[0, 0, :, at] * (head ** -0.5)
        outs = []
        for h in range(2):
            mine = jnp.where(low_lane if h == 0 else ~low_lane, queries, 0).astype(BF)
            scores = [
                lax.dot_general(k_ref[j, 0, :, at], mine, (((1,), (1,)), ((), ())), preferred_element_type=F32)
                for j in range(blocks)
            ]
            scores[0] = jnp.where(allowed, scores[0], masked_score)
            top = jnp.max(scores[0], axis=0, keepdims=True)
            for j in range(1, blocks):
                top = jnp.maximum(top, jnp.max(scores[j], axis=0, keepdims=True) - outside[j])
            soft = [jnp.exp(scores[0] - top)]
            soft += [jnp.exp(scores[j] - (top + outside[j])) for j in range(1, blocks)]
            total = sum(jnp.sum(s, axis=0, keepdims=True) for s in soft)
            lse_ref[0, pair, h : h + 1, :] = top + jnp.log(total)
            low = jnp.concatenate([s.astype(BF) for s in soft], axis=0)
            out = jnp.dot(values_t[h * head : (h + 1) * head], low, preferred_element_type=F32)
            outs.append(out / total)
        o_ref[0, :, at] = jnp.concatenate(outs, axis=0).T.astype(BF)

def attend(kind, info, queries, q_at, keyed, k_at, valued, v_at, group=1):
    blocks, items, span, _ = keyed.shape
    count = queries.shape[2]
    pairs = HEADS // 2
    lanes = 128 * group
    width = pairs * 128
    return pl.pallas_call(
        functools.partial(attend_kernel, kind),
        out_shape=[jax.ShapeDtypeStruct((items, count, width), BF), jax.ShapeDtypeStruct((items, pairs, 2, count), F32)],
        grid_spec=pltpu.PrefetchScalarGridSpec(
            num_scalar_prefetch=1, grid=(items, pairs // group),
            in_specs=[
                pl.BlockSpec((1, 1, count, lanes), lambda i, p, s: (0, i, 0, p + q_at // lanes)),
                pl.BlockSpec((blocks, 1, span, lanes), lambda i, p, s: (0, i, 0, p + k_at // lanes)),
                pl.BlockSpec((blocks, 1, span, lanes), lambda i, p, s: (0, i, 0, p + v_at // lanes)),
            ],
            out_specs=[
                pl.BlockSpec((1, count, lanes), lambda i, p, s: (i, 0, p)),
                pl.BlockSpec((1, group, 2, count), lambda i, p, s: (i, p, 0, 0)),
            ]),
        compiler_params=pltpu.CompilerParams(vmem_limit_bytes=VMEM_LIMIT),
        cost_estimate=pl.CostEstimate(flops=8*items*count*blocks*span*width, bytes_accessed=2*(2*items*count*width+2*items*blocks*span*width), transcendentals=items*HEADS*count*blocks*span),
        name="attend",
    )(info, queries, keyed, valued)

def attend_back_kernel(kind, info_ref, q_ref, k_ref, v_ref, o_ref, lse_ref, do_ref, dq_ref, dk_ref, dv_ref):
    blocks, _, span, wide_lanes = k_ref.shape
    count = q_ref.shape[2]
    lanes = 128
    head = lanes // 2
    scaling = head ** -0.5
    low_lane = lax.broadcasted_iota(jnp.int32, (count, lanes), 1) < head
    allowed = allowed_keys(info_ref, kind, pl.program_id(0), span, count)
    outside = [shifts(info_ref, kind, j) for j in range(blocks)]
    for pair in range(wide_lanes // lanes):
        at = slice(pair * lanes, (pair + 1) * lanes)
        keys_t = k_ref[:, :, :, at].reshape(blocks * span, lanes).T
        queries = q_ref[0, 0, :, at] * scaling
        grad = do_ref[0, :, at]
        product_t = (grad.astype(F32) * o_ref[0, :, at].astype(F32)).T
        grad_q, dk, dv = [], [0.0] * blocks, [0.0] * blocks
        for h in range(2):
            lane = low_lane if h == 0 else ~low_lane
            mine = jnp.where(lane, queries, 0).astype(BF)
            grad_mine = jnp.where(lane, grad, 0).astype(BF)
            lse = lse_ref[0, pair, h : h + 1, :]
            delta = jnp.sum(product_t[h * head : (h + 1) * head], axis=0, keepdims=True)
            grads = []
            for j in range(blocks):
                scores = lax.dot_general(k_ref[j, 0, :, at], mine, (((1,), (1,)), ((), ())), preferred_element_type=F32)
                if j == 0:
                    soft = jnp.where(allowed, jnp.exp(scores - lse), 0.0)
                else:
                    soft = jnp.exp(scores - (lse + outside[j]))
                grad_soft = lax.dot_general(v_ref[j, 0, :, at], grad_mine, (((1,), (1,)), ((), ())), preferred_element_type=F32)
                grads.append((soft * (grad_soft - delta)).astype(BF))
                dv[j] += jnp.dot(soft.astype(BF), grad_mine, preferred_element_type=F32)
                dk[j] += jnp.dot(grads[j], mine, preferred_element_type=F32)
            grad_scores = jnp.concatenate(grads, axis=0)
            grad_q.append(jnp.dot(keys_t[h * head : (h + 1) * head], grad_scores, preferred_element_type=F32))
        dq_ref[0, :, at] = (jnp.concatenate(grad_q, axis=0) * scaling).T.astype(BF)
        for j in range(blocks):
            dk_ref[j, 0, :, at] = dk[j].astype(BF)
            dv_ref[j, 0, :, at] = dv[j].astype(BF)

def attend_back(kind, info, queries, q_at, keyed, k_at, valued, v_at, attended, lse, grad, group=1):
    blocks, items, span, _ = keyed.shape
    count = queries.shape[2]
    pairs = HEADS // 2
    lanes = 128 * group
    width = pairs * 128
    row = pl.BlockSpec((1, count, lanes), lambda i, p, s: (i, 0, p))
    key = pl.BlockSpec((blocks, 1, span, lanes), lambda i, p, s: (0, i, 0, p))
    return pl.pallas_call(
        functools.partial(attend_back_kernel, kind),
        out_shape=[jax.ShapeDtypeStruct((items, count, width), BF)] + [jax.ShapeDtypeStruct((blocks, items, span, width), BF)]*2,
        grid_spec=pltpu.PrefetchScalarGridSpec(
            num_scalar_prefetch=1, grid=(items, pairs // group),
            in_specs=[
                pl.BlockSpec((1, 1, count, lanes), lambda i, p, s: (0, i, 0, p + q_at // lanes)),
                pl.BlockSpec((blocks, 1, span, lanes), lambda i, p, s: (0, i, 0, p + k_at // lanes)),
                pl.BlockSpec((blocks, 1, span, lanes), lambda i, p, s: (0, i, 0, p + v_at // lanes)),
                row,
                pl.BlockSpec((1, group, 2, count), lambda i, p, s: (i, p, 0, 0)),
                row,
            ],
            out_specs=[row, key, key]),
        compiler_params=pltpu.CompilerParams(vmem_limit_bytes=VMEM_LIMIT),
        cost_estimate=pl.CostEstimate(flops=20*items*count*blocks*span*width, bytes_accessed=2*(4*items*count*width+4*items*blocks*span*width), transcendentals=items*HEADS*count*blocks*span),
        name="attend_back",
    )(info, queries, keyed, valued, attended, lse, grad)

def up_kernel(x_ref, w_ref, b_ref, act_ref, slope_ref):
    before = jnp.dot(x_ref[...], w_ref[...], preferred_element_type=F32) + b_ref[...]
    phi = 0.5 + 0.5 * lax.erf(before * (0.5 ** 0.5))
    act_ref[...] = (before * phi).astype(BF)
    slope_ref[...] = (phi + before * (jnp.exp(-0.5 * before * before) * 0.3989422804014327)).astype(BF)

def up_gelu(x, w, bias, block=512):
    rows, depth = x.shape
    hidden = w.shape[1]
    return pl.pallas_call(
        up_kernel,
        out_shape=[jax.ShapeDtypeStruct((rows, hidden), BF)] * 2,
        grid=(hidden // block,),
        in_specs=[pl.BlockSpec((rows, depth), lambda n: (0, 0)), pl.BlockSpec((depth, block), lambda n: (0, n)), pl.BlockSpec((1, block), lambda n: (0, n))],
        out_specs=[pl.BlockSpec((rows, block), lambda n: (0, n))]*2,
        compiler_params=pltpu.CompilerParams(vmem_limit_bytes=VMEM_LIMIT),
        cost_estimate=pl.CostEstimate(flops=2*rows*depth*hidden, bytes_accessed=2*(rows*depth+depth*hidden+2*rows*hidden), transcendentals=2*rows*hidden),
        name="up_gelu",
    )(x, w, bias)


def flat(tensor):
    return tensor.reshape(-1, tensor.shape[-1])


def flat_blocks(tensor):
    return tensor.reshape(-1, *tensor.shape[2:])


def dot(left, right):
    return jnp.dot(left, right, preferred_element_type=F32)


def dot_t(left, right):
    return lax.dot_general(
        left, right, (((left.ndim - 1,), (1,)), ((), ())), preferred_element_type=F32
    )


def hop_seq(values, step):
    size = lax.axis_size("seq")
    return hop(values, lambda i: i // size * size + (i % size ^ step))


def sum_seq(values):
    size = lax.axis_size("seq")
    step = 1
    total = values.astype(BF)
    while step < size:
        total = wide(total) + wide(hop_seq(total, step))
        step *= 2
        if step < size:
            total = total.astype(BF)
    return total


def gather_seq(values):
    step = lax.axis_size("seq") // 2
    blocks = {0: values}
    while step:
        blocks.update({j ^ step: hop_seq(b, step) for j, b in list(blocks.items())})
        step //= 2
    return jnp.stack([blocks[j] for j in range(len(blocks))])


def scatter_seq(blocks):
    size = lax.axis_size("seq")
    blocks = {j: blocks[j] for j in range(size)}
    step = 1
    while step < size:
        blocks = {
            j: b + wide(hop_seq(blocks[j ^ step].astype(BF), step))
            for j, b in blocks.items()
            if not j & step
        }
        step *= 2
    return blocks[0]


def body(
    tokens,
    captions,
    caption_lengths,
    cotangent,
    self_gain,
    self_shift,
    self_in_weight,
    self_out_weight,
    cross_gain,
    cross_shift,
    cross_query_weight,
    cross_memory_weight,
    cross_out_weight,
    feed_gain,
    feed_shift,
    up_weight,
    up_bias,
    down_weight,
    down_bias,
):
    features = tokens.shape[2]
    k_bias = up_weight.shape[1] // features
    small = pack_small(
        [self_gain, self_shift, cross_gain, cross_shift, feed_gain, feed_shift, down_bias], up_bias
    )
    groups = (
        (
            self_in_weight[:, :features],
            self_in_weight[:, features : 2 * features],
            self_in_weight[:, 2 * features :],
            self_out_weight,
            small,
        ),
        (cross_query_weight, cross_memory_weight, cross_out_weight),
        (up_weight,),
    )
    shards = [s for g in groups for s in g]
    rows = chip_rows(shards)
    blocks, widths, start = [], [], 0
    for group in groups:
        widths.append(tuple(s.shape[1] // 2 for s in group))
        blocks.append(rows[:, start : start + sum(widths[-1])])
        start += sum(widths[-1])
    blocks.append(chip_rows([down_weight]))
    widths.append((down_weight.shape[1] // 2,))
    ga, gb, gc, gd = (Gather(b) for b in blocks)
    size = lax.axis_size("seq")
    line = Line()
    tokens_y = hop_seq(tokens, 2)
    ga.far(line)
    tokens_1 = hop_seq(tokens, 1)
    ga.first(line)
    gb.far(line)
    ga.near(line)
    gb.first(line)
    gc.far(line)
    tokens_y = after(tokens_y, *line.last)
    tokens_3 = hop_seq(tokens_y, 1)
    gd.far(line)
    ga.second(line)
    gc.first(line)
    all_tokens = line(lambda a, b, c, d: jnp.stack([d, b, c, a]), tokens_3, tokens_1, tokens_y, tokens)
    gb.near(line)
    ga.pair(line)
    gb.second(line)
    gc.near(line)
    (self_q, self_k, self_v, self_out, small_full) = line(
        lambda *p: assemble(p, widths[0]), *ga.pieces()
    )
    vectors, up_offset = unpack_small(small_full, 7, k_bias)
    self_gain, self_shift, cross_gain, cross_shift, feed_gain, feed_shift, down_offset = (
        wide(v) for v in vectors
    )
    up_offset = wide(up_offset)
    seq_place = lax.axis_index("seq").astype(jnp.int32)[None]

    inputs = wide(tokens)
    normed1 = line(
        lambda g, t, s: normalize(wide(t), g, s).astype(BF), self_gain, all_tokens, self_shift
    )
    normed1 = lax.optimization_barrier(normed1)
    queries = line(lambda a, w: dot(a[0], w).astype(BF)[None], normed1, self_q)
    key_rows = line(lambda a, w: dot(a, w).astype(BF), normed1, self_k)
    value_rows = line(lambda a, w: dot(a, w).astype(BF), normed1, self_v)
    gd.first(line)
    gb.pair(line)
    gc.second(line)
    gd.near(line)
    attended1, lse1 = line(
        lambda q: attend("causal", seq_place, q, 0, key_rows, 0, value_rows, 0, 2), queries
    )
    gc.pair(line)
    gd.second(line)
    cross_query, cross_memory, cross_out = line(lambda *p: assemble(p, widths[1]), *gb.pieces())
    residual1 = line(lambda a: inputs + dot(a, self_out), attended1)

    normed2 = line(lambda r: normalize(r, cross_gain, cross_shift).astype(BF), residual1)
    normed2 = lax.optimization_barrier(normed2)
    cross_queries = line(lambda a: dot(a, cross_query).astype(BF)[None], normed2)
    memory = line(lambda a: dot(a, cross_memory).astype(BF)[None], captions)
    attended2, lse2 = line(
        lambda q: attend("length", caption_lengths, q, 0, memory, 0, memory, features, 8),
        cross_queries,
    )
    gd.pair(line)
    residual2 = line(lambda a: residual1 + dot(a, cross_out), attended2)

    normed3 = line(lambda r: normalize(r, feed_gain, feed_shift).astype(BF), residual2)
    normed3 = lax.optimization_barrier(normed3)
    (up,) = line(lambda *p: assemble(p, widths[2]), *gc.pieces())
    activated, slope = line(lambda a: up_gelu(flat(a), up, up_offset[None]), normed3)
    low3 = flat(cotangent)
    s1 = Scatter(line, [(activated, low3)])
    (down,) = line(lambda *p: assemble(p, widths[3]), *gd.pieces())
    s1.second(line)

    grad_before = line(lambda g: (dot_t(g, down) * wide(slope)).astype(BF), low3)
    s2 = Scatter(line, [(flat(normed3), grad_before)])
    s2.second(line)

    def back3(g):
        d = dot_t(g, up).reshape(inputs.shape)
        grad_in, gain, shift = norm_back(residual2, feed_gain, d)
        out = wide(cotangent) + grad_in
        return out, out.astype(BF), gain, shift

    grad_second, low2, grad_feed_gain, grad_feed_shift = line(back3, grad_before)

    s1.near(line)
    grad_attended2 = line(lambda g: dot_t(g, cross_out).astype(BF), low2)
    grad_cq, grad_mk, grad_mv = line(
        lambda g: attend_back(
            "length", caption_lengths, cross_queries, 0, memory, 0, memory, features,
            attended2, lse2, g, 8,
        ),
        grad_attended2,
    )
    grad_memory = line(lambda k, v: jnp.concatenate([k[0], v[0]], axis=-1), grad_mk, grad_mv)

    def back2(g):
        grad_in, gain, shift = norm_back(residual1, cross_gain, dot_t(g, cross_query))
        out = grad_second + grad_in
        return out, out.astype(BF), gain, shift

    grad_first, low1, grad_cross_gain, grad_cross_shift = line(back2, grad_cq)
    s1.first(line)
    s2.near(line)
    s3 = Scatter(
        line,
        [
            (flat(normed2), flat(grad_cq)),
            (flat(captions), flat(grad_memory)),
            (flat(attended2), flat(low2)),
            (flat(attended1), flat(low1)),
        ],
    )
    s1.far(line)
    s3.second(line)
    grad_attended1 = line(lambda g: dot_t(g, self_out).astype(BF), low1)
    s2.first(line)
    grad_q, grad_keys, grad_values = line(
        lambda g: attend_back(
            "causal", seq_place, queries, 0, key_rows, 0, value_rows, 0, attended1, lse1, g, 2
        ),
        grad_attended1,
    )
    s1.close(line)
    s2.far(line)
    s3.near(line)
    s4 = Scatter(
        line,
        [
            (flat(normed1[0]), flat(grad_q)),
            (flat(normed1), flat(grad_keys)),
            (flat(normed1), flat(grad_values)),
        ],
    )
    s4.second(line)
    grad_blocks = line(
        lambda k: dot_t(k, self_k) + dot_t(grad_values, self_v), grad_keys
    )
    grad_blocks = jnp.concatenate([grad_blocks[:1] + dot_t(grad_q, self_q)[None], grad_blocks[1:]])
    s3.first(line)
    _, grad_self_gain, grad_self_shift = norm_back(
        wide(flat_blocks(all_tokens)), self_gain, flat_blocks(grad_blocks)
    )
    (grad_down,) = s1.result(line)
    s4.near(line)
    s3.far(line)
    (final, grad_captions) = line(
        lambda a: (
            (residual2 + dot(a, down).reshape(inputs.shape) + down_offset).astype(BF),
            None,
        ),
        activated,
    )
    grad_captions = sum_seq(line(lambda a: dot_t(a, cross_memory), grad_memory))
    s2.close(line)
    grad_in1, _, _ = norm_back(inputs, self_gain, scatter_seq(grad_blocks))
    grad_up_bias = jnp.sum(wide(grad_before), axis=0)
    grad_down_bias = jnp.sum(wide(cotangent), axis=(0, 1))
    small_grads = pack_small_grads(
        [
            grad_self_gain,
            grad_self_shift,
            grad_cross_gain,
            grad_cross_shift,
            grad_feed_gain,
            grad_feed_shift,
            grad_down_bias,
        ],
        grad_up_bias,
    )
    s5 = Scatter(line, [(small_grads,)])
    s4.first(line)
    s5.second(line)
    (grad_up,) = s2.result(line)
    s3.close(line)
    s5.near(line)
    s4.far(line)
    s5.first(line)
    s5.far(line)
    grad_cross_query, grad_cross_memory, grad_cross_out, grad_self_out = s3.result(line)
    s4.close(line)
    s5.close(line)
    grad_self_q, grad_self_k, grad_self_v = s4.result(line)
    (small_out,) = s5.result(line)
    small_columns = small_out.T
    return (
        final,
        grad_first + grad_in1,
        grad_captions,
        small_columns[0],
        small_columns[1],
        jnp.concatenate([grad_self_q, grad_self_k, grad_self_v], axis=1),
        grad_self_out,
        small_columns[2],
        small_columns[3],
        grad_cross_query,
        grad_cross_memory,
        grad_cross_out,
        small_columns[4],
        small_columns[5],
        grad_up,
        small_columns[128 : 128 + k_bias].reshape(-1),
        grad_down,
        small_columns[6],
    )


def solution(mesh):
    tokens_spec = P("dp", "seq", None)
    rows1, rows2 = P(AXES), P(AXES, None)
    return jax.shard_map(
        body,
        mesh=mesh,
        in_specs=(
            tokens_spec, P("dp", None, None), P("dp"), tokens_spec,
            rows1, rows1, rows2, rows2, rows1, rows1, rows2, rows2, rows2,
            rows1, rows1, rows2, rows1, rows2, rows1,
        ),
        out_specs=(
            tokens_spec, tokens_spec, P("dp", None, None),
            rows1, rows1, rows2, rows2, rows1, rows1, rows2, rows2, rows2,
            rows1, rows1, rows2, rows1, rows2, rows1,
        ),
        check_vma=False,
    )
```

```python
import functools
import itertools

import jax
import jax.numpy as jnp
from jax import lax
from jax.experimental import pallas as pl
from jax.experimental.pallas import tpu as pltpu
from jax.sharding import PartitionSpec as P

HEADS = 16
AXES = ("dp", "seq")
BF = jnp.bfloat16
F32 = jnp.float32
epsilon = 1e-05
masked_score = -1e30
VMEM_LIMIT = 56 * 1024 * 1024


def device_count():
    return lax.axis_size("dp") * lax.axis_size("seq")


def place():
    index = lax.axis_index("dp") * lax.axis_size("seq") + lax.axis_index("seq")
    return index


def spots(core):
    index = place()
    c = index % 2
    half = c if core == "own" else 1 - c
    return jnp.stack(
        [half, (index // 4) % 2, (index // 2) % 2, (index // 8) % 2, index // 16]
    ).astype(jnp.int32)


def hop(values, change):
    count = device_count()
    pairs = [(i, change(i)) for i in range(count)]
    return lax.ppermute(values, AXES, pairs)


def hop_core(values):
    return hop(values, lambda i: i ^ 1)


def hop_first(values):
    return hop(values, lambda i: i ^ 4 if i % 2 == 0 else i ^ 2)


def hop_second(values):
    return hop(values, lambda i: i ^ 2 if i % 2 == 0 else i ^ 4)


def hop_z0(values):
    return hop(values, lambda i: i ^ 8)


def hop_z1(values, step):
    return hop(values, lambda i: i ^ (16 * step))


def far_count():
    return device_count() // 16


def column_half(values, half):
    width = values.shape[-1] // 2
    return lax.dynamic_slice_in_dim(values, half * width, width, values.ndim - 1)


def after(value, *others):
    return lax.optimization_barrier((value, *others))[0]


class Line:
    def __init__(self):
        self.last = ()

    def __call__(self, function, first, *rest):
        if self.last:
            first = after(first, *self.last)
        result = function(first, *rest)
        self.last = jax.tree.leaves(result)[:1]
        return result


class Gather:
    def __init__(self, shards):
        c = place() % 2
        self.mine = jnp.concatenate([column_half(s, c) for s in shards], axis=1)
        other = jnp.concatenate([column_half(s, 1 - c) for s in shards], axis=1)
        self.came = hop_core(other)

    def far(self, line):
        c = place() % 2
        self.sent = line(
            lambda came, mine: jnp.where(
                c == 0, jnp.concatenate([mine, came]), jnp.concatenate([came, mine])
            ),
            self.came,
            self.mine,
        )
        self.came = [hop_z1(self.sent, k) for k in range(1, far_count())]

    def first(self, line):
        self.sent = line(lambda c, s, *o: jnp.stack([s, *o, c]), self.came[-1], self.sent, *self.came[:-1])
        self.came = hop_first(self.sent)

    def near(self, line):
        self.sent = line(lambda c, s: jnp.stack([s, c]), self.came, self.sent)
        self.came = hop_z0(self.sent)

    def second(self, line):
        self.sent = line(lambda c, s: jnp.stack([s, c]), self.came, self.sent)
        self.came = hop_second(self.sent)
        self.sent_other = hop_core(self.sent)

    def pair(self, line):
        self.came = after(self.came, *line.last)
        self.came_other = hop_core(self.came)

    def pieces(self):
        return self.came_other, self.sent, self.came, self.sent_other


def fetch(spot_ref, pieces, targets, sems):
    far_other, near_own, far_own, near_other = pieces
    far, rows = near_own.shape[2], near_own.shape[3]
    c, mx, my, mz0, mz1 = (spot_ref[i] for i in range(5))
    started, start = [], 0
    for k, (target, first, both) in enumerate(targets):
        width = both // 2
        copies = []
        for half, sides in ((c, (near_own, far_own)), (1 - c, (near_other, far_other))):
            column = pl.multiple_of(first + half * width, 128)
            for d4, dz0, d2, dz1 in itertools.product(range(2), range(2), range(2), range(far)):
                x = jnp.where(half == 0, d2, d4) ^ mx
                y = jnp.where(half == 0, d4, d2) ^ my
                z = (dz1 ^ mz1) * 2 + (dz0 ^ mz0)
                row = pl.multiple_of(((z * 2 + x) * 2 + y) * rows, rows)
                copies.append(
                    pltpu.make_async_copy(
                        sides[d4].at[dz0, d2, dz1, :, pl.ds(start, width)],
                        target.at[pl.ds(row, rows), pl.ds(column, width)],
                        sems.at[k],
                    )
                )
        for copy in copies:
            copy.start()
        started.append(copies)
        start += width
    return started


def finish(copies):
    for copy in copies:
        copy.wait()


SHORT = pl.CostEstimate(flops=1, bytes_accessed=1, transcendentals=0)
ANY = pl.BlockSpec(memory_space=pl.ANY)
SMEM = pl.BlockSpec(memory_space=pltpu.SMEM)
VMEM = pl.BlockSpec(memory_space=pltpu.VMEM)


def call(kernel, name, outs, in_specs, out_specs, scratch, grid=()):
    return pl.pallas_call(
        kernel,
        out_shape=outs,
        grid=grid,
        in_specs=in_specs,
        out_specs=out_specs,
        scratch_shapes=scratch,
        compiler_params=pltpu.CompilerParams(vmem_limit_bytes=VMEM_LIMIT),
        cost_estimate=SHORT,
        name=name,
    )


def shaped(shape, dtype):
    return jax.ShapeDtypeStruct(tuple(shape), dtype)


def kdot(left, right):
    return jnp.dot(left, right, preferred_element_type=F32)


def kdot_t(left, right):
    return lax.dot_general(left, right, (((1,), (1,)), ((), ())), preferred_element_type=F32)


def unit_of(values):
    centered = values - jnp.mean(values, axis=-1, keepdims=True)
    inverse = lax.rsqrt(jnp.mean(centered * centered, axis=-1, keepdims=True) + epsilon)
    return centered * inverse, inverse


def unit_back(unit, inverse, grad_unit):
    return inverse * (
        grad_unit
        - jnp.mean(grad_unit, axis=-1, keepdims=True)
        - unit * jnp.mean(grad_unit * unit, axis=-1, keepdims=True)
    )


def project_kernel(
    spot_ref, token_ref, small_ref, p0, p1, p2, p3, p4, p5, p6, p7,
    a_ref, q_ref, k_ref, v_ref, w_ref, w, sems, out_sem,
):
    first = (pl.program_id(0) == 0) & (pl.program_id(1) == 0)
    last = (pl.program_id(0) == pl.num_programs(0) - 1) & (
        pl.program_id(1) == pl.num_programs(1) - 1
    )
    d = token_ref.shape[3]
    kept = pltpu.make_async_copy(w, w_ref, out_sem)

    @pl.when(first)
    def _():
        half = 3 * d // 2
        one = fetch(spot_ref, (p0, p1, p2, p3), [(w, 0, half)], sems)
        two = fetch(spot_ref, (p4, p5, p6, p7), [(w, half, half)], sems.at[pl.ds(1, 1)])
        finish(one[0])
        finish(two[0])
        kept.start()

    unit, _ = unit_of(token_ref[0, 0].astype(F32))
    normed = (unit * small_ref[0:1, :] + small_ref[1:2, :]).astype(BF)
    a_ref[0, 0] = normed
    k_ref[0, 0] = kdot(normed, w[:, d : 2 * d]).astype(BF)
    v_ref[0, 0] = kdot(normed, w[:, 2 * d :]).astype(BF)

    @pl.when(pl.program_id(0) == 0)
    def _():
        q_ref[0, 0] = kdot(normed, w[:, :d]).astype(BF)

    @pl.when(last)
    def _():
        kept.wait()


def project(tokens, small, pieces):
    blocks, items, count, d = tokens.shape
    block = pl.BlockSpec((1, 1, count, d), lambda b, i: (b, i, 0, 0))
    own = pl.BlockSpec(
        (1, 1, count, d), lambda b, i: (0, jnp.where(b == 0, i, items - 1), 0, 0)
    )
    big = shaped(tokens.shape, BF)
    return call(
        project_kernel,
        "project",
        [big, shaped((1, items, count, d), BF), big, big, shaped((d, 3 * d), BF)],
        [SMEM, block, pl.BlockSpec((16, d), lambda b, i: (0, 0))] + [ANY] * 8,
        [block, own, block, block, ANY],
        [pltpu.VMEM((d, 3 * d), BF), pltpu.SemaphoreType.DMA((2,)), pltpu.SemaphoreType.DMA],
        grid=(blocks, items),
    )(spots("own"), tokens, small, *pieces)


def mix_kernel(
    spot_ref, att_ref, token_ref, caption_ref, small_ref, p0, p1, p2, p3,
    r_ref, a_ref, cq_ref, memory_ref, wso_ref, wcq_ref, wcm_ref, wco_ref,
    wso, wcq, wcm, wco, sems, out_sems,
):
    weights = (wso, wcq, wcm, wco)
    targets = [(w, 0, w.shape[1]) for w in weights]
    groups = fetch(spot_ref, (p0, p1, p2, p3), targets, sems)
    kept = [
        pltpu.make_async_copy(w, out, out_sems.at[i])
        for i, (w, out) in enumerate(zip(weights, (wso_ref, wcq_ref, wcm_ref, wco_ref)))
    ]
    finish(groups[0])
    kept[0].start()
    residual = token_ref[...].astype(F32) + kdot(att_ref[...], wso[...])
    r_ref[...] = residual
    unit, _ = unit_of(residual)
    normed = (unit * small_ref[2:3, :] + small_ref[3:4, :]).astype(BF)
    a_ref[...] = normed
    finish(groups[1])
    kept[1].start()
    cq_ref[...] = kdot(normed, wcq[...]).astype(BF)
    finish(groups[2])
    kept[2].start()
    memory_ref[...] = kdot(caption_ref[...], wcm[...]).astype(BF)
    finish(groups[3])
    kept[3].start()
    finish(kept)


def mix(attended, tokens, captions, small, pieces):
    rows, d = tokens.shape
    weights = [(d, d), (d, d), (d, 2 * d), (d, d)]
    return call(
        mix_kernel,
        "mix",
        [shaped((rows, d), F32), shaped((rows, d), BF), shaped((rows, d), BF)]
        + [shaped((captions.shape[0], 2 * d), BF)]
        + [shaped(w, BF) for w in weights],
        [SMEM, VMEM, VMEM, VMEM, VMEM, ANY, ANY, ANY, ANY],
        [VMEM] * 4 + [ANY] * 4,
        [pltpu.VMEM(w, BF) for w in weights]
        + [pltpu.SemaphoreType.DMA((4,)), pltpu.SemaphoreType.DMA((4,))],
    )(spots("own"), attended, tokens, captions, small, *pieces)


def up_kernel(
    spot_ref, att_ref, r1_ref, wco_ref, small_ref, bias_ref, p0, p1, p2, p3,
    r2_ref, a_ref, act_ref, slope_ref, w_ref, w, sems, out_sem,
):
    n = pl.program_id(0)
    width = act_ref.shape[1]
    kept = pltpu.make_async_copy(w, w_ref, out_sem)

    @pl.when(n == 0)
    def _():
        (copies,) = fetch(spot_ref, (p0, p1, p2, p3), [(w, 0, w.shape[1])], sems)
        residual = r1_ref[...] + kdot(att_ref[...], wco_ref[...])
        r2_ref[...] = residual
        unit, _ = unit_of(residual)
        a_ref[...] = (unit * small_ref[4:5, :] + small_ref[5:6, :]).astype(BF)
        finish(copies)
        kept.start()

    part = w[:, pl.ds(pl.multiple_of(n * width, width), width)]
    before = kdot(a_ref[...], part) + bias_ref[...]
    phi = 0.5 + 0.5 * lax.erf(before * (0.5 ** 0.5))
    act_ref[...] = (before * phi).astype(BF)
    slope_ref[...] = (phi + before * (jnp.exp(-0.5 * before * before) * 0.3989422804014327)).astype(BF)

    @pl.when(n == pl.num_programs(0) - 1)
    def _():
        kept.wait()


def up_gelu(attended, residual, cross_out, small, bias, pieces, block=512):
    rows, d = residual.shape
    hidden = bias.shape[1]
    whole = pl.BlockSpec((rows, d), lambda n: (0, 0))
    column = pl.BlockSpec((rows, block), lambda n: (0, n))
    return call(
        up_kernel,
        "up_gelu",
        [shaped((rows, d), F32), shaped((rows, d), BF)]
        + [shaped((rows, hidden), BF)] * 2
        + [shaped((d, hidden), BF)],
        [
            SMEM, whole, whole, pl.BlockSpec((d, d), lambda n: (0, 0)),
            pl.BlockSpec((16, d), lambda n: (0, 0)), pl.BlockSpec((1, block), lambda n: (0, n)),
            ANY, ANY, ANY, ANY,
        ],
        [whole, whole, column, column, ANY],
        [pltpu.VMEM((d, hidden), BF), pltpu.SemaphoreType.DMA((1,)), pltpu.SemaphoreType.DMA],
        grid=(hidden // block,),
    )(spots("own"), attended, residual, cross_out, small, bias, *pieces)


def down_kernel(
    spot_ref, g_ref, slope_ref, act_ref, r2_ref, small_ref, p0, p1, p2, p3,
    out_ref, grad_ref, bias_ref, down_bias_ref, w, total, sems,
):
    n = pl.program_id(0)
    height = act_ref.shape[1]

    @pl.when(n == 0)
    def _():
        (copies,) = fetch(spot_ref, (p0, p1, p2, p3), [(w, 0, w.shape[1])], sems)
        total[...] = r2_ref[...] + small_ref[6:7, :]
        down_bias_ref[...] = jnp.sum(g_ref[...].astype(F32), axis=0, keepdims=True)
        finish(copies)

    part = w[pl.ds(pl.multiple_of(n * height, height), height), :]
    grad = (kdot_t(g_ref[...], part) * slope_ref[...].astype(F32)).astype(BF)
    grad_ref[...] = grad
    bias_ref[...] = jnp.sum(grad.astype(F32), axis=0, keepdims=True)
    total[...] += kdot(act_ref[...], part)

    @pl.when(n == pl.num_programs(0) - 1)
    def _():
        out_ref[...] = total[...].astype(BF)


def down_both(grad, slope, activated, residual, small, pieces, block=512):
    rows, d = residual.shape
    hidden = slope.shape[1]
    whole = pl.BlockSpec((rows, d), lambda n: (0, 0))
    column = pl.BlockSpec((rows, block), lambda n: (0, n))
    return call(
        down_kernel,
        "down",
        [shaped((rows, d), BF), shaped((rows, hidden), BF), shaped((1, hidden), F32), shaped((1, d), F32)],
        [SMEM, whole, column, column, whole, pl.BlockSpec((16, d), lambda n: (0, 0)), ANY, ANY, ANY, ANY],
        [whole, column, pl.BlockSpec((1, block), lambda n: (0, n)), pl.BlockSpec((1, d), lambda n: (0, 0))],
        [pltpu.VMEM((hidden, d), BF), pltpu.VMEM((rows, d), F32), pltpu.SemaphoreType.DMA((1,))],
        grid=(hidden // block,),
    )(spots("own"), grad, slope, activated, residual, small, *pieces)


def feed_back_kernel(
    g_ref, w_ref, r2_ref, cot_ref, small_ref, wco_ref, dr_ref, low_ref, datt_ref, vec_ref, total
):
    n = pl.program_id(0)

    @pl.when(n == 0)
    def _():
        total[...] = jnp.zeros_like(total)

    total[...] += kdot_t(g_ref[...], w_ref[...])

    @pl.when(n == pl.num_programs(0) - 1)
    def _():
        grad = total[...]
        unit, inverse = unit_of(r2_ref[...])
        vec_ref[0:1, :] = jnp.sum(grad * unit, axis=0, keepdims=True)
        vec_ref[1:2, :] = jnp.sum(grad, axis=0, keepdims=True)
        out = cot_ref[...].astype(F32) + unit_back(unit, inverse, grad * small_ref[4:5, :])
        dr_ref[...] = out
        low = out.astype(BF)
        low_ref[...] = low
        datt_ref[...] = kdot_t(low, wco_ref[...]).astype(BF)


def feed_back(grad, up, residual, cotangent, small, cross_out, block=1024):
    rows, d = residual.shape
    hidden = grad.shape[1]
    whole = pl.BlockSpec((rows, d), lambda n: (0, 0))
    return call(
        feed_back_kernel,
        "feed_back",
        [shaped((rows, d), F32), shaped((rows, d), BF), shaped((rows, d), BF), shaped((8, d), F32)],
        [
            pl.BlockSpec((rows, block), lambda n: (0, n)), pl.BlockSpec((d, block), lambda n: (0, n)),
            whole, whole, pl.BlockSpec((16, d), lambda n: (0, 0)), pl.BlockSpec((d, d), lambda n: (0, 0)),
        ],
        [whole, whole, whole, pl.BlockSpec((8, d), lambda n: (0, 0))],
        [pltpu.VMEM((rows, d), F32)],
        grid=(hidden // block,),
    )(grad, up, residual, cotangent, small, cross_out)


def cross_back_kernel(
    g_ref, wcq_ref, r1_ref, dr2_ref, small_ref, wso_ref, dr_ref, low_ref, datt_ref, vec_ref
):
    grad = kdot_t(g_ref[...], wcq_ref[...])
    unit, inverse = unit_of(r1_ref[...])
    vec_ref[0:1, :] = jnp.sum(grad * unit, axis=0, keepdims=True)
    vec_ref[1:2, :] = jnp.sum(grad, axis=0, keepdims=True)
    out = dr2_ref[...] + unit_back(unit, inverse, grad * small_ref[2:3, :])
    dr_ref[...] = out
    low = out.astype(BF)
    low_ref[...] = low
    datt_ref[...] = kdot_t(low, wso_ref[...]).astype(BF)


def cross_back(grad, cross_query, residual, grad_residual, small, self_out):
    rows, d = residual.shape
    return call(
        cross_back_kernel,
        "cross_back",
        [shaped((rows, d), F32), shaped((rows, d), BF), shaped((rows, d), BF), shaped((8, d), F32)],
        [VMEM] * 6,
        [VMEM] * 4,
        [],
    )(grad, cross_query, residual, grad_residual, small, self_out)


def self_back_kernel(
    dq0_ref, dk0_ref, dv0_ref, dq1_ref, dk1_ref, dv1_ref, token_ref, w_ref,
    cross_ref, feed_ref, down_ref, up_ref, *refs,
):
    *da_refs, vec_ref, own = refs
    first = (pl.program_id(0) == 0) & (pl.program_id(1) == 0)
    d = token_ref.shape[3]
    half = d // 2

    def back(ref, at):
        return kdot_t(ref[...].reshape(ref.shape[-2:]), w_ref[:, at : at + half])

    own[...] = (back(dk0_ref, d) + back(dk1_ref, d + half)) + (
        back(dv0_ref, 2 * d) + back(dv1_ref, 2 * d + half)
    )

    @pl.when(pl.program_id(0) == 0)
    def _():
        own[...] += back(dq0_ref, 0) + back(dq1_ref, half)

    grad = own[...]
    for b, da_ref in enumerate(da_refs):

        @pl.when(pl.program_id(0) == b)
        def _():
            da_ref[0] = grad.astype(BF)

    unit, _ = unit_of(token_ref[0, 0].astype(F32))
    gain = jnp.sum(grad * unit, axis=0, keepdims=True)
    shift = jnp.sum(grad, axis=0, keepdims=True)

    @pl.when(first)
    def _():
        vec_ref[0:1, :] = gain
        vec_ref[1:2, :] = shift
        vec_ref[2:4, :] = cross_ref[0:2, :]
        vec_ref[4:6, :] = feed_ref[0:2, :]
        vec_ref[6:7, :] = down_ref[...]
        for k in range(up_ref.shape[1] // d):
            vec_ref[7 + k : 8 + k, :] = up_ref[:, k * d : (k + 1) * d]

    @pl.when(jnp.logical_not(first))
    def _():
        vec_ref[0:1, :] += gain
        vec_ref[1:2, :] += shift


def self_back(grads, tokens, weight, cross, feed, down, up):
    blocks, items, count, d = tokens.shape
    block = pl.BlockSpec((1, 1, count, d), lambda b, i: (b, i, 0, 0))
    part = pl.BlockSpec((1, 1, count, d // 2), lambda b, i: (b, i, 0, 0))

    def only(at):
        return lambda b, i: (jnp.where(b == at, i, jnp.where(b < at, 0, items - 1)), 0, 0)

    def whole(array):
        return pl.BlockSpec(array.shape, lambda b, i: (0, 0))

    own = pl.BlockSpec((1, count, d // 2), only(0))
    height = 7 + up.shape[1] // d
    return call(
        self_back_kernel,
        "self_back",
        [shaped((items, count, d), BF)] * blocks + [shaped((height, d), F32)],
        [own, part, part, own, part, part, block]
        + [whole(a) for a in (weight, cross, feed, down, up)],
        [pl.BlockSpec((1, count, d), only(b)) for b in range(blocks)]
        + [pl.BlockSpec((height, d), lambda b, i: (0, 0))],
        [pltpu.VMEM((count, d), F32)],
        grid=(blocks, items),
    )(*grads, tokens, weight, cross, feed, down, up)


def wgrad_kernel(kinds, rows, side, spot_ref, *refs):
    half, mx, my, mz0 = (spot_ref[i] for i in range(4))
    scratch = refs[-1]
    outs = refs[-5:-1] if side == "other" else refs[-3:-1]
    at, start = 0, 0
    for kind in kinds:
        if kind == "dot":
            left, right = refs[at], refs[at + 1]
            at += 2
            block = lax.dot_general(
                left[...], right[...], (((0,), (0,)), ((), ())), preferred_element_type=F32
            )
        else:
            block = refs[at][...].astype(F32)
            at += 1
        scratch[:, start : start + block.shape[1]] = block
        start += block.shape[1]
    for d4, dz0, d2 in itertools.product(range(2), range(2), range(2)):
        x = jnp.where(half == 0, d2, d4) ^ mx
        y = jnp.where(half == 0, d4, d2) ^ my
        j = ((dz0 ^ mz0) * 2 + x) * 2 + y
        part = scratch[pl.ds(pl.multiple_of(j * rows, rows), rows), :]
        if side == "other":
            outs[d4 * 2 + dz0][d2, 0] = part.astype(BF)
        else:
            came = refs[at + d4 * 2 + dz0]
            outs[d4][dz0, d2, 0] = (part + came[d2, 0].astype(F32)).astype(BF)


def wgrad(terms, side, came=None):
    far = far_count()
    kinds = tuple("dot" if len(t) == 2 else "raw" for t in terms)
    height = terms[0][0].shape[1] if kinds[0] == "dot" else terms[0][0].shape[0]
    rows = height // (8 * far)
    specs, args, total = [], [], 0
    for term in terms:
        right = term[-1]
        width = right.shape[1] // 2
        if len(term) == 2:
            left = term[0]
            specs.append(pl.BlockSpec((left.shape[0], 8 * rows), lambda z, s: (0, z)))
            specs.append(pl.BlockSpec((right.shape[0], width), lambda z, s: (0, s[0])))
        else:
            specs.append(pl.BlockSpec((8 * rows, width), lambda z, s: (z, s[0])))
        args += list(term)
        total += width
    piece = pl.BlockSpec((2, 1, rows, total), lambda z, s: (0, z ^ s[4], 0, 0))
    part = pl.BlockSpec((2, 2, 1, rows, total), lambda z, s: (0, 0, z ^ s[4], 0, 0))
    if side == "other":
        out_shape, out_specs = [shaped((2, far, rows, total), BF)] * 4, [piece] * 4
    else:
        specs += [piece] * 4
        args += came
        out_shape, out_specs = [shaped((2, 2, far, rows, total), BF)] * 2, [part] * 2
    return pl.pallas_call(
        functools.partial(wgrad_kernel, kinds, rows, side),
        out_shape=out_shape,
        grid_spec=pltpu.PrefetchScalarGridSpec(
            num_scalar_prefetch=1,
            grid=(far,),
            in_specs=specs,
            out_specs=out_specs,
            scratch_shapes=[pltpu.VMEM((8 * rows, total), F32)],
        ),
        compiler_params=pltpu.CompilerParams(vmem_limit_bytes=VMEM_LIMIT),
        cost_estimate=SHORT,
        name="wgrad",
    )(spots(side), *args)


def wide(values):
    return values.astype(F32)


class Scatter:
    def __init__(self, line, terms):
        self.widths = [t[-1].shape[1] // 2 for t in terms]

        self.terms = terms
        sent = line(lambda f: wgrad([(f, *terms[0][1:]), *terms[1:]], "other"), terms[0][0])
        self.came0 = [hop_core(v) for v in sent]

    def second(self, line):
        self.own, sent = line(lambda *c: wgrad(self.terms, "own", c), *self.came0)
        self.came1 = hop_second(sent)

    def near(self, line):
        def add(c1, o):
            return (wide(o[1]) + wide(c1[1])).astype(BF)

        self.came2 = hop_z0(line(add, self.came1, self.own))

    def first(self, line):
        def add(c2, c1, o):
            return (wide(o[0, 1]) + wide(c1[0, 1]) + wide(c2[1])).astype(BF)

        self.came3 = hop_first(line(add, self.came2, self.came1, self.own))

    def far(self, line):
        def add(c3, c2, c1, o):
            kept = wide(o[0, 0]) + wide(c1[0, 0]) + wide(c2[0]) + wide(c3)
            return kept.astype(BF), kept[0]

        low, self.kept = line(add, self.came3, self.came2, self.came1, self.own)
        self.came4 = [hop_z1(low[k], k) for k in range(1, far_count())]

    def close(self, line):
        total = line(lambda c, t, *o: sum(map(wide, o), t + wide(c)), self.came4[-1], self.kept, *self.came4[:-1])
        rows = total.shape[0] // 2
        c = place() % 2
        self.mine = lax.dynamic_slice_in_dim(total, c * rows, rows, 0)
        self.theirs = hop_core(lax.dynamic_slice_in_dim(total, (1 - c) * rows, rows, 0))

    def result(self, line):
        c = place() % 2

        def join(came, mine):
            left = jnp.where(c == 0, mine, came)
            right = jnp.where(c == 0, came, mine)
            results, start = [], 0
            for width in self.widths:
                at = slice(start, start + width)
                results.append(jnp.concatenate([left[:, at], right[:, at]], axis=1))
                start += width
            return results

        return line(join, self.theirs, self.mine)


class SmallSum:
    def __init__(self, values):
        self.values, self.distance = values, 1
        self.send()

    def send(self):
        self.came = hop(self.values, lambda i: i ^ self.distance)

    def step(self, line):
        self.values = line(lambda c, v: c + v, self.came, self.values)
        self.distance *= 2
        if self.distance < device_count():
            self.send()

    def finish(self, line):
        while self.distance < device_count():
            self.step(line)
        return self.values


def small_rows(vectors, bias):
    n = device_count()
    part = vectors[0].shape[0]
    width = part * n
    rows = jnp.zeros((len(vectors), width), BF)
    rows = lax.dynamic_update_slice(rows, jnp.stack(vectors), (0, place() * part))
    long = jnp.zeros((bias.shape[0] * n,), BF)
    long = lax.dynamic_update_slice(long, bias, (place() * bias.shape[0],))
    return jnp.concatenate([rows, long.reshape(-1, width)])


def small_parts(rows, count):
    n = device_count()
    part = rows.shape[1] // n
    own = lax.dynamic_slice_in_dim(rows[:count], place() * part, part, 1)
    long = rows[count:].reshape(-1)
    share = long.shape[0] // n
    return [own[i] for i in range(count)], lax.dynamic_slice_in_dim(long, place() * share, share)


def shifts(info_ref, kind, block):
    if kind == "length" or block == 0:
        return None
    me = info_ref[0]
    return jnp.where((me ^ block) < me, 0.0, -masked_score).astype(F32)

def allowed_keys(info_ref, kind, item, span, count):
    shape = (span, count)
    row = lax.broadcasted_iota(jnp.int32, shape, 0)
    if kind == "length":
        return row < info_ref[item]
    return row <= lax.broadcasted_iota(jnp.int32, shape, 1)

def attend_kernel(kind, info_ref, q_ref, k_ref, v_ref, o_ref, lse_ref):
    blocks, _, span, wide_lanes = k_ref.shape
    count = q_ref.shape[2]
    lanes = 128
    head = lanes // 2
    low_lane = lax.broadcasted_iota(jnp.int32, (count, lanes), 1) < head
    allowed = allowed_keys(info_ref, kind, pl.program_id(0), span, count)
    outside = [shifts(info_ref, kind, j) for j in range(blocks)]
    for pair in range(wide_lanes // lanes):
        at = slice(pair * lanes, (pair + 1) * lanes)
        values_t = v_ref[:, :, :, at].reshape(blocks * span, lanes).T
        queries = q_ref[0, 0, :, at] * (head ** -0.5)
        outs = []
        for h in range(2):
            mine = jnp.where(low_lane if h == 0 else ~low_lane, queries, 0).astype(BF)
            scores = [
                lax.dot_general(k_ref[j, 0, :, at], mine, (((1,), (1,)), ((), ())), preferred_element_type=F32)
                for j in range(blocks)
            ]
            scores[0] = jnp.where(allowed, scores[0], masked_score)
            top = jnp.max(scores[0], axis=0, keepdims=True)
            for j in range(1, blocks):
                top = jnp.maximum(top, jnp.max(scores[j], axis=0, keepdims=True) - outside[j])
            soft = [jnp.exp(scores[0] - top)]
            soft += [jnp.exp(scores[j] - (top + outside[j])) for j in range(1, blocks)]
            total = sum(jnp.sum(s, axis=0, keepdims=True) for s in soft)
            lse_ref[0, pair, h : h + 1, :] = top + jnp.log(total)
            low = jnp.concatenate([s.astype(BF) for s in soft], axis=0)
            out = jnp.dot(values_t[h * head : (h + 1) * head], low, preferred_element_type=F32)
            outs.append(out / total)
        o_ref[0, :, at] = jnp.concatenate(outs, axis=0).T.astype(BF)

def attend(kind, info, queries, q_at, keyed, k_at, valued, v_at, group=1):
    blocks, items, span, _ = keyed.shape
    count = queries.shape[2]
    pairs = HEADS // 2
    lanes = 128 * group
    width = pairs * 128
    return pl.pallas_call(
        functools.partial(attend_kernel, kind),
        out_shape=[jax.ShapeDtypeStruct((items, count, width), BF), jax.ShapeDtypeStruct((items, pairs, 2, count), F32)],
        grid_spec=pltpu.PrefetchScalarGridSpec(
            num_scalar_prefetch=1, grid=(items, pairs // group),
            in_specs=[
                pl.BlockSpec((1, 1, count, lanes), lambda i, p, s: (0, i, 0, p + q_at // lanes)),
                pl.BlockSpec((blocks, 1, span, lanes), lambda i, p, s: (0, i, 0, p + k_at // lanes)),
                pl.BlockSpec((blocks, 1, span, lanes), lambda i, p, s: (0, i, 0, p + v_at // lanes)),
            ],
            out_specs=[
                pl.BlockSpec((1, count, lanes), lambda i, p, s: (i, 0, p)),
                pl.BlockSpec((1, group, 2, count), lambda i, p, s: (i, p, 0, 0)),
            ]),
        compiler_params=pltpu.CompilerParams(vmem_limit_bytes=VMEM_LIMIT),
        cost_estimate=SHORT,
        name="attend",
    )(info, queries, keyed, valued)

def attend_back_kernel(kind, info_ref, q_ref, k_ref, v_ref, o_ref, lse_ref, do_ref, dq_ref, dk_ref, dv_ref):
    blocks, _, span, wide_lanes = k_ref.shape
    count = q_ref.shape[2]
    lanes = 128
    head = lanes // 2
    scaling = head ** -0.5
    low_lane = lax.broadcasted_iota(jnp.int32, (count, lanes), 1) < head
    allowed = allowed_keys(info_ref, kind, pl.program_id(0), span, count)
    outside = [shifts(info_ref, kind, j) for j in range(blocks)]
    for pair in range(wide_lanes // lanes):
        at = slice(pair * lanes, (pair + 1) * lanes)
        keys_t = k_ref[:, :, :, at].reshape(blocks * span, lanes).T
        queries = q_ref[0, 0, :, at] * scaling
        grad = do_ref[0, :, at]
        product_t = (grad.astype(F32) * o_ref[0, :, at].astype(F32)).T
        grad_q, dk, dv = [], [0.0] * blocks, [0.0] * blocks
        for h in range(2):
            lane = low_lane if h == 0 else ~low_lane
            mine = jnp.where(lane, queries, 0).astype(BF)
            grad_mine = jnp.where(lane, grad, 0).astype(BF)
            lse = lse_ref[0, pair, h : h + 1, :]
            delta = jnp.sum(product_t[h * head : (h + 1) * head], axis=0, keepdims=True)
            grads = []
            for j in range(blocks):
                scores = lax.dot_general(k_ref[j, 0, :, at], mine, (((1,), (1,)), ((), ())), preferred_element_type=F32)
                if j == 0:
                    soft = jnp.where(allowed, jnp.exp(scores - lse), 0.0)
                else:
                    soft = jnp.exp(scores - (lse + outside[j]))
                grad_soft = lax.dot_general(v_ref[j, 0, :, at], grad_mine, (((1,), (1,)), ((), ())), preferred_element_type=F32)
                grads.append((soft * (grad_soft - delta)).astype(BF))
                dv[j] += jnp.dot(soft.astype(BF), grad_mine, preferred_element_type=F32)
                dk[j] += jnp.dot(grads[j], mine, preferred_element_type=F32)
            grad_scores = jnp.concatenate(grads, axis=0)
            grad_q.append(jnp.dot(keys_t[h * head : (h + 1) * head], grad_scores, preferred_element_type=F32))
        dq_ref[0, :, at] = (jnp.concatenate(grad_q, axis=0) * scaling).T.astype(BF)
        for j in range(blocks):
            dk_ref[j, 0, :, at] = dk[j].astype(BF)
            dv_ref[j, 0, :, at] = dv[j].astype(BF)

def attend_back(kind, info, queries, q_at, keyed, k_at, valued, v_at, attended, lse, grad, group=1, part=(0, 1)):
    blocks, items, span, _ = keyed.shape
    count = queries.shape[2]
    pairs = HEADS // 2 // part[1]
    skip = part[0] * pairs // group
    lanes = 128 * group
    width = pairs * 128
    row = pl.BlockSpec((1, count, lanes), lambda i, p, s: (i, 0, p + skip))
    out = pl.BlockSpec((1, count, lanes), lambda i, p, s: (i, 0, p))
    key = pl.BlockSpec((blocks, 1, span, lanes), lambda i, p, s: (0, i, 0, p))
    return pl.pallas_call(
        functools.partial(attend_back_kernel, kind),
        out_shape=[jax.ShapeDtypeStruct((items, count, width), BF)] + [jax.ShapeDtypeStruct((blocks, items, span, width), BF)]*2,
        grid_spec=pltpu.PrefetchScalarGridSpec(
            num_scalar_prefetch=1, grid=(items, pairs // group),
            in_specs=[
                pl.BlockSpec((1, 1, count, lanes), lambda i, p, s: (0, i, 0, p + skip + q_at // lanes)),
                pl.BlockSpec((blocks, 1, span, lanes), lambda i, p, s: (0, i, 0, p + skip + k_at // lanes)),
                pl.BlockSpec((blocks, 1, span, lanes), lambda i, p, s: (0, i, 0, p + skip + v_at // lanes)),
                row,
                pl.BlockSpec((1, group, 2, count), lambda i, p, s: (i, p + skip, 0, 0)),
                row,
            ],
            out_specs=[out, key, key]),
        compiler_params=pltpu.CompilerParams(vmem_limit_bytes=VMEM_LIMIT),
        cost_estimate=SHORT,
        name="attend_back",
    )(info, queries, keyed, valued, attended, lse, grad)

def flat(tensor):
    return tensor.reshape(-1, tensor.shape[-1])


def dot_t(left, right):
    return lax.dot_general(
        left, right, (((left.ndim - 1,), (1,)), ((), ())), preferred_element_type=F32
    )


def hop_seq(values, step):
    size = lax.axis_size("seq")
    return hop(values, lambda i: i // size * size + (i % size ^ step))


def body(
    tokens,
    captions,
    caption_lengths,
    cotangent,
    self_gain,
    self_shift,
    self_in_weight,
    self_out_weight,
    cross_gain,
    cross_shift,
    cross_query_weight,
    cross_memory_weight,
    cross_out_weight,
    feed_gain,
    feed_shift,
    up_weight,
    up_bias,
    down_weight,
    down_bias,
):
    features = tokens.shape[2]
    k_bias = up_weight.shape[1] // features
    half = 3 * features // 2
    ga = Gather([self_in_weight[:, :half]])
    line = Line()
    ga.far(line)
    tokens_y = hop_seq(tokens, 2)
    tokens_1 = hop_seq(tokens, 1)
    ge = Gather([self_in_weight[:, half:]])
    gb = Gather([self_out_weight, cross_query_weight, cross_memory_weight, cross_out_weight])
    gc = Gather([up_weight])
    gd = Gather([down_weight])
    small = SmallSum(
        small_rows(
            [self_gain, self_shift, cross_gain, cross_shift, feed_gain, feed_shift, down_bias],
            up_bias,
        )
    )
    ga.first(line)
    ge.far(line)
    ga.near(line)
    ge.first(line)
    ga.second(line)
    ge.near(line)
    small.step(line)
    gb.far(line)
    small.step(line)
    tokens_y = after(tokens_y, *line.last)
    tokens_3 = hop_seq(tokens_y, 1)
    ga.pair(line)
    ge.second(line)
    small.step(line)
    gb.first(line)
    small.step(line)
    small_low = small.finish(line)
    small_full = line(
        lambda v: jnp.pad(wide(v), ((0, 16 - v.shape[0]), (0, 0))), small_low
    )
    up_offset = wide(small_low[7:]).reshape(1, -1)
    all_tokens = line(lambda a, b, c, d: jnp.stack([d, b, c, a]), tokens_3, tokens_1, tokens_y, tokens)
    ge.pair(line)
    gb.near(line)
    gc.far(line)
    seq_place = lax.axis_index("seq").astype(jnp.int32)[None]

    normed1, queries, key_rows, value_rows, self_in = line(
        lambda t: project(t, small_full, ga.pieces() + ge.pieces()), all_tokens
    )
    gc.first(line)
    gb.second(line)
    gc.near(line)
    gd.far(line)
    attended1, lse1 = line(
        lambda q: attend("causal", seq_place, q, 0, key_rows, 0, value_rows, 0, 2), queries
    )
    gb.pair(line)
    gd.first(line)
    gc.second(line)
    gd.near(line)
    flat_tokens, flat_captions = flat(tokens), flat(captions)
    residual1, normed2, cross_queries, memory, self_out, cross_query, cross_memory, cross_out = line(
        lambda a: mix(flat(a), flat_tokens, flat_captions, small_full, gb.pieces()), attended1
    )
    cross_queries = cross_queries.reshape(1, *tokens.shape)
    memory = memory.reshape(1, *captions.shape[:2], -1)

    attended2, lse2 = line(
        lambda q: attend("length", caption_lengths, q, 0, memory, 0, memory, features, 8),
        cross_queries,
    )
    gc.pair(line)
    gd.second(line)

    residual2, normed3, activated, slope, up = line(
        lambda a: up_gelu(flat(a), residual1, cross_out, small_full, up_offset, gc.pieces()),
        attended2,
    )
    low3 = flat(cotangent)
    s1 = Scatter(line, [(activated, low3)])
    gd.pair(line)

    final, grad_before, grad_up_bias, grad_down_bias = line(
        lambda g: down_both(g, slope, activated, residual2, small_full, gd.pieces()), low3
    )
    s1.second(line)
    s2 = Scatter(line, [(normed3, grad_before)])
    grad_second, low2, grad_attended2, grad_feed = line(
        lambda g: feed_back(g, up, residual2, low3, small_full, cross_out), grad_before
    )
    s2.second(line)

    grad_attended2 = grad_attended2.reshape(tokens.shape)
    grad_cq, grad_mk, grad_mv = line(
        lambda g: attend_back(
            "length", caption_lengths, cross_queries, 0, memory, 0, memory, features,
            attended2, lse2, g, 8,
        ),
        grad_attended2,
    )
    s1.near(line)
    grad_cq = flat(grad_cq)
    grad_first, low1, grad_attended1, grad_cross = line(
        lambda g: cross_back(g, cross_query, residual1, grad_second, small_full, self_out), grad_cq
    )
    grad_memory = line(
        lambda k, v: jnp.concatenate([flat(k), flat(v)], axis=-1), grad_mk, grad_mv
    )
    caption_sum = line(lambda a: dot_t(a, cross_memory).astype(BF), grad_memory)
    caption_came = hop_seq(caption_sum, 1)
    s3 = Scatter(
        line,
        [
            (normed2, grad_cq),
            (flat_captions, grad_memory),
            (flat(attended2), low2),
            (flat(attended1), low1),
        ],
    )

    grad_attended1 = grad_attended1.reshape(tokens.shape)
    flat_normed1 = flat(normed1)

    def heads_back(i):
        return line(
            lambda g: attend_back(
                "causal", seq_place, queries, 0, key_rows, 0, value_rows, 0, attended1, lse1, g, 2,
                (i, 2),
            ),
            grad_attended1,
        )

    def heads_terms(grads):
        return [
            (flat_normed1[: low1.shape[0]], flat(grads[0])),
            (flat_normed1, flat(grads[1])),
            (flat_normed1, flat(grads[2])),
        ]

    s2.near(line)
    grads_a = heads_back(0)
    s1.first(line)
    s3.second(line)
    s4 = Scatter(line, heads_terms(grads_a))
    caption_sum = line(lambda c, v: (wide(c) + wide(v)).astype(BF), caption_came, caption_sum)
    caption_came = hop_seq(caption_sum, 2)
    s1.far(line)
    grads_b = heads_back(1)
    s2.first(line)
    s3.near(line)
    s5 = Scatter(line, heads_terms(grads_b))
    s4.second(line)
    s2.far(line)
    s1.close(line)
    s5.second(line)
    s4.near(line)
    *grad_blocks, small_grads = line(
        lambda g, *o: self_back(
            (g, *o, *grads_b), all_tokens, self_in, grad_cross, grad_feed, grad_down_bias, grad_up_bias
        ),
        *grads_a,
    )
    grad_ones = hop_seq(grad_blocks[1], 1)
    grad_threes = hop_seq(grad_blocks[3], 1)
    small = SmallSum(small_grads)
    s3.first(line)
    s5.near(line)
    grad_far = line(lambda a, b: (wide(a) + wide(b)).astype(BF), grad_threes, grad_blocks[2])
    grad_twos = hop_seq(grad_far, 2)
    s4.first(line)
    small.step(line)
    s2.close(line)
    small.step(line)
    s3.far(line)
    small.step(line)
    (grad_down,) = s1.result(line)
    s4.far(line)
    small.step(line)
    s5.first(line)
    small.step(line)
    (grad_up,) = s2.result(line)
    s3.close(line)
    grad_captions = line(lambda c, v: wide(c) + wide(v), caption_came, caption_sum)
    grad_captions = grad_captions.reshape(captions.shape)
    small_parts_out, grad_bias = small_parts(small.finish(line), 7)

    def last_norm(came, one, own):
        grad = wide(own) + wide(one) + wide(came)
        unit, inverse = unit_of(wide(tokens))
        return grad_first.reshape(tokens.shape) + unit_back(unit, inverse, grad * small_full[0])

    s5.far(line)
    grad_tokens = line(last_norm, grad_twos, grad_ones, grad_blocks[0])
    s4.close(line)
    results3 = s3.result(line)
    grad_cross_query, grad_cross_memory, grad_cross_out, grad_self_out = results3
    s5.close(line)
    grads_4 = s4.result(line)
    grads_5 = s5.result(line)
    return (
        final.reshape(tokens.shape),
        grad_tokens,
        grad_captions,
        small_parts_out[0],
        small_parts_out[1],
        jnp.concatenate([g for pair in zip(grads_4, grads_5) for g in pair], axis=1),
        grad_self_out,
        small_parts_out[2],
        small_parts_out[3],
        grad_cross_query,
        grad_cross_memory,
        grad_cross_out,
        small_parts_out[4],
        small_parts_out[5],
        grad_up,
        grad_bias,
        grad_down,
        small_parts_out[6],
    )


def solution(mesh):
    tokens_spec = P("dp", "seq", None)
    rows1, rows2 = P(AXES), P(AXES, None)
    return jax.shard_map(
        body,
        mesh=mesh,
        in_specs=(
            tokens_spec, P("dp", None, None), P("dp"), tokens_spec,
            rows1, rows1, rows2, rows2, rows1, rows1, rows2, rows2, rows2,
            rows1, rows1, rows2, rows1, rows2, rows1,
        ),
        out_specs=(
            tokens_spec, tokens_spec, P("dp", None, None),
            rows1, rows1, rows2, rows2, rows1, rows1, rows2, rows2, rows2,
            rows1, rows1, rows2, rows1, rows2, rows1,
        ),
        check_vma=False,
    )
```

```python
import functools
import itertools

import jax
import jax.numpy as jnp
from jax import lax
from jax.experimental import pallas as pl
from jax.experimental.pallas import tpu as pltpu
from jax.sharding import PartitionSpec as P

HEADS = 16
AXES = ("dp", "seq")
BF = jnp.bfloat16
F32 = jnp.float32
epsilon = 1e-05
masked_score = -1e30
VMEM_LIMIT = 56 * 1024 * 1024


def device_count():
    return lax.axis_size("dp") * lax.axis_size("seq")


def place():
    index = lax.axis_index("dp") * lax.axis_size("seq") + lax.axis_index("seq")
    return index


def spots(core):
    index = place()
    c = index % 2
    half = c if core == "own" else 1 - c
    return jnp.stack(
        [half, (index // 4) % 2, (index // 2) % 2, (index // 8) % 2, index // 16]
    ).astype(jnp.int32)


def hop(values, change):
    count = device_count()
    pairs = [(i, change(i)) for i in range(count)]
    return lax.ppermute(values, AXES, pairs)


def hop_core(values):
    return hop(values, lambda i: i ^ 1)


def hop_first(values):
    return hop(values, lambda i: i ^ 4 if i % 2 == 0 else i ^ 2)


def hop_second(values):
    return hop(values, lambda i: i ^ 2 if i % 2 == 0 else i ^ 4)


def hop_z0(values):
    return hop(values, lambda i: i ^ 8)


def hop_z1(values, step):
    return hop(values, lambda i: i ^ (16 * step))


def far_count():
    return device_count() // 16


def column_half(values, half):
    width = values.shape[-1] // 2
    return lax.dynamic_slice_in_dim(values, half * width, width, values.ndim - 1)


def after(value, *others):
    return lax.optimization_barrier((value, *others))[0]


class Line:
    def __init__(self):
        self.last = ()

    def __call__(self, function, first, *rest, whole=False):
        if self.last and whole:
            first, *rest = lax.optimization_barrier((first, *rest, *self.last))[: 1 + len(rest)]
        elif self.last:
            first = after(first, *self.last)
        result = function(first, *rest)
        self.last = jax.tree.leaves(result)[:1]
        return result


class Gather:
    def __init__(self, line, shards):
        c = place() % 2

        def split(*parts):
            return [
                jnp.concatenate([column_half(p, half) for p in parts], axis=1)
                for half in (1 - c, c)
            ]

        other, self.mine = line(split, *shards, whole=True)
        self.came = hop_core(other)

    def far(self, line):
        c = place() % 2
        self.sent = line(
            lambda came, mine: jnp.where(
                c == 0, jnp.concatenate([mine, came]), jnp.concatenate([came, mine])
            ),
            self.came,
            self.mine,
        )
        self.came = [hop_z1(self.sent, k) for k in range(1, far_count())]

    def first(self, line):
        self.sent = line(lambda c, s, *o: jnp.stack([s, *o, c]), self.came[-1], self.sent, *self.came[:-1])
        self.came = hop_first(self.sent)

    def near(self, line):
        self.sent = line(lambda c, s: jnp.stack([s, c]), self.came, self.sent)
        self.came = hop_z0(self.sent)

    def second(self, line):
        self.sent = line(lambda c, s: jnp.stack([s, c]), self.came, self.sent)
        self.came = hop_second(self.sent)
        self.sent_other = hop_core(self.sent)

    def pair(self, line):
        self.came = line(lambda v: v, self.came)
        self.came_other = hop_core(self.came)

    def pieces(self):
        return self.came_other, self.sent, self.came, self.sent_other


def fetch(spot_ref, pieces, targets, sems):
    far_other, near_own, far_own, near_other = pieces
    far, rows = near_own.shape[2], near_own.shape[3]
    c, mx, my, mz0, mz1 = (spot_ref[i] for i in range(5))
    started, start = [], 0
    for k, (target, first, both) in enumerate(targets):
        width = both // 2
        copies = []
        for half, sides in ((c, (near_own, far_own)), (1 - c, (near_other, far_other))):
            column = pl.multiple_of(first + half * width, 128)
            for d4, dz0, d2, dz1 in itertools.product(range(2), range(2), range(2), range(far)):
                x = jnp.where(half == 0, d2, d4) ^ mx
                y = jnp.where(half == 0, d4, d2) ^ my
                z = (dz1 ^ mz1) * 2 + (dz0 ^ mz0)
                row = pl.multiple_of(((z * 2 + x) * 2 + y) * rows, rows)
                copies.append(
                    pltpu.make_async_copy(
                        sides[d4].at[dz0, d2, dz1, :, pl.ds(start, width)],
                        target.at[pl.ds(row, rows), pl.ds(column, width)],
                        sems.at[k],
                    )
                )
        for copy in copies:
            copy.start()
        started.append(copies)
        start += width
    return started


def finish(copies):
    for copy in copies:
        copy.wait()


SHORT = pl.CostEstimate(flops=1, bytes_accessed=1, transcendentals=0)
ANY = pl.BlockSpec(memory_space=pl.ANY)
SMEM = pl.BlockSpec(memory_space=pltpu.SMEM)
VMEM = pl.BlockSpec(memory_space=pltpu.VMEM)


def call(kernel, name, outs, in_specs, out_specs, scratch, grid=()):
    return pl.pallas_call(
        kernel,
        out_shape=outs,
        grid=grid,
        in_specs=in_specs,
        out_specs=out_specs,
        scratch_shapes=scratch,
        compiler_params=pltpu.CompilerParams(vmem_limit_bytes=VMEM_LIMIT),
        cost_estimate=SHORT,
        name=name,
    )


def shaped(shape, dtype):
    return jax.ShapeDtypeStruct(tuple(shape), dtype)


def kdot(left, right):
    return jnp.dot(left, right, preferred_element_type=F32)


def kdot_t(left, right):
    return lax.dot_general(left, right, (((1,), (1,)), ((), ())), preferred_element_type=F32)


def unit_of(values):
    centered = values - jnp.mean(values, axis=-1, keepdims=True)
    inverse = lax.rsqrt(jnp.mean(centered * centered, axis=-1, keepdims=True) + epsilon)
    return centered * inverse, inverse


def unit_back(unit, inverse, grad_unit):
    return inverse * (
        grad_unit
        - jnp.mean(grad_unit, axis=-1, keepdims=True)
        - unit * jnp.mean(grad_unit * unit, axis=-1, keepdims=True)
    )


def project_kernel(
    spot_ref, token_ref, p0, p1, p2, p3, p4, p5, p6, p7,
    a_ref, q_ref, k_ref, v_ref, small_ref, w_ref, w, packed, vectors, sems, out_sem,
):
    _, items, count, d = token_ref.shape
    kept = pltpu.make_async_copy(w, w_ref, out_sem)

    @pl.when(pl.program_id(0) == 0)
    def _():
        half = 3 * d // 2
        one = fetch(spot_ref, (p0, p1, p2, p3), [(w, 0, half)], sems.at[pl.ds(0, 1)])
        two = fetch(
            spot_ref, (p4, p5, p6, p7), [(w, half, half), (packed, 0, 256)], sems.at[pl.ds(1, 2)]
        )
        finish(two[1])
        vectors[...] = packed[...].astype(F32).T
        small_ref[...] = vectors[0:16, :]
        finish(one[0])
        finish(two[0])
        kept.start()

    unit, _ = unit_of(token_ref[...].reshape(items * count, d).astype(F32))
    normed = (unit * vectors[0:1, :] + vectors[1:2, :]).astype(BF)
    a_ref[...] = normed.reshape(a_ref.shape)
    k_ref[...] = kdot(normed, w[:, d : 2 * d]).astype(BF).reshape(k_ref.shape)
    v_ref[...] = kdot(normed, w[:, 2 * d :]).astype(BF).reshape(v_ref.shape)

    @pl.when(pl.program_id(0) == 0)
    def _():
        q_ref[...] = kdot(normed, w[:, :d]).astype(BF).reshape(q_ref.shape)

    @pl.when(pl.program_id(0) == pl.num_programs(0) - 1)
    def _():
        kept.wait()


def project(tokens, pieces):
    blocks, items, count, d = tokens.shape
    block = pl.BlockSpec((1, items, count, d), lambda b: (b, 0, 0, 0))
    own = pl.BlockSpec((1, items, count, d), lambda b: (0, 0, 0, 0))
    big = shaped(tokens.shape, BF)
    return call(
        project_kernel,
        "project",
        [big, shaped((1, items, count, d), BF), big, big, shaped((16, d), F32), shaped((d, 3 * d), BF)],
        [SMEM, block] + [ANY] * 8,
        [block, own, block, block, pl.BlockSpec((16, d), lambda b: (0, 0)), ANY],
        [
            pltpu.VMEM((d, 3 * d), BF),
            pltpu.VMEM((d, 256), BF),
            pltpu.VMEM((256, d), F32),
            pltpu.SemaphoreType.DMA((3,)),
            pltpu.SemaphoreType.DMA,
        ],
        grid=(blocks,),
    )(spots("own"), tokens, *pieces)


def mix_kernel(
    spot_ref, att0_ref, att1_ref, token_ref, small_ref, p0, p1, p2, p3,
    r_ref, a_ref, cq_ref, wso_ref, wcq_ref, wso, wcq, sems, out_sems,
):
    weights = (wso, wcq)
    groups = fetch(spot_ref, (p0, p1, p2, p3), [(w, 0, w.shape[1]) for w in weights], sems)
    kept = [
        pltpu.make_async_copy(w, out, out_sems.at[i])
        for i, (w, out) in enumerate(zip(weights, (wso_ref, wcq_ref)))
    ]
    finish(groups[0])
    kept[0].start()
    half = att0_ref.shape[1]
    residual = token_ref[...].astype(F32) + (
        kdot(att0_ref[...], wso[:half]) + kdot(att1_ref[...], wso[half:])
    )
    r_ref[...] = residual
    unit, _ = unit_of(residual)
    normed = (unit * small_ref[2:3, :] + small_ref[3:4, :]).astype(BF)
    a_ref[...] = normed
    finish(groups[1])
    kept[1].start()
    cq_ref[...] = kdot(normed, wcq[...]).astype(BF)
    finish(kept)


def mix(attended0, attended1, tokens, small, pieces):
    rows, d = tokens.shape
    return call(
        mix_kernel,
        "mix",
        [shaped((rows, d), F32), shaped((rows, d), BF), shaped((rows, d), BF)]
        + [shaped((d, d), BF)] * 2,
        [SMEM, VMEM, VMEM, VMEM, VMEM] + [ANY] * 4,
        [VMEM] * 3 + [ANY] * 2,
        [pltpu.VMEM((d, d), BF)] * 2
        + [pltpu.SemaphoreType.DMA((2,)), pltpu.SemaphoreType.DMA((2,))],
    )(spots("own"), attended0, attended1, tokens, small, *pieces)


def memory_kernel(
    spot_ref, caption_ref, p0, p1, p2, p3, memory_ref, wcm_ref, wco_ref, wcm, wco, sems, out_sems
):
    weights = (wcm, wco)
    groups = fetch(spot_ref, (p0, p1, p2, p3), [(w, 0, w.shape[1]) for w in weights], sems)
    kept = [
        pltpu.make_async_copy(w, out, out_sems.at[i])
        for i, (w, out) in enumerate(zip(weights, (wcm_ref, wco_ref)))
    ]
    finish(groups[0])
    kept[0].start()
    memory_ref[...] = kdot(caption_ref[...], wcm[...]).astype(BF)
    finish(groups[1])
    kept[1].start()
    finish(kept)


def remember(captions, pieces):
    rows, d = captions.shape
    weights = [(d, 2 * d), (d, d)]
    return call(
        memory_kernel,
        "memory",
        [shaped((rows, 2 * d), BF)] + [shaped(w, BF) for w in weights],
        [SMEM, VMEM] + [ANY] * 4,
        [VMEM] + [ANY] * 2,
        [pltpu.VMEM(w, BF) for w in weights]
        + [pltpu.SemaphoreType.DMA((2,)), pltpu.SemaphoreType.DMA((2,))],
    )(spots("own"), captions, *pieces)


def up_kernel(
    spot_ref, att_ref, r1_ref, wco_ref, small_ref, bias_ref, p0, p1, p2, p3,
    r2_ref, a_ref, act_ref, slope_ref, w_ref, w, sems, out_sem,
):
    n = pl.program_id(0)
    width = act_ref.shape[1]
    kept = pltpu.make_async_copy(w, w_ref, out_sem)

    @pl.when(n == 0)
    def _():
        (copies,) = fetch(spot_ref, (p0, p1, p2, p3), [(w, 0, w.shape[1])], sems)
        residual = r1_ref[...] + kdot(att_ref[...], wco_ref[...])
        r2_ref[...] = residual
        unit, _ = unit_of(residual)
        a_ref[...] = (unit * small_ref[4:5, :] + small_ref[5:6, :]).astype(BF)
        finish(copies)
        kept.start()

    part = w[:, pl.ds(pl.multiple_of(n * width, width), width)]
    before = kdot(a_ref[...], part) + bias_ref[...]
    phi = 0.5 + 0.5 * lax.erf(before * (0.5 ** 0.5))
    act_ref[...] = (before * phi).astype(BF)
    slope_ref[...] = (phi + before * (jnp.exp(-0.5 * before * before) * 0.3989422804014327)).astype(BF)

    @pl.when(n == pl.num_programs(0) - 1)
    def _():
        kept.wait()


def up_gelu(attended, residual, cross_out, small, bias, pieces, block=512):
    rows, d = residual.shape
    hidden = bias.shape[1]
    whole = pl.BlockSpec((rows, d), lambda n: (0, 0))
    column = pl.BlockSpec((rows, block), lambda n: (0, n))
    return call(
        up_kernel,
        "up_gelu",
        [shaped((rows, d), F32), shaped((rows, d), BF)]
        + [shaped((rows, hidden), BF)] * 2
        + [shaped((d, hidden), BF)],
        [
            SMEM, whole, whole, pl.BlockSpec((d, d), lambda n: (0, 0)),
            pl.BlockSpec((16, d), lambda n: (0, 0)), pl.BlockSpec((1, block), lambda n: (0, n)),
            ANY, ANY, ANY, ANY,
        ],
        [whole, whole, column, column, ANY],
        [pltpu.VMEM((d, hidden), BF), pltpu.SemaphoreType.DMA((1,)), pltpu.SemaphoreType.DMA],
        grid=(hidden // block,),
    )(spots("own"), attended, residual, cross_out, small, bias, *pieces)


def down_kernel(
    spot_ref, g_ref, slope_ref, act_ref, r2_ref, small_ref, p0, p1, p2, p3,
    out_ref, grad_ref, bias_ref, down_bias_ref, w, total, sems,
):
    n = pl.program_id(0)
    height = act_ref.shape[1]

    @pl.when(n == 0)
    def _():
        (copies,) = fetch(spot_ref, (p0, p1, p2, p3), [(w, 0, w.shape[1])], sems)
        total[...] = r2_ref[...] + small_ref[6:7, :]
        down_bias_ref[...] = jnp.sum(g_ref[...].astype(F32), axis=0, keepdims=True)
        finish(copies)

    part = w[pl.ds(pl.multiple_of(n * height, height), height), :]
    grad = (kdot_t(g_ref[...], part) * slope_ref[...].astype(F32)).astype(BF)
    grad_ref[...] = grad
    bias_ref[...] = jnp.sum(grad.astype(F32), axis=0, keepdims=True)
    total[...] += kdot(act_ref[...], part)

    @pl.when(n == pl.num_programs(0) - 1)
    def _():
        out_ref[...] = total[...].astype(BF)


def down_both(grad, slope, activated, residual, small, pieces, block=512):
    rows, d = residual.shape
    hidden = slope.shape[1]
    whole = pl.BlockSpec((rows, d), lambda n: (0, 0))
    column = pl.BlockSpec((rows, block), lambda n: (0, n))
    return call(
        down_kernel,
        "down",
        [shaped((rows, d), BF), shaped((rows, hidden), BF), shaped((1, hidden), F32), shaped((1, d), F32)],
        [SMEM, whole, column, column, whole, pl.BlockSpec((16, d), lambda n: (0, 0)), ANY, ANY, ANY, ANY],
        [whole, column, pl.BlockSpec((1, block), lambda n: (0, n)), pl.BlockSpec((1, d), lambda n: (0, 0))],
        [pltpu.VMEM((hidden, d), BF), pltpu.VMEM((rows, d), F32), pltpu.SemaphoreType.DMA((1,))],
        grid=(hidden // block,),
    )(spots("own"), grad, slope, activated, residual, small, *pieces)


def feed_back_kernel(
    g_ref, w_ref, r2_ref, cot_ref, small_ref, wco_ref, dr_ref, low_ref, datt_ref, vec_ref, total
):
    n = pl.program_id(0)

    @pl.when(n == 0)
    def _():
        total[...] = jnp.zeros_like(total)

    total[...] += kdot_t(g_ref[...], w_ref[...])

    @pl.when(n == pl.num_programs(0) - 1)
    def _():
        grad = total[...]
        unit, inverse = unit_of(r2_ref[...])
        vec_ref[0:1, :] = jnp.sum(grad * unit, axis=0, keepdims=True)
        vec_ref[1:2, :] = jnp.sum(grad, axis=0, keepdims=True)
        out = cot_ref[...].astype(F32) + unit_back(unit, inverse, grad * small_ref[4:5, :])
        dr_ref[...] = out
        low = out.astype(BF)
        low_ref[...] = low
        datt_ref[...] = kdot_t(low, wco_ref[...]).astype(BF)


def feed_back(grad, up, residual, cotangent, small, cross_out, block=1024):
    rows, d = residual.shape
    hidden = grad.shape[1]
    whole = pl.BlockSpec((rows, d), lambda n: (0, 0))
    return call(
        feed_back_kernel,
        "feed_back",
        [shaped((rows, d), F32), shaped((rows, d), BF), shaped((rows, d), BF), shaped((8, d), F32)],
        [
            pl.BlockSpec((rows, block), lambda n: (0, n)), pl.BlockSpec((d, block), lambda n: (0, n)),
            whole, whole, pl.BlockSpec((16, d), lambda n: (0, 0)), pl.BlockSpec((d, d), lambda n: (0, 0)),
        ],
        [whole, whole, whole, pl.BlockSpec((8, d), lambda n: (0, 0))],
        [pltpu.VMEM((rows, d), F32)],
        grid=(hidden // block,),
    )(grad, up, residual, cotangent, small, cross_out)


def cross_back_kernel(
    g_ref, wcq_ref, r1_ref, dr2_ref, small_ref, wso_ref, dr_ref, low_ref, datt_ref, vec_ref
):
    grad = kdot_t(g_ref[...], wcq_ref[...])
    unit, inverse = unit_of(r1_ref[...])
    vec_ref[0:1, :] = jnp.sum(grad * unit, axis=0, keepdims=True)
    vec_ref[1:2, :] = jnp.sum(grad, axis=0, keepdims=True)
    out = dr2_ref[...] + unit_back(unit, inverse, grad * small_ref[2:3, :])
    dr_ref[...] = out
    low = out.astype(BF)
    low_ref[...] = low
    datt_ref[...] = kdot_t(low, wso_ref[...]).astype(BF)


def cross_back(grad, cross_query, residual, grad_residual, small, self_out):
    rows, d = residual.shape
    return call(
        cross_back_kernel,
        "cross_back",
        [shaped((rows, d), F32), shaped((rows, d), BF), shaped((rows, d), BF), shaped((8, d), F32)],
        [VMEM] * 6,
        [VMEM] * 4,
        [],
    )(grad, cross_query, residual, grad_residual, small, self_out)


def self_back_kernel(
    dq0_ref, dk0_ref, dv0_ref, dq1_ref, dk1_ref, dv1_ref, token_ref, w_ref,
    cross_ref, feed_ref, down_ref, up_ref, *refs,
):
    *da_refs, vec_ref, own = refs
    b = pl.program_id(0)
    _, items, count, d = token_ref.shape
    half = d // 2

    def back(ref, at):
        return kdot_t(ref[...].reshape(items * count, half), w_ref[:, at : at + half])

    own[...] = (back(dk0_ref, d) + back(dk1_ref, d + half)) + (
        back(dv0_ref, 2 * d) + back(dv1_ref, 2 * d + half)
    )

    @pl.when(b == 0)
    def _():
        own[...] += back(dq0_ref, 0) + back(dq1_ref, half)
        vec_ref[0:2, :] = jnp.zeros((2, d), F32)
        vec_ref[2:4, :] = cross_ref[0:2, :]
        vec_ref[4:6, :] = feed_ref[0:2, :]
        vec_ref[6:7, :] = down_ref[...]
        for k in range(up_ref.shape[1] // d):
            vec_ref[7 + k : 8 + k, :] = up_ref[:, k * d : (k + 1) * d]

    grad = own[...]
    for k in range(len(da_refs) // items):

        @pl.when(b == k)
        def _():
            for i in range(items):
                da_refs[k * items + i][...] = grad[i * count : (i + 1) * count].astype(BF)

    unit, _ = unit_of(token_ref[...].reshape(items * count, d).astype(F32))
    vec_ref[0:1, :] += jnp.sum(grad * unit, axis=0, keepdims=True)
    vec_ref[1:2, :] += jnp.sum(grad, axis=0, keepdims=True)


def self_back(grads, tokens, weight, cross, feed, down, up):
    blocks, items, count, d = tokens.shape
    block = pl.BlockSpec((1, items, count, d), lambda b: (b, 0, 0, 0))
    part = pl.BlockSpec((1, items, count, d // 2), lambda b: (b, 0, 0, 0))

    height = 7 + up.shape[1] // d

    def whole(array):
        return pl.BlockSpec(array.shape, lambda b: (0,) * array.ndim)

    return call(
        self_back_kernel,
        "self_back",
        [shaped((count, d), BF)] * (blocks * items) + [shaped((height, d), F32)],
        [whole(grads[0]), part, part, whole(grads[3]), part, part, block]
        + [whole(a) for a in (weight, cross, feed, down, up)],
        [pl.BlockSpec((count, d), lambda b: (0, 0))] * (blocks * items)
        + [pl.BlockSpec((height, d), lambda b: (0, 0))],
        [pltpu.VMEM((items * count, d), F32)],
        grid=(blocks,),
    )(*grads, tokens, weight, cross, feed, down, up)


def wgrad_kernel(kinds, rows, side, spot_ref, *refs):
    half, mx, my, mz0 = (spot_ref[i] for i in range(4))
    scratch = refs[-1]
    outs = refs[-5:-1] if side == "other" else refs[-3:-1]
    at, start = 0, 0
    for kind in kinds:
        if kind == "dot":
            left, right = refs[at], refs[at + 1]
            at += 2
            block = lax.dot_general(
                left[...], right[...], (((0,), (0,)), ((), ())), preferred_element_type=F32
            )
        else:
            block = refs[at][...].astype(F32)
            at += 1
        scratch[:, start : start + block.shape[1]] = block
        start += block.shape[1]
    for d4, dz0, d2 in itertools.product(range(2), range(2), range(2)):
        x = jnp.where(half == 0, d2, d4) ^ mx
        y = jnp.where(half == 0, d4, d2) ^ my
        j = ((dz0 ^ mz0) * 2 + x) * 2 + y
        part = scratch[pl.ds(pl.multiple_of(j * rows, rows), rows), :]
        if side == "other":
            outs[d4 * 2 + dz0][d2, 0] = part.astype(BF)
        else:
            came = refs[at + d4 * 2 + dz0]
            outs[d4][dz0, d2, 0] = (part + came[d2, 0].astype(F32)).astype(BF)


def wgrad(terms, side, came=None):
    far = far_count()
    kinds = tuple("dot" if len(t) == 2 else "raw" for t in terms)
    height = terms[0][0].shape[1] if kinds[0] == "dot" else terms[0][0].shape[0]
    rows = height // (8 * far)
    specs, args, total = [], [], 0
    for term in terms:
        right = term[-1]
        width = right.shape[1] // 2
        if len(term) == 2:
            left = term[0]
            specs.append(pl.BlockSpec((left.shape[0], 8 * rows), lambda z, s: (0, z)))
            specs.append(pl.BlockSpec((right.shape[0], width), lambda z, s: (0, s[0])))
        else:
            specs.append(pl.BlockSpec((8 * rows, width), lambda z, s: (z, s[0])))
        args += list(term)
        total += width
    piece = pl.BlockSpec((2, 1, rows, total), lambda z, s: (0, z ^ s[4], 0, 0))
    part = pl.BlockSpec((2, 2, 1, rows, total), lambda z, s: (0, 0, z ^ s[4], 0, 0))
    if side == "other":
        out_shape, out_specs = [shaped((2, far, rows, total), BF)] * 4, [piece] * 4
    else:
        specs += [piece] * 4
        args += came
        out_shape, out_specs = [shaped((2, 2, far, rows, total), BF)] * 2, [part] * 2
    return pl.pallas_call(
        functools.partial(wgrad_kernel, kinds, rows, side),
        out_shape=out_shape,
        grid_spec=pltpu.PrefetchScalarGridSpec(
            num_scalar_prefetch=1,
            grid=(far,),
            in_specs=specs,
            out_specs=out_specs,
            scratch_shapes=[pltpu.VMEM((8 * rows, total), F32)],
        ),
        compiler_params=pltpu.CompilerParams(vmem_limit_bytes=VMEM_LIMIT),
        cost_estimate=SHORT,
        name="wgrad",
    )(spots(side), *args)


def wide(values):
    return values.astype(F32)


class Scatter:
    def __init__(self, line, terms):
        self.widths = [t[-1].shape[1] // 2 for t in terms]

        self.terms = terms
        sent = line(lambda f: wgrad([(f, *terms[0][1:]), *terms[1:]], "other"), terms[0][0])
        self.came0 = [hop_core(v) for v in sent]

    def second(self, line):
        self.own, sent = line(lambda *c: wgrad(self.terms, "own", c), *self.came0)
        self.came1 = hop_second(sent)

    def near(self, line):
        def add(c1, o):
            return (wide(o[1]) + wide(c1[1])).astype(BF)

        self.came2 = hop_z0(line(add, self.came1, self.own))

    def first(self, line):
        def add(c2, c1, o):
            return (wide(o[0, 1]) + wide(c1[0, 1]) + wide(c2[1])).astype(BF)

        self.came3 = hop_first(line(add, self.came2, self.came1, self.own))

    def far(self, line):
        def add(c3, c2, c1, o):
            kept = wide(o[0, 0]) + wide(c1[0, 0]) + wide(c2[0]) + wide(c3)
            return kept.astype(BF), kept[0]

        low, self.kept = line(add, self.came3, self.came2, self.came1, self.own)
        self.came4 = [hop_z1(low[k], k) for k in range(1, far_count())]

    def close(self, line):
        total = line(lambda c, t, *o: sum(map(wide, o), t + wide(c)), self.came4[-1], self.kept, *self.came4[:-1])
        rows = total.shape[0] // 2
        c = place() % 2
        self.mine = lax.dynamic_slice_in_dim(total, c * rows, rows, 0)
        self.theirs = hop_core(lax.dynamic_slice_in_dim(total, (1 - c) * rows, rows, 0))

    def result(self, line):
        c = place() % 2

        def join(came, mine):
            left = jnp.where(c == 0, mine, came)
            right = jnp.where(c == 0, came, mine)
            results, start = [], 0
            for width in self.widths:
                at = slice(start, start + width)
                results.append(jnp.concatenate([left[:, at], right[:, at]], axis=1))
                start += width
            return results

        return line(join, self.theirs, self.mine)


def pack_small(vectors, bias):
    r = vectors[0].shape[0]
    k = bias.shape[0] // r
    rows = jnp.concatenate([jnp.stack(vectors), bias.reshape(k, r)])
    return jnp.pad(rows.T, ((0, 0), (0, 256 - rows.shape[0])))


def offset_rows(rows):
    k, d = rows.shape
    n = device_count()
    return rows.reshape(k, n, d // n).transpose(1, 0, 2).reshape(1, k * d)


class SmallSum:
    def __init__(self, values):
        self.values = values
        far = 16
        self.distances = [1, 4]
        while far < device_count():
            self.distances.append(far)
            far *= 2
        self.distances += [8, 2]
        self.send()

    def send(self):
        distance = self.distances.pop(0)
        self.came = hop(self.values, lambda i: i ^ distance)

    def step(self, line):
        self.values = line(lambda c, v: c + v, self.came, self.values)
        if self.distances:
            self.send()
            return True
        return False

    def parts(self, line, count):
        while self.step(line):
            pass
        rows = self.values
        n = device_count()
        part = rows.shape[1] // n
        own = lax.dynamic_slice_in_dim(rows[:count], place() * part, part, 1)
        long = rows[count:].reshape(-1)
        share = long.shape[0] // n
        return own, lax.dynamic_slice_in_dim(long, place() * share, share)


def shifts(info_ref, kind, block):
    if kind == "length" or block == 0:
        return None
    me = info_ref[0]
    return jnp.where((me ^ block) < me, 0.0, -masked_score).astype(F32)

def allowed_keys(info_ref, kind, item, span, count):
    shape = (span, count)
    row = lax.broadcasted_iota(jnp.int32, shape, 0)
    if kind == "length":
        return row < info_ref[item]
    return row <= lax.broadcasted_iota(jnp.int32, shape, 1)

def attend_kernel(kind, info_ref, q_ref, k_ref, v_ref, o_ref, lse_ref):
    blocks, _, span, wide_lanes = k_ref.shape
    count = q_ref.shape[2]
    lanes = 128
    head = lanes // 2
    low_lane = lax.broadcasted_iota(jnp.int32, (count, lanes), 1) < head
    allowed = allowed_keys(info_ref, kind, pl.program_id(0), span, count)
    outside = [shifts(info_ref, kind, j) for j in range(blocks)]
    for pair in range(wide_lanes // lanes):
        at = slice(pair * lanes, (pair + 1) * lanes)
        values_t = v_ref[:, :, :, at].reshape(blocks * span, lanes).T
        queries = q_ref[0, 0, :, at] * (head ** -0.5)
        outs = []
        for h in range(2):
            mine = jnp.where(low_lane if h == 0 else ~low_lane, queries, 0).astype(BF)
            scores = [
                lax.dot_general(k_ref[j, 0, :, at], mine, (((1,), (1,)), ((), ())), preferred_element_type=F32)
                for j in range(blocks)
            ]
            scores[0] = jnp.where(allowed, scores[0], masked_score)
            top = jnp.max(scores[0], axis=0, keepdims=True)
            for j in range(1, blocks):
                top = jnp.maximum(top, jnp.max(scores[j], axis=0, keepdims=True) - outside[j])
            soft = [jnp.exp(scores[0] - top)]
            soft += [jnp.exp(scores[j] - (top + outside[j])) for j in range(1, blocks)]
            total = sum(jnp.sum(s, axis=0, keepdims=True) for s in soft)
            lse_ref[0, pair, h : h + 1, :] = top + jnp.log(total)
            low = jnp.concatenate([s.astype(BF) for s in soft], axis=0)
            out = jnp.dot(values_t[h * head : (h + 1) * head], low, preferred_element_type=F32)
            outs.append(out / total)
        o_ref[0, :, at] = jnp.concatenate(outs, axis=0).T.astype(BF)

def attend(kind, info, queries, q_at, keyed, k_at, valued, v_at, group=1, part=(0, 1)):
    blocks, items, span, _ = keyed.shape
    count = queries.shape[2]
    pairs = HEADS // 2 // part[1]
    skip = part[0] * pairs // group
    lanes = 128 * group
    width = pairs * 128
    return pl.pallas_call(
        functools.partial(attend_kernel, kind),
        out_shape=[jax.ShapeDtypeStruct((items, count, width), BF), jax.ShapeDtypeStruct((items, pairs, 2, count), F32)],
        grid_spec=pltpu.PrefetchScalarGridSpec(
            num_scalar_prefetch=1, grid=(items, pairs // group),
            in_specs=[
                pl.BlockSpec((1, 1, count, lanes), lambda i, p, s: (0, i, 0, p + skip + q_at // lanes)),
                pl.BlockSpec((blocks, 1, span, lanes), lambda i, p, s: (0, i, 0, p + skip + k_at // lanes)),
                pl.BlockSpec((blocks, 1, span, lanes), lambda i, p, s: (0, i, 0, p + skip + v_at // lanes)),
            ],
            out_specs=[
                pl.BlockSpec((1, count, lanes), lambda i, p, s: (i, 0, p)),
                pl.BlockSpec((1, group, 2, count), lambda i, p, s: (i, p, 0, 0)),
            ]),
        compiler_params=pltpu.CompilerParams(vmem_limit_bytes=VMEM_LIMIT),
        cost_estimate=SHORT,
        name="attend",
    )(info, queries, keyed, valued)

def attend_back_kernel(kind, info_ref, q_ref, k_ref, v_ref, o_ref, lse_ref, do_ref, dq_ref, dk_ref, dv_ref):
    blocks, _, span, wide_lanes = k_ref.shape
    count = q_ref.shape[2]
    lanes = 128
    head = lanes // 2
    scaling = head ** -0.5
    low_lane = lax.broadcasted_iota(jnp.int32, (count, lanes), 1) < head
    allowed = allowed_keys(info_ref, kind, pl.program_id(0), span, count)
    outside = [shifts(info_ref, kind, j) for j in range(blocks)]
    for pair in range(wide_lanes // lanes):
        at = slice(pair * lanes, (pair + 1) * lanes)
        keys_t = k_ref[:, :, :, at].reshape(blocks * span, lanes).T
        queries = q_ref[0, 0, :, at] * scaling
        grad = do_ref[0, :, at]
        product_t = (grad.astype(F32) * o_ref[0, :, at].astype(F32)).T
        grad_q, dk, dv = [], [0.0] * blocks, [0.0] * blocks
        for h in range(2):
            lane = low_lane if h == 0 else ~low_lane
            mine = jnp.where(lane, queries, 0).astype(BF)
            grad_mine = jnp.where(lane, grad, 0).astype(BF)
            lse = lse_ref[0, pair, h : h + 1, :]
            delta = jnp.sum(product_t[h * head : (h + 1) * head], axis=0, keepdims=True)
            grads = []
            for j in range(blocks):
                scores = lax.dot_general(k_ref[j, 0, :, at], mine, (((1,), (1,)), ((), ())), preferred_element_type=F32)
                if j == 0:
                    soft = jnp.where(allowed, jnp.exp(scores - lse), 0.0)
                else:
                    soft = jnp.exp(scores - (lse + outside[j]))
                grad_soft = lax.dot_general(v_ref[j, 0, :, at], grad_mine, (((1,), (1,)), ((), ())), preferred_element_type=F32)
                grads.append((soft * (grad_soft - delta)).astype(BF))
                dv[j] += jnp.dot(soft.astype(BF), grad_mine, preferred_element_type=F32)
                dk[j] += jnp.dot(grads[j], mine, preferred_element_type=F32)
            grad_scores = jnp.concatenate(grads, axis=0)
            grad_q.append(jnp.dot(keys_t[h * head : (h + 1) * head], grad_scores, preferred_element_type=F32))
        dq_ref[0, :, at] = (jnp.concatenate(grad_q, axis=0) * scaling).T.astype(BF)
        for j in range(blocks):
            dk_ref[j, 0, :, at] = dk[j].astype(BF)
            dv_ref[j, 0, :, at] = dv[j].astype(BF)

def attend_back(kind, info, queries, q_at, keyed, k_at, valued, v_at, attended, lse, grad, group=1, part=(0, 1)):
    blocks, items, span, _ = keyed.shape
    count = queries.shape[2]
    pairs = HEADS // 2 // part[1]
    skip = part[0] * pairs // group
    lanes = 128 * group
    width = pairs * 128
    row = pl.BlockSpec((1, count, lanes), lambda i, p, s: (i, 0, p + skip))
    out = pl.BlockSpec((1, count, lanes), lambda i, p, s: (i, 0, p))
    key = pl.BlockSpec((blocks, 1, span, lanes), lambda i, p, s: (0, i, 0, p))
    return pl.pallas_call(
        functools.partial(attend_back_kernel, kind),
        out_shape=[jax.ShapeDtypeStruct((items, count, width), BF)] + [jax.ShapeDtypeStruct((blocks, items, span, width), BF)]*2,
        grid_spec=pltpu.PrefetchScalarGridSpec(
            num_scalar_prefetch=1, grid=(items, pairs // group),
            in_specs=[
                pl.BlockSpec((1, 1, count, lanes), lambda i, p, s: (0, i, 0, p + skip + q_at // lanes)),
                pl.BlockSpec((blocks, 1, span, lanes), lambda i, p, s: (0, i, 0, p + skip + k_at // lanes)),
                pl.BlockSpec((blocks, 1, span, lanes), lambda i, p, s: (0, i, 0, p + skip + v_at // lanes)),
                row,
                pl.BlockSpec((1, group, 2, count), lambda i, p, s: (i, p + skip, 0, 0)),
                row,
            ],
            out_specs=[out, key, key]),
        compiler_params=pltpu.CompilerParams(vmem_limit_bytes=VMEM_LIMIT),
        cost_estimate=SHORT,
        name="attend_back",
    )(info, queries, keyed, valued, attended, lse, grad)

def flat(tensor):
    return tensor.reshape(-1, tensor.shape[-1])


def dot_t(left, right):
    return lax.dot_general(
        left, right, (((left.ndim - 1,), (1,)), ((), ())), preferred_element_type=F32
    )


def hop_seq(values, step):
    size = lax.axis_size("seq")
    return hop(values, lambda i: i // size * size + (i % size ^ step))


def body(
    tokens,
    captions,
    caption_lengths,
    cotangent,
    self_gain,
    self_shift,
    self_in_weight,
    self_out_weight,
    cross_gain,
    cross_shift,
    cross_query_weight,
    cross_memory_weight,
    cross_out_weight,
    feed_gain,
    feed_shift,
    up_weight,
    up_bias,
    down_weight,
    down_bias,
):
    features = tokens.shape[2]
    k_bias = up_weight.shape[1] // features
    half = 3 * features // 2
    line = Line()
    tokens_y = hop_seq(tokens, 2)
    ga = Gather(line, [self_in_weight[:, :half]])
    ga.far(line)
    small = line(
        lambda *v: pack_small(list(v[:-1]), v[-1]),
        self_gain, self_shift, cross_gain, cross_shift, feed_gain, feed_shift, down_bias, up_bias,
        whole=True,
    )
    ge = Gather(line, [self_in_weight[:, half:], small])
    ga.first(line)
    ge.far(line)
    ga.near(line)
    ge.first(line)
    tokens_y = line(lambda v: v, tokens_y)
    tokens_3 = hop_seq(tokens_y, 1)
    gb = Gather(line, [self_out_weight, cross_query_weight])
    ga.second(line)
    ge.near(line)
    gb.far(line)
    gf = Gather(line, [cross_memory_weight, cross_out_weight])
    gc = Gather(line, [up_weight])
    ga.pair(line)
    ge.second(line)
    gb.first(line)
    gf.far(line)
    tokens_1 = hop_seq(tokens, 1)
    all_tokens = line(lambda a, b, c, d: jnp.stack([d, b, c, a]), tokens_3, tokens_1, tokens_y, tokens)
    gd = Gather(line, [down_weight])
    ge.pair(line)
    gf.first(line)
    gb.near(line)
    gc.far(line)
    seq_place = lax.axis_index("seq").astype(jnp.int32)[None]

    normed1, queries, key_rows, value_rows, small_full, self_in = line(
        lambda t: project(t, ga.pieces() + ge.pieces()), all_tokens
    )
    up_offset = offset_rows(small_full[7 : 7 + k_bias])
    gd.far(line)
    gc.first(line)
    gf.near(line)
    gb.second(line)
    halves = []
    for i in range(2):
        halves.append(
            line(
                lambda q: attend("causal", seq_place, q, 0, key_rows, 0, value_rows, 0, 2, (i, 2)),
                queries,
            )
        )
        if i == 0:
            gd.first(line)
            gc.near(line)
            gf.second(line)
            gb.pair(line)
    flat_tokens, flat_captions = flat(tokens), flat(captions)
    residual1, normed2, cross_queries, self_out, cross_query = line(
        lambda b, a: mix(flat(a), flat(b), flat_tokens, small_full, gb.pieces()),
        halves[1][0],
        halves[0][0],
    )
    cross_queries = cross_queries.reshape(1, *tokens.shape)
    gd.near(line)
    gc.second(line)
    gf.pair(line)
    attended1 = jnp.concatenate([h[0] for h in halves], axis=2)
    lse1 = jnp.concatenate([h[1] for h in halves], axis=1)

    memory, cross_memory, cross_out = line(lambda c: remember(c, gf.pieces()), flat_captions)
    memory = memory.reshape(1, *captions.shape[:2], -1)
    attended2, lse2 = line(
        lambda q: attend("length", caption_lengths, q, 0, memory, 0, memory, features, 8),
        cross_queries,
    )
    gd.second(line)
    gc.pair(line)

    residual2, normed3, activated, slope, up = line(
        lambda a: up_gelu(flat(a), residual1, cross_out, small_full, up_offset, gc.pieces()),
        attended2,
    )
    low3 = flat(cotangent)
    s1 = Scatter(line, [(activated, low3)])
    gd.pair(line)

    final, grad_before, grad_up_bias, grad_down_bias = line(
        lambda g: down_both(g, slope, activated, residual2, small_full, gd.pieces()), low3
    )
    s1.second(line)
    s2 = Scatter(line, [(normed3, grad_before)])
    grad_second, low2, grad_attended2, grad_feed = line(
        lambda g: feed_back(g, up, residual2, low3, small_full, cross_out), grad_before
    )
    s2.second(line)

    grad_attended2 = grad_attended2.reshape(tokens.shape)
    grad_cq, grad_mk, grad_mv = line(
        lambda g: attend_back(
            "length", caption_lengths, cross_queries, 0, memory, 0, memory, features,
            attended2, lse2, g, 8,
        ),
        grad_attended2,
    )
    s1.near(line)
    grad_cq = flat(grad_cq)
    grad_first, low1, grad_attended1, grad_cross = line(
        lambda g: cross_back(g, cross_query, residual1, grad_second, small_full, self_out), grad_cq
    )
    grad_memory = line(
        lambda k, v: jnp.concatenate([flat(k), flat(v)], axis=-1), grad_mk, grad_mv
    )
    caption_sum = line(lambda a: dot_t(a, cross_memory).astype(BF), grad_memory)
    caption_came = hop_seq(caption_sum, 1)
    s3 = Scatter(
        line,
        [
            (normed2, grad_cq),
            (flat_captions, grad_memory),
            (flat(attended2), low2),
            (flat(attended1), low1),
        ],
    )

    grad_attended1 = grad_attended1.reshape(tokens.shape)
    flat_normed1 = flat(normed1)

    def heads_back(i):
        return line(
            lambda g: attend_back(
                "causal", seq_place, queries, 0, key_rows, 0, value_rows, 0, attended1, lse1, g, 2,
                (i, 2),
            ),
            grad_attended1,
        )

    def heads_terms(grads):
        return [
            (flat_normed1[: low1.shape[0]], flat(grads[0])),
            (flat_normed1, flat(grads[1])),
            (flat_normed1, flat(grads[2])),
        ]

    caption_sum = line(lambda c, v: (wide(c) + wide(v)).astype(BF), caption_came, caption_sum)
    caption_came = hop_seq(caption_sum, 2)
    s2.near(line)
    grads_a = heads_back(0)
    s1.first(line)
    s3.second(line)
    s4 = Scatter(line, heads_terms(grads_a))
    s1.far(line)
    grads_b = heads_back(1)
    s4.second(line)
    s5 = Scatter(line, heads_terms(grads_b))
    s2.first(line)
    s3.near(line)
    grad_captions = line(lambda c, v: wide(c) + wide(v), caption_came, caption_sum)
    grad_captions = grad_captions.reshape(captions.shape)
    s5.second(line)
    s4.near(line)
    *grad_blocks, small_grads = line(
        lambda g, *o: self_back(
            (g, *o, *grads_b), all_tokens, self_in, grad_cross, grad_feed, grad_down_bias,
            grad_up_bias,
        ),
        *grads_a,
    )
    items = tokens.shape[0]
    grad_blocks = [grad_blocks[k * items : (k + 1) * items] for k in range(4)]
    small = SmallSum(small_grads)
    grad_threes = [hop_seq(v, 1) for v in grad_blocks[3]]
    grad_ones = [hop_seq(v, 1) for v in grad_blocks[1]]
    s5.near(line)
    s3.first(line)
    grad_twos = [
        hop_seq(line(lambda a, b: (wide(a) + wide(b)).astype(BF), came, own), 2)
        for came, own in zip(grad_threes, grad_blocks[2])
    ]
    s2.far(line)
    small.step(line)
    s4.first(line)
    s3.far(line)
    small.step(line)
    s5.first(line)
    s4.far(line)
    small.step(line)
    s1.close(line)
    s5.far(line)

    def last_norm(came, one, own, token, residual):
        grad = wide(own) + wide(one) + wide(came)
        unit, inverse = unit_of(wide(token))
        return residual + unit_back(unit, inverse, grad * small_full[0])

    grad_first = grad_first.reshape(tokens.shape)
    grad_tokens = jnp.stack(
        [
            line(last_norm, grad_twos[i], grad_ones[i], grad_blocks[0][i], tokens[i], grad_first[i])
            for i in range(items)
        ]
    )
    small.step(line)
    s2.close(line)
    s3.close(line)
    s4.close(line)
    s5.close(line)
    small_out, grad_bias = small.parts(line, 7)
    (grad_down,) = s1.result(line)
    (grad_up,) = s2.result(line)
    results3 = s3.result(line)
    grad_cross_query, grad_cross_memory, grad_cross_out, grad_self_out = results3
    grads_4 = s4.result(line)
    grads_5 = s5.result(line)
    return (
        final.reshape(tokens.shape),
        grad_tokens,
        grad_captions,
        small_out[0],
        small_out[1],
        jnp.concatenate([g for pair in zip(grads_4, grads_5) for g in pair], axis=1),
        grad_self_out,
        small_out[2],
        small_out[3],
        grad_cross_query,
        grad_cross_memory,
        grad_cross_out,
        small_out[4],
        small_out[5],
        grad_up,
        grad_bias,
        grad_down,
        small_out[6],
    )


def solution(mesh):
    tokens_spec = P("dp", "seq", None)
    rows1, rows2 = P(AXES), P(AXES, None)
    return jax.shard_map(
        body,
        mesh=mesh,
        in_specs=(
            tokens_spec, P("dp", None, None), P("dp"), tokens_spec,
            rows1, rows1, rows2, rows2, rows1, rows1, rows2, rows2, rows2,
            rows1, rows1, rows2, rows1, rows2, rows1,
        ),
        out_specs=(
            tokens_spec, tokens_spec, P("dp", None, None),
            rows1, rows1, rows2, rows2, rows1, rows1, rows2, rows2, rows2,
            rows1, rows1, rows2, rows1, rows2, rows1,
        ),
        check_vma=False,
    )
```

```python
import functools
import itertools

import jax
import jax.numpy as jnp
from jax import lax
from jax.experimental import pallas as pl
from jax.experimental.pallas import tpu as pltpu
from jax.sharding import PartitionSpec as P

HEADS = 16
AXES = ("dp", "seq")
BF = jnp.bfloat16
F32 = jnp.float32
epsilon = 1e-05
masked_score = -1e30
VMEM_LIMIT = 34 * 1024 * 1024


def device_count():
    return lax.axis_size("dp") * lax.axis_size("seq")


def place():
    index = lax.axis_index("dp") * lax.axis_size("seq") + lax.axis_index("seq")
    return index


def spots(core):
    index = place()
    c = index % 2
    half = c if core == "own" else 1 - c
    return jnp.stack(
        [half, (index // 4) % 2, (index // 2) % 2, (index // 8) % 2, index // 16]
    ).astype(jnp.int32)


def hop(values, change):
    count = device_count()
    pairs = [(i, change(i)) for i in range(count)]
    return lax.ppermute(values, AXES, pairs)


def hop_core(values):
    return hop(values, lambda i: i ^ 1)


def hop_first(values):
    return hop(values, lambda i: i ^ 4 if i % 2 == 0 else i ^ 2)


def hop_second(values):
    return hop(values, lambda i: i ^ 2 if i % 2 == 0 else i ^ 4)


def hop_z0(values):
    return hop(values, lambda i: i ^ 8)


def hop_z1(values, step):
    return hop(values, lambda i: i ^ (16 * step))


def far_count():
    return device_count() // 16


def column_half(values, half):
    width = values.shape[-1] // 2
    return lax.dynamic_slice_in_dim(values, half * width, width, values.ndim - 1)


def after(value, *others):
    return lax.optimization_barrier((value, *others))[0]


class Line:
    def __init__(self):
        self.last = ()

    def __call__(self, function, first, *rest, whole=False):
        if self.last and whole:
            first, *rest = lax.optimization_barrier((first, *rest, *self.last))[: 1 + len(rest)]
        elif self.last:
            first = after(first, *self.last)
        result = function(first, *rest)
        self.last = jax.tree.leaves(result)[:1]
        return result


class Gather:
    def __init__(self, line, shards):
        c = place() % 2

        def split(*parts):
            return [
                jnp.concatenate([column_half(p, half) for p in parts], axis=1)
                for half in (1 - c, c)
            ]

        other, self.mine = line(split, *shards, whole=True)
        self.came = hop_core(other)

    def far(self, line):
        c = place() % 2
        self.sent = line(
            lambda came, mine: jnp.where(
                c == 0, jnp.concatenate([mine, came]), jnp.concatenate([came, mine])
            ),
            self.came,
            self.mine,
        )
        self.came = [hop_z1(self.sent, k) for k in range(1, far_count())]

    def first(self, line):
        self.sent = line(lambda c, s, *o: jnp.stack([s, *o, c]), self.came[-1], self.sent, *self.came[:-1])
        self.came = hop_first(self.sent)

    def near(self, line):
        self.sent = line(lambda c, s: jnp.stack([s, c]), self.came, self.sent)
        self.came = hop_z0(self.sent)

    def second(self, line):
        self.sent = line(lambda c, s: jnp.stack([s, c]), self.came, self.sent)
        self.came = hop_second(self.sent)
        self.sent_other = hop_core(self.sent)

    def pair(self, line):
        self.came = line(lambda v: v, self.came)
        self.came_other = hop_core(self.came)

    def pieces(self):
        return self.came_other, self.sent, self.came, self.sent_other


def fetch(spot_ref, pieces, targets, sems):
    far_other, near_own, far_own, near_other = pieces
    far, rows = near_own.shape[2], near_own.shape[3]
    c, mx, my, mz0, mz1 = (spot_ref[i] for i in range(5))
    started, start = [], 0
    for k, (target, first, both) in enumerate(targets):
        width = both // 2
        copies = []
        for half, sides in ((c, (near_own, far_own)), (1 - c, (near_other, far_other))):
            column = pl.multiple_of(first + half * width, 128)
            for d4, dz0, d2, dz1 in itertools.product(range(2), range(2), range(2), range(far)):
                x = jnp.where(half == 0, d2, d4) ^ mx
                y = jnp.where(half == 0, d4, d2) ^ my
                z = (dz1 ^ mz1) * 2 + (dz0 ^ mz0)
                row = pl.multiple_of(((z * 2 + x) * 2 + y) * rows, rows)
                copies.append(
                    pltpu.make_async_copy(
                        sides[d4].at[dz0, d2, dz1, :, pl.ds(start, width)],
                        target.at[pl.ds(row, rows), pl.ds(column, width)],
                        sems.at[k],
                    )
                )
        for copy in copies:
            copy.start()
        started.append(copies)
        start += width
    return started


def finish(copies):
    for copy in copies:
        copy.wait()


SHORT = pl.CostEstimate(flops=1, bytes_accessed=1, transcendentals=0)
ANY = pl.BlockSpec(memory_space=pl.ANY)
SMEM = pl.BlockSpec(memory_space=pltpu.SMEM)
VMEM = pl.BlockSpec(memory_space=pltpu.VMEM)


def call(kernel, name, outs, in_specs, out_specs, scratch, grid=()):
    return pl.pallas_call(
        kernel,
        out_shape=outs,
        grid=grid,
        in_specs=in_specs,
        out_specs=out_specs,
        scratch_shapes=scratch,
        compiler_params=pltpu.CompilerParams(vmem_limit_bytes=VMEM_LIMIT),
        cost_estimate=SHORT,
        name=name,
    )


def shaped(shape, dtype):
    return jax.ShapeDtypeStruct(tuple(shape), dtype)


def kdot(left, right):
    return jnp.dot(left, right, preferred_element_type=F32)


def kdot_t(left, right):
    return lax.dot_general(left, right, (((1,), (1,)), ((), ())), preferred_element_type=F32)


def unit_of(values):
    centered = values - jnp.mean(values, axis=-1, keepdims=True)
    inverse = lax.rsqrt(jnp.mean(centered * centered, axis=-1, keepdims=True) + epsilon)
    return centered * inverse, inverse


def unit_back(unit, inverse, grad_unit):
    return inverse * (
        grad_unit
        - jnp.mean(grad_unit, axis=-1, keepdims=True)
        - unit * jnp.mean(grad_unit * unit, axis=-1, keepdims=True)
    )


def project_kernel(
    spot_ref, token_ref, p0, p1, p2, p3, p4, p5, p6, p7,
    a_ref, q_ref, k_ref, v_ref, small_ref, w_ref, w, packed, vectors, sems, out_sem,
):
    _, items, count, d = token_ref.shape
    kept = pltpu.make_async_copy(w, w_ref, out_sem)

    @pl.when(pl.program_id(0) == 0)
    def _():
        half = 3 * d // 2
        one = fetch(spot_ref, (p0, p1, p2, p3), [(w, 0, half)], sems.at[pl.ds(0, 1)])
        two = fetch(
            spot_ref, (p4, p5, p6, p7), [(w, half, half), (packed, 0, 256)], sems.at[pl.ds(1, 2)]
        )
        finish(two[1])
        vectors[...] = packed[...].astype(F32).T
        small_ref[...] = vectors[0:16, :]
        finish(one[0])
        finish(two[0])
        kept.start()

    unit, _ = unit_of(token_ref[...].reshape(items * count, d).astype(F32))
    normed = (unit * vectors[0:1, :] + vectors[1:2, :]).astype(BF)
    a_ref[...] = normed.reshape(a_ref.shape)
    k_ref[...] = kdot(normed, w[:, d : 2 * d]).astype(BF).reshape(k_ref.shape)
    v_ref[...] = kdot(normed, w[:, 2 * d :]).astype(BF).reshape(v_ref.shape)

    @pl.when(pl.program_id(0) == 0)
    def _():
        q_ref[...] = kdot(normed, w[:, :d]).astype(BF).reshape(q_ref.shape)

    @pl.when(pl.program_id(0) == pl.num_programs(0) - 1)
    def _():
        kept.wait()


def project(tokens, pieces):
    blocks, items, count, d = tokens.shape
    block = pl.BlockSpec((1, items, count, d), lambda b: (b, 0, 0, 0))
    own = pl.BlockSpec((1, items, count, d), lambda b: (0, 0, 0, 0))
    big = shaped(tokens.shape, BF)
    return call(
        project_kernel,
        "project",
        [big, shaped((1, items, count, d), BF), big, big, shaped((16, d), F32), shaped((d, 3 * d), BF)],
        [SMEM, block] + [ANY] * 8,
        [block, own, block, block, pl.BlockSpec((16, d), lambda b: (0, 0)), ANY],
        [
            pltpu.VMEM((d, 3 * d), BF),
            pltpu.VMEM((d, 256), BF),
            pltpu.VMEM((256, d), F32),
            pltpu.SemaphoreType.DMA((3,)),
            pltpu.SemaphoreType.DMA,
        ],
        grid=(blocks,),
    )(spots("own"), tokens, *pieces)


def mix_kernel(
    spot_ref, att0_ref, att1_ref, token_ref, small_ref, p0, p1, p2, p3,
    r_ref, a_ref, cq_ref, wso_ref, wcq_ref, wso, wcq, sems, out_sems,
):
    weights = (wso, wcq)
    groups = fetch(spot_ref, (p0, p1, p2, p3), [(w, 0, w.shape[1]) for w in weights], sems)
    kept = [
        pltpu.make_async_copy(w, out, out_sems.at[i])
        for i, (w, out) in enumerate(zip(weights, (wso_ref, wcq_ref)))
    ]
    finish(groups[0])
    kept[0].start()
    half = att0_ref.shape[1]
    residual = token_ref[...].astype(F32) + (
        kdot(att0_ref[...], wso[:half]) + kdot(att1_ref[...], wso[half:])
    )
    r_ref[...] = residual
    unit, _ = unit_of(residual)
    normed = (unit * small_ref[2:3, :] + small_ref[3:4, :]).astype(BF)
    a_ref[...] = normed
    finish(groups[1])
    kept[1].start()
    cq_ref[...] = kdot(normed, wcq[...]).astype(BF)
    finish(kept)


def mix(attended0, attended1, tokens, small, pieces):
    rows, d = tokens.shape
    return call(
        mix_kernel,
        "mix",
        [shaped((rows, d), F32), shaped((rows, d), BF), shaped((rows, d), BF)]
        + [shaped((d, d), BF)] * 2,
        [SMEM, VMEM, VMEM, VMEM, VMEM] + [ANY] * 4,
        [VMEM] * 3 + [ANY] * 2,
        [pltpu.VMEM((d, d), BF)] * 2
        + [pltpu.SemaphoreType.DMA((2,)), pltpu.SemaphoreType.DMA((2,))],
    )(spots("own"), attended0, attended1, tokens, small, *pieces)


def memory_kernel(
    spot_ref, caption_ref, p0, p1, p2, p3, memory_ref, wcm_ref, wco_ref, wcm, wco, sems, out_sems
):
    weights = (wcm, wco)
    groups = fetch(spot_ref, (p0, p1, p2, p3), [(w, 0, w.shape[1]) for w in weights], sems)
    kept = [
        pltpu.make_async_copy(w, out, out_sems.at[i])
        for i, (w, out) in enumerate(zip(weights, (wcm_ref, wco_ref)))
    ]
    finish(groups[0])
    kept[0].start()
    memory_ref[...] = kdot(caption_ref[...], wcm[...]).astype(BF)
    finish(groups[1])
    kept[1].start()
    finish(kept)


def remember(captions, pieces):
    rows, d = captions.shape
    weights = [(d, 2 * d), (d, d)]
    return call(
        memory_kernel,
        "memory",
        [shaped((rows, 2 * d), BF)] + [shaped(w, BF) for w in weights],
        [SMEM, VMEM] + [ANY] * 4,
        [VMEM] + [ANY] * 2,
        [pltpu.VMEM(w, BF) for w in weights]
        + [pltpu.SemaphoreType.DMA((2,)), pltpu.SemaphoreType.DMA((2,))],
    )(spots("own"), captions, *pieces)


def up_kernel(
    spot_ref, att_ref, r1_ref, wco_ref, small_ref, bias_ref, p0, p1, p2, p3,
    r2_ref, a_ref, act_ref, slope_ref, w_ref, w, sems, out_sem,
):
    n = pl.program_id(0)
    width = act_ref.shape[1]
    kept = pltpu.make_async_copy(w, w_ref, out_sem)

    @pl.when(n == 0)
    def _():
        (copies,) = fetch(spot_ref, (p0, p1, p2, p3), [(w, 0, w.shape[1])], sems)
        residual = r1_ref[...] + kdot(att_ref[...], wco_ref[...])
        r2_ref[...] = residual
        unit, _ = unit_of(residual)
        a_ref[...] = (unit * small_ref[4:5, :] + small_ref[5:6, :]).astype(BF)
        finish(copies)
        kept.start()

    part = w[:, pl.ds(pl.multiple_of(n * width, width), width)]
    before = kdot(a_ref[...], part) + bias_ref[...]
    phi = 0.5 + 0.5 * lax.erf(before * (0.5 ** 0.5))
    act_ref[...] = (before * phi).astype(BF)
    slope_ref[...] = (phi + before * (jnp.exp(-0.5 * before * before) * 0.3989422804014327)).astype(BF)

    @pl.when(n == pl.num_programs(0) - 1)
    def _():
        kept.wait()


def up_gelu(attended, residual, cross_out, small, bias, pieces, block=512):
    rows, d = residual.shape
    hidden = bias.shape[1]
    whole = pl.BlockSpec((rows, d), lambda n: (0, 0))
    column = pl.BlockSpec((rows, block), lambda n: (0, n))
    return call(
        up_kernel,
        "up_gelu",
        [shaped((rows, d), F32), shaped((rows, d), BF)]
        + [shaped((rows, hidden), BF)] * 2
        + [shaped((d, hidden), BF)],
        [
            SMEM, whole, whole, pl.BlockSpec((d, d), lambda n: (0, 0)),
            pl.BlockSpec((16, d), lambda n: (0, 0)), pl.BlockSpec((1, block), lambda n: (0, n)),
            ANY, ANY, ANY, ANY,
        ],
        [whole, whole, column, column, ANY],
        [pltpu.VMEM((d, hidden), BF), pltpu.SemaphoreType.DMA((1,)), pltpu.SemaphoreType.DMA],
        grid=(hidden // block,),
    )(spots("own"), attended, residual, cross_out, small, bias, *pieces)


def down_kernel(
    spot_ref, g_ref, slope_ref, act_ref, r2_ref, small_ref, p0, p1, p2, p3,
    out_ref, grad_ref, bias_ref, down_bias_ref, w, total, sems,
):
    n = pl.program_id(0)
    height = act_ref.shape[1]

    @pl.when(n == 0)
    def _():
        (copies,) = fetch(spot_ref, (p0, p1, p2, p3), [(w, 0, w.shape[1])], sems)
        total[...] = r2_ref[...] + small_ref[6:7, :]
        down_bias_ref[...] = jnp.sum(g_ref[...].astype(F32), axis=0, keepdims=True)
        finish(copies)

    part = w[pl.ds(pl.multiple_of(n * height, height), height), :]
    grad = (kdot_t(g_ref[...], part) * slope_ref[...].astype(F32)).astype(BF)
    grad_ref[...] = grad
    bias_ref[...] = jnp.sum(grad.astype(F32), axis=0, keepdims=True)
    total[...] += kdot(act_ref[...], part)

    @pl.when(n == pl.num_programs(0) - 1)
    def _():
        out_ref[...] = total[...].astype(BF)


def down_both(grad, slope, activated, residual, small, pieces, block=512):
    rows, d = residual.shape
    hidden = slope.shape[1]
    whole = pl.BlockSpec((rows, d), lambda n: (0, 0))
    column = pl.BlockSpec((rows, block), lambda n: (0, n))
    return call(
        down_kernel,
        "down",
        [shaped((rows, d), BF), shaped((rows, hidden), BF), shaped((1, hidden), F32), shaped((1, d), F32)],
        [SMEM, whole, column, column, whole, pl.BlockSpec((16, d), lambda n: (0, 0)), ANY, ANY, ANY, ANY],
        [whole, column, pl.BlockSpec((1, block), lambda n: (0, n)), pl.BlockSpec((1, d), lambda n: (0, 0))],
        [pltpu.VMEM((hidden, d), BF), pltpu.VMEM((rows, d), F32), pltpu.SemaphoreType.DMA((1,))],
        grid=(hidden // block,),
    )(spots("own"), grad, slope, activated, residual, small, *pieces)


def feed_back_kernel(
    g_ref, w_ref, r2_ref, cot_ref, small_ref, wco_ref, dr_ref, low_ref, datt_ref, vec_ref, total
):
    n = pl.program_id(0)

    @pl.when(n == 0)
    def _():
        total[...] = jnp.zeros_like(total)

    total[...] += kdot_t(g_ref[...], w_ref[...])

    @pl.when(n == pl.num_programs(0) - 1)
    def _():
        grad = total[...]
        unit, inverse = unit_of(r2_ref[...])
        vec_ref[0:1, :] = jnp.sum(grad * unit, axis=0, keepdims=True)
        vec_ref[1:2, :] = jnp.sum(grad, axis=0, keepdims=True)
        out = cot_ref[...].astype(F32) + unit_back(unit, inverse, grad * small_ref[4:5, :])
        dr_ref[...] = out
        low = out.astype(BF)
        low_ref[...] = low
        datt_ref[...] = kdot_t(low, wco_ref[...]).astype(BF)


def feed_back(grad, up, residual, cotangent, small, cross_out, block=1024):
    rows, d = residual.shape
    hidden = grad.shape[1]
    whole = pl.BlockSpec((rows, d), lambda n: (0, 0))
    return call(
        feed_back_kernel,
        "feed_back",
        [shaped((rows, d), F32), shaped((rows, d), BF), shaped((rows, d), BF), shaped((8, d), F32)],
        [
            pl.BlockSpec((rows, block), lambda n: (0, n)), pl.BlockSpec((d, block), lambda n: (0, n)),
            whole, whole, pl.BlockSpec((16, d), lambda n: (0, 0)), pl.BlockSpec((d, d), lambda n: (0, 0)),
        ],
        [whole, whole, whole, pl.BlockSpec((8, d), lambda n: (0, 0))],
        [pltpu.VMEM((rows, d), F32)],
        grid=(hidden // block,),
    )(grad, up, residual, cotangent, small, cross_out)


def cross_back_kernel(
    g_ref, wcq_ref, r1_ref, dr2_ref, small_ref, wso_ref, dr_ref, low_ref, datt_ref, vec_ref
):
    grad = kdot_t(g_ref[...], wcq_ref[...])
    unit, inverse = unit_of(r1_ref[...])
    vec_ref[0:1, :] = jnp.sum(grad * unit, axis=0, keepdims=True)
    vec_ref[1:2, :] = jnp.sum(grad, axis=0, keepdims=True)
    out = dr2_ref[...] + unit_back(unit, inverse, grad * small_ref[2:3, :])
    dr_ref[...] = out
    low = out.astype(BF)
    low_ref[...] = low
    datt_ref[...] = kdot_t(low, wso_ref[...]).astype(BF)


def cross_back(grad, cross_query, residual, grad_residual, small, self_out):
    rows, d = residual.shape
    return call(
        cross_back_kernel,
        "cross_back",
        [shaped((rows, d), F32), shaped((rows, d), BF), shaped((rows, d), BF), shaped((8, d), F32)],
        [VMEM] * 6,
        [VMEM] * 4,
        [],
    )(grad, cross_query, residual, grad_residual, small, self_out)


def self_back_kernel(
    dq0_ref, dk0_ref, dv0_ref, dq1_ref, dk1_ref, dv1_ref, token_ref, w_ref,
    cross_ref, feed_ref, down_ref, up_ref, *refs,
):
    *da_refs, vec_ref, own = refs
    b = pl.program_id(0)
    _, items, count, d = token_ref.shape
    half = d // 2

    def back(ref, at):
        return kdot_t(ref[...].reshape(items * count, half), w_ref[:, at : at + half])

    own[...] = (back(dk0_ref, d) + back(dk1_ref, d + half)) + (
        back(dv0_ref, 2 * d) + back(dv1_ref, 2 * d + half)
    )

    @pl.when(b == 0)
    def _():
        own[...] += back(dq0_ref, 0) + back(dq1_ref, half)
        vec_ref[0:2, :] = jnp.zeros((2, d), F32)
        vec_ref[2:4, :] = cross_ref[0:2, :]
        vec_ref[4:6, :] = feed_ref[0:2, :]
        vec_ref[6:7, :] = down_ref[...]
        for k in range(up_ref.shape[1] // d):
            vec_ref[7 + k : 8 + k, :] = up_ref[:, k * d : (k + 1) * d]

    grad = own[...]
    for k in range(len(da_refs) // items):

        @pl.when(b == k)
        def _():
            for i in range(items):
                da_refs[k * items + i][...] = grad[i * count : (i + 1) * count].astype(BF)

    unit, _ = unit_of(token_ref[...].reshape(items * count, d).astype(F32))
    vec_ref[0:1, :] += jnp.sum(grad * unit, axis=0, keepdims=True)
    vec_ref[1:2, :] += jnp.sum(grad, axis=0, keepdims=True)


def self_back(grads, tokens, weight, cross, feed, down, up):
    blocks, items, count, d = tokens.shape
    block = pl.BlockSpec((1, items, count, d), lambda b: (b, 0, 0, 0))
    part = pl.BlockSpec((1, items, count, d // 2), lambda b: (b, 0, 0, 0))

    height = 7 + up.shape[1] // d

    def whole(array):
        return pl.BlockSpec(array.shape, lambda b: (0,) * array.ndim)

    return call(
        self_back_kernel,
        "self_back",
        [shaped((count, d), BF)] * (blocks * items) + [shaped((height, d), F32)],
        [whole(grads[0]), part, part, whole(grads[3]), part, part, block]
        + [whole(a) for a in (weight, cross, feed, down, up)],
        [pl.BlockSpec((count, d), lambda b: (0, 0))] * (blocks * items)
        + [pl.BlockSpec((height, d), lambda b: (0, 0))],
        [pltpu.VMEM((items * count, d), F32)],
        grid=(blocks,),
    )(*grads, tokens, weight, cross, feed, down, up)


def wgrad_kernel(kinds, rows, side, spot_ref, *refs):
    half, mx, my, mz0 = (spot_ref[i] for i in range(4))
    scratch = refs[-1]
    outs = refs[-5:-1] if side == "other" else refs[-3:-1]
    at, start = 0, 0
    for kind in kinds:
        if kind == "dot":
            left, right = refs[at], refs[at + 1]
            at += 2
            block = lax.dot_general(
                left[...], right[...], (((0,), (0,)), ((), ())), preferred_element_type=F32
            )
        else:
            block = refs[at][...].astype(F32)
            at += 1
        scratch[:, start : start + block.shape[1]] = block
        start += block.shape[1]
    for d4, dz0, d2 in itertools.product(range(2), range(2), range(2)):
        x = jnp.where(half == 0, d2, d4) ^ mx
        y = jnp.where(half == 0, d4, d2) ^ my
        j = ((dz0 ^ mz0) * 2 + x) * 2 + y
        part = scratch[pl.ds(pl.multiple_of(j * rows, rows), rows), :]
        if side == "other":
            outs[d4 * 2 + dz0][d2, 0] = part.astype(BF)
        else:
            came = refs[at + d4 * 2 + dz0]
            outs[d4][dz0, d2, 0] = (part + came[d2, 0].astype(F32)).astype(BF)


def wgrad(terms, side, came=None):
    far = far_count()
    kinds = tuple("dot" if len(t) == 2 else "raw" for t in terms)
    height = terms[0][0].shape[1] if kinds[0] == "dot" else terms[0][0].shape[0]
    rows = height // (8 * far)
    specs, args, total = [], [], 0
    for term in terms:
        right = term[-1]
        width = right.shape[1] // 2
        if len(term) == 2:
            left = term[0]
            specs.append(pl.BlockSpec((left.shape[0], 8 * rows), lambda z, s: (0, z)))
            specs.append(pl.BlockSpec((right.shape[0], width), lambda z, s: (0, s[0])))
        else:
            specs.append(pl.BlockSpec((8 * rows, width), lambda z, s: (z, s[0])))
        args += list(term)
        total += width
    piece = pl.BlockSpec((2, 1, rows, total), lambda z, s: (0, z ^ s[4], 0, 0))
    part = pl.BlockSpec((2, 2, 1, rows, total), lambda z, s: (0, 0, z ^ s[4], 0, 0))
    if side == "other":
        out_shape, out_specs = [shaped((2, far, rows, total), BF)] * 4, [piece] * 4
    else:
        specs += [piece] * 4
        args += came
        out_shape, out_specs = [shaped((2, 2, far, rows, total), BF)] * 2, [part] * 2
    return pl.pallas_call(
        functools.partial(wgrad_kernel, kinds, rows, side),
        out_shape=out_shape,
        grid_spec=pltpu.PrefetchScalarGridSpec(
            num_scalar_prefetch=1,
            grid=(far,),
            in_specs=specs,
            out_specs=out_specs,
            scratch_shapes=[pltpu.VMEM((8 * rows, total), F32)],
        ),
        compiler_params=pltpu.CompilerParams(vmem_limit_bytes=VMEM_LIMIT),
        cost_estimate=SHORT,
        name="wgrad",
    )(spots(side), *args)


def wide(values):
    return values.astype(F32)


class Scatter:
    def __init__(self, line, terms):
        self.widths = [t[-1].shape[1] // 2 for t in terms]

        self.terms = terms
        sent = line(lambda f: wgrad([(f, *terms[0][1:]), *terms[1:]], "other"), terms[0][0])
        self.came0 = [hop_core(v) for v in sent]

    def second(self, line):
        self.own, sent = line(lambda *c: wgrad(self.terms, "own", c), *self.came0)
        self.came1 = hop_second(sent)

    def near(self, line):
        def add(c1, o):
            return (wide(o[1]) + wide(c1[1])).astype(BF)

        self.came2 = hop_z0(line(add, self.came1, self.own))

    def first(self, line):
        def add(c2, c1, o):
            return (wide(o[0, 1]) + wide(c1[0, 1]) + wide(c2[1])).astype(BF)

        self.came3 = hop_first(line(add, self.came2, self.came1, self.own))

    def far(self, line):
        def add(c3, c2, c1, o):
            kept = wide(o[0, 0]) + wide(c1[0, 0]) + wide(c2[0]) + wide(c3)
            return kept.astype(BF), kept[0]

        low, self.kept = line(add, self.came3, self.came2, self.came1, self.own)
        self.came4 = [hop_z1(low[k], k) for k in range(1, far_count())]

    def close(self, line):
        total = line(lambda c, t, *o: sum(map(wide, o), t + wide(c)), self.came4[-1], self.kept, *self.came4[:-1])
        rows = total.shape[0] // 2
        c = place() % 2
        self.mine = lax.dynamic_slice_in_dim(total, c * rows, rows, 0)
        self.theirs = hop_core(lax.dynamic_slice_in_dim(total, (1 - c) * rows, rows, 0))

    def result(self, line):
        c = place() % 2

        def join(came, mine):
            left = jnp.where(c == 0, mine, came)
            right = jnp.where(c == 0, came, mine)
            results, start = [], 0
            for width in self.widths:
                at = slice(start, start + width)
                results.append(jnp.concatenate([left[:, at], right[:, at]], axis=1))
                start += width
            return results

        return line(join, self.theirs, self.mine)


def pack_small(vectors, bias):
    r = vectors[0].shape[0]
    k = bias.shape[0] // r
    rows = jnp.concatenate([jnp.stack(vectors), bias.reshape(k, r)])
    return jnp.pad(rows.T, ((0, 0), (0, 256 - rows.shape[0])))


def offset_rows(rows):
    k, d = rows.shape
    n = device_count()
    return rows.reshape(k, n, d // n).transpose(1, 0, 2).reshape(1, k * d)


class SmallSum:
    def __init__(self, values):
        self.values = values
        far = 16
        self.distances = [1, 4]
        while far < device_count():
            self.distances.append(far)
            far *= 2
        self.distances += [8, 2]
        self.send()

    def send(self):
        distance = self.distances.pop(0)
        self.came = hop(self.values, lambda i: i ^ distance)

    def step(self, line):
        self.values = line(lambda c, v: c + v, self.came, self.values)
        if self.distances:
            self.send()
            return True
        return False

    def parts(self, line, count):
        while self.step(line):
            pass
        rows = self.values
        n = device_count()
        part = rows.shape[1] // n
        own = lax.dynamic_slice_in_dim(rows[:count], place() * part, part, 1)
        long = rows[count:].reshape(-1)
        share = long.shape[0] // n
        return own, lax.dynamic_slice_in_dim(long, place() * share, share)


def shifts(info_ref, kind, block):
    if kind == "length" or block == 0:
        return None
    me = info_ref[0]
    return jnp.where((me ^ block) < me, 0.0, -masked_score).astype(F32)

def allowed_keys(info_ref, kind, item, span, count):
    shape = (span, count)
    row = lax.broadcasted_iota(jnp.int32, shape, 0)
    if kind == "length":
        return row < info_ref[item]
    return row <= lax.broadcasted_iota(jnp.int32, shape, 1)

def attend_kernel(kind, info_ref, q_ref, k_ref, v_ref, o_ref, lse_ref):
    blocks, _, span, wide_lanes = k_ref.shape
    count = q_ref.shape[2]
    lanes = 128
    head = lanes // 2
    low_lane = lax.broadcasted_iota(jnp.int32, (count, lanes), 1) < head
    allowed = allowed_keys(info_ref, kind, pl.program_id(0), span, count)
    outside = [shifts(info_ref, kind, j) for j in range(blocks)]
    for pair in range(wide_lanes // lanes):
        at = slice(pair * lanes, (pair + 1) * lanes)
        values_t = v_ref[:, :, :, at].reshape(blocks * span, lanes).T
        queries = q_ref[0, 0, :, at] * (head ** -0.5)
        outs = []
        for h in range(2):
            mine = jnp.where(low_lane if h == 0 else ~low_lane, queries, 0).astype(BF)
            scores = [
                lax.dot_general(k_ref[j, 0, :, at], mine, (((1,), (1,)), ((), ())), preferred_element_type=F32)
                for j in range(blocks)
            ]
            scores[0] = jnp.where(allowed, scores[0], masked_score)
            top = jnp.max(scores[0], axis=0, keepdims=True)
            for j in range(1, blocks):
                top = jnp.maximum(top, jnp.max(scores[j], axis=0, keepdims=True) - outside[j])
            soft = [jnp.exp(scores[0] - top)]
            soft += [jnp.exp(scores[j] - (top + outside[j])) for j in range(1, blocks)]
            total = sum(jnp.sum(s, axis=0, keepdims=True) for s in soft)
            lse_ref[0, pair, h : h + 1, :] = top + jnp.log(total)
            low = jnp.concatenate([s.astype(BF) for s in soft], axis=0)
            out = jnp.dot(values_t[h * head : (h + 1) * head], low, preferred_element_type=F32)
            outs.append(out / total)
        o_ref[0, :, at] = jnp.concatenate(outs, axis=0).T.astype(BF)

def attend(kind, info, queries, q_at, keyed, k_at, valued, v_at, group=1, part=(0, 1)):
    blocks, items, span, _ = keyed.shape
    count = queries.shape[2]
    pairs = HEADS // 2 // part[1]
    skip = part[0] * pairs // group
    lanes = 128 * group
    width = pairs * 128
    return pl.pallas_call(
        functools.partial(attend_kernel, kind),
        out_shape=[jax.ShapeDtypeStruct((items, count, width), BF), jax.ShapeDtypeStruct((items, pairs, 2, count), F32)],
        grid_spec=pltpu.PrefetchScalarGridSpec(
            num_scalar_prefetch=1, grid=(items, pairs // group),
            in_specs=[
                pl.BlockSpec((1, 1, count, lanes), lambda i, p, s: (0, i, 0, p + skip + q_at // lanes)),
                pl.BlockSpec((blocks, 1, span, lanes), lambda i, p, s: (0, i, 0, p + skip + k_at // lanes)),
                pl.BlockSpec((blocks, 1, span, lanes), lambda i, p, s: (0, i, 0, p + skip + v_at // lanes)),
            ],
            out_specs=[
                pl.BlockSpec((1, count, lanes), lambda i, p, s: (i, 0, p)),
                pl.BlockSpec((1, group, 2, count), lambda i, p, s: (i, p, 0, 0)),
            ]),
        compiler_params=pltpu.CompilerParams(vmem_limit_bytes=VMEM_LIMIT),
        cost_estimate=SHORT,
        name="attend",
    )(info, queries, keyed, valued)

def attend_back_kernel(kind, info_ref, q_ref, k_ref, v_ref, o_ref, lse_ref, do_ref, dq_ref, dk_ref, dv_ref):
    blocks, _, span, wide_lanes = k_ref.shape
    count = q_ref.shape[2]
    lanes = 128
    head = lanes // 2
    scaling = head ** -0.5
    low_lane = lax.broadcasted_iota(jnp.int32, (count, lanes), 1) < head
    allowed = allowed_keys(info_ref, kind, pl.program_id(0), span, count)
    outside = [shifts(info_ref, kind, j) for j in range(blocks)]
    for pair in range(wide_lanes // lanes):
        at = slice(pair * lanes, (pair + 1) * lanes)
        keys_t = k_ref[:, :, :, at].reshape(blocks * span, lanes).T
        queries = q_ref[0, 0, :, at] * scaling
        grad = do_ref[0, :, at]
        product_t = (grad.astype(F32) * o_ref[0, :, at].astype(F32)).T
        grad_q, dk, dv = [], [0.0] * blocks, [0.0] * blocks
        for h in range(2):
            lane = low_lane if h == 0 else ~low_lane
            mine = jnp.where(lane, queries, 0).astype(BF)
            grad_mine = jnp.where(lane, grad, 0).astype(BF)
            lse = lse_ref[0, pair, h : h + 1, :]
            delta = jnp.sum(product_t[h * head : (h + 1) * head], axis=0, keepdims=True)
            grads = []
            for j in range(blocks):
                scores = lax.dot_general(k_ref[j, 0, :, at], mine, (((1,), (1,)), ((), ())), preferred_element_type=F32)
                if j == 0:
                    soft = jnp.where(allowed, jnp.exp(scores - lse), 0.0)
                else:
                    soft = jnp.exp(scores - (lse + outside[j]))
                grad_soft = lax.dot_general(v_ref[j, 0, :, at], grad_mine, (((1,), (1,)), ((), ())), preferred_element_type=F32)
                grads.append((soft * (grad_soft - delta)).astype(BF))
                dv[j] += jnp.dot(soft.astype(BF), grad_mine, preferred_element_type=F32)
                dk[j] += jnp.dot(grads[j], mine, preferred_element_type=F32)
            grad_scores = jnp.concatenate(grads, axis=0)
            grad_q.append(jnp.dot(keys_t[h * head : (h + 1) * head], grad_scores, preferred_element_type=F32))
        dq_ref[0, :, at] = (jnp.concatenate(grad_q, axis=0) * scaling).T.astype(BF)
        for j in range(blocks):
            dk_ref[j, 0, :, at] = dk[j].astype(BF)
            dv_ref[j, 0, :, at] = dv[j].astype(BF)

def attend_back(kind, info, queries, q_at, keyed, k_at, valued, v_at, attended, lse, grad, group=1, part=(0, 1)):
    blocks, items, span, _ = keyed.shape
    count = queries.shape[2]
    pairs = HEADS // 2 // part[1]
    skip = part[0] * pairs // group
    lanes = 128 * group
    width = pairs * 128
    row = pl.BlockSpec((1, count, lanes), lambda i, p, s: (i, 0, p + skip))
    out = pl.BlockSpec((1, count, lanes), lambda i, p, s: (i, 0, p))
    key = pl.BlockSpec((blocks, 1, span, lanes), lambda i, p, s: (0, i, 0, p))
    return pl.pallas_call(
        functools.partial(attend_back_kernel, kind),
        out_shape=[jax.ShapeDtypeStruct((items, count, width), BF)] + [jax.ShapeDtypeStruct((blocks, items, span, width), BF)]*2,
        grid_spec=pltpu.PrefetchScalarGridSpec(
            num_scalar_prefetch=1, grid=(items, pairs // group),
            in_specs=[
                pl.BlockSpec((1, 1, count, lanes), lambda i, p, s: (0, i, 0, p + skip + q_at // lanes)),
                pl.BlockSpec((blocks, 1, span, lanes), lambda i, p, s: (0, i, 0, p + skip + k_at // lanes)),
                pl.BlockSpec((blocks, 1, span, lanes), lambda i, p, s: (0, i, 0, p + skip + v_at // lanes)),
                row,
                pl.BlockSpec((1, group, 2, count), lambda i, p, s: (i, p + skip, 0, 0)),
                row,
            ],
            out_specs=[out, key, key]),
        compiler_params=pltpu.CompilerParams(vmem_limit_bytes=VMEM_LIMIT),
        cost_estimate=SHORT,
        name="attend_back",
    )(info, queries, keyed, valued, attended, lse, grad)

def flat(tensor):
    return tensor.reshape(-1, tensor.shape[-1])


def dot_t(left, right):
    return lax.dot_general(
        left, right, (((left.ndim - 1,), (1,)), ((), ())), preferred_element_type=F32
    )


def hop_seq(values, step):
    size = lax.axis_size("seq")
    return hop(values, lambda i: i // size * size + (i % size ^ step))


def body(
    tokens,
    captions,
    caption_lengths,
    cotangent,
    self_gain,
    self_shift,
    self_in_weight,
    self_out_weight,
    cross_gain,
    cross_shift,
    cross_query_weight,
    cross_memory_weight,
    cross_out_weight,
    feed_gain,
    feed_shift,
    up_weight,
    up_bias,
    down_weight,
    down_bias,
):
    features = tokens.shape[2]
    k_bias = up_weight.shape[1] // features
    half = 3 * features // 2
    line = Line()
    tokens_y = hop_seq(tokens, 2)
    ga = Gather(line, [self_in_weight[:, :half]])
    ga.far(line)
    small = line(
        lambda *v: pack_small(list(v[:-1]), v[-1]),
        self_gain, self_shift, cross_gain, cross_shift, feed_gain, feed_shift, down_bias, up_bias,
        whole=True,
    )
    ge = Gather(line, [self_in_weight[:, half:], small])
    ga.first(line)
    ge.far(line)
    ga.near(line)
    ge.first(line)
    tokens_y = line(lambda v: v, tokens_y)
    tokens_3 = hop_seq(tokens_y, 1)
    gb = Gather(line, [self_out_weight, cross_query_weight])
    ga.second(line)
    ge.near(line)
    gb.far(line)
    gf = Gather(line, [cross_memory_weight, cross_out_weight])
    gc = Gather(line, [up_weight])
    ga.pair(line)
    ge.second(line)
    gb.first(line)
    gf.far(line)
    tokens_1 = hop_seq(tokens, 1)
    all_tokens = line(lambda a, b, c, d: jnp.stack([d, b, c, a]), tokens_3, tokens_1, tokens_y, tokens)
    gd = Gather(line, [down_weight])
    ge.pair(line)
    gf.first(line)
    gb.near(line)
    gc.far(line)
    seq_place = lax.axis_index("seq").astype(jnp.int32)[None]

    normed1, queries, key_rows, value_rows, small_full, self_in = line(
        lambda t: project(t, ga.pieces() + ge.pieces()), all_tokens
    )
    up_offset = offset_rows(small_full[7 : 7 + k_bias])
    gd.far(line)
    gc.first(line)
    gf.near(line)
    gb.second(line)
    halves = []
    for i in range(2):
        halves.append(
            line(
                lambda q: attend("causal", seq_place, q, 0, key_rows, 0, value_rows, 0, 2, (i, 2)),
                queries,
            )
        )
        if i == 0:
            gd.first(line)
            gc.near(line)
            gf.second(line)
            gb.pair(line)
    flat_tokens, flat_captions = flat(tokens), flat(captions)
    residual1, normed2, cross_queries, self_out, cross_query = line(
        lambda b, a: mix(flat(a), flat(b), flat_tokens, small_full, gb.pieces()),
        halves[1][0],
        halves[0][0],
    )
    cross_queries = cross_queries.reshape(1, *tokens.shape)
    gd.near(line)
    gc.second(line)
    gf.pair(line)
    attended1 = jnp.concatenate([h[0] for h in halves], axis=2)
    lse1 = jnp.concatenate([h[1] for h in halves], axis=1)

    memory, cross_memory, cross_out = line(lambda c: remember(c, gf.pieces()), flat_captions)
    memory = memory.reshape(1, *captions.shape[:2], -1)
    attended2, lse2 = line(
        lambda q: attend("length", caption_lengths, q, 0, memory, 0, memory, features, 8),
        cross_queries,
    )
    gd.second(line)
    gc.pair(line)

    residual2, normed3, activated, slope, up = line(
        lambda a: up_gelu(flat(a), residual1, cross_out, small_full, up_offset, gc.pieces()),
        attended2,
    )
    low3 = flat(cotangent)
    s1 = Scatter(line, [(activated, low3)])
    gd.pair(line)

    final, grad_before, grad_up_bias, grad_down_bias = line(
        lambda g: down_both(g, slope, activated, residual2, small_full, gd.pieces()), low3
    )
    s1.second(line)
    s2 = Scatter(line, [(normed3, grad_before)])
    grad_second, low2, grad_attended2, grad_feed = line(
        lambda g: feed_back(g, up, residual2, low3, small_full, cross_out), grad_before
    )
    s2.second(line)

    grad_attended2 = grad_attended2.reshape(tokens.shape)
    grad_cq, grad_mk, grad_mv = line(
        lambda g: attend_back(
            "length", caption_lengths, cross_queries, 0, memory, 0, memory, features,
            attended2, lse2, g, 8,
        ),
        grad_attended2,
    )
    s1.near(line)
    grad_cq = flat(grad_cq)
    grad_first, low1, grad_attended1, grad_cross = line(
        lambda g: cross_back(g, cross_query, residual1, grad_second, small_full, self_out), grad_cq
    )
    grad_memory = line(
        lambda k, v: jnp.concatenate([flat(k), flat(v)], axis=-1), grad_mk, grad_mv
    )
    caption_sum = line(lambda a: dot_t(a, cross_memory).astype(BF), grad_memory)
    caption_came = hop_seq(caption_sum, 1)
    s3 = Scatter(
        line,
        [
            (normed2, grad_cq),
            (flat_captions, grad_memory),
            (flat(attended2), low2),
            (flat(attended1), low1),
        ],
    )

    grad_attended1 = grad_attended1.reshape(tokens.shape)
    flat_normed1 = flat(normed1)

    def heads_back(i):
        return line(
            lambda g: attend_back(
                "causal", seq_place, queries, 0, key_rows, 0, value_rows, 0, attended1, lse1, g, 2,
                (i, 2),
            ),
            grad_attended1,
        )

    caption_sum = line(lambda c, v: (wide(c) + wide(v)).astype(BF), caption_came, caption_sum)
    caption_came = hop_seq(caption_sum, 2)
    s2.near(line)
    grads_a = heads_back(0)
    s1.first(line)
    s3.second(line)
    grads_b = heads_back(1)
    own1 = flat_normed1[: low1.shape[0]]
    s4 = Scatter(
        line,
        [
            (own1 if k == 0 else flat_normed1, flat(g))
            for k, pair in enumerate(zip(grads_a, grads_b))
            for g in pair
        ],
    )
    s1.far(line)
    s2.first(line)
    s3.near(line)
    grad_captions = line(lambda c, v: wide(c) + wide(v), caption_came, caption_sum)
    grad_captions = grad_captions.reshape(captions.shape)
    s4.second(line)
    *grad_blocks, small_grads = line(
        lambda g, *o: self_back(
            (g, *o, *grads_b), all_tokens, self_in, grad_cross, grad_feed, grad_down_bias,
            grad_up_bias,
        ),
        *grads_a,
    )
    items = tokens.shape[0]
    grad_blocks = [grad_blocks[k * items : (k + 1) * items] for k in range(4)]
    small = SmallSum(small_grads)
    grad_threes = [hop_seq(v, 1) for v in grad_blocks[3]]
    grad_ones = [hop_seq(v, 1) for v in grad_blocks[1]]
    s3.first(line)
    s4.near(line)
    small.step(line)
    grad_twos = [
        hop_seq(line(lambda a, b: (wide(a) + wide(b)).astype(BF), came, own), 2)
        for came, own in zip(grad_threes, grad_blocks[2])
    ]
    s2.far(line)
    small.step(line)

    def last_norm(i):
        def run(came, one, own, token, residual):
            grad = wide(own) + wide(one) + wide(came)
            unit, inverse = unit_of(wide(token))
            return residual + unit_back(unit, inverse, grad * small_full[0])

        return line(
            run, grad_twos[i], grad_ones[i], grad_blocks[0][i], tokens[i],
            grad_first.reshape(tokens.shape)[i],
        )

    grad_tokens = [last_norm(0)]
    s3.far(line)
    s4.first(line)
    small.step(line)
    grad_tokens += [last_norm(i) for i in range(1, items)]
    grad_tokens = jnp.stack(grad_tokens)
    s4.far(line)
    s2.close(line)
    s3.close(line)
    s1.close(line)
    small_out, grad_bias = small.parts(line, 7)
    s4.close(line)
    (grad_down,) = s1.result(line)
    (grad_up,) = s2.result(line)
    results3 = s3.result(line)
    grad_cross_query, grad_cross_memory, grad_cross_out, grad_self_out = results3
    grads_4 = s4.result(line)
    return (
        final.reshape(tokens.shape),
        grad_tokens,
        grad_captions,
        small_out[0],
        small_out[1],
        jnp.concatenate(grads_4, axis=1),
        grad_self_out,
        small_out[2],
        small_out[3],
        grad_cross_query,
        grad_cross_memory,
        grad_cross_out,
        small_out[4],
        small_out[5],
        grad_up,
        grad_bias,
        grad_down,
        small_out[6],
    )


def solution(mesh):
    tokens_spec = P("dp", "seq", None)
    rows1, rows2 = P(AXES), P(AXES, None)
    return jax.shard_map(
        body,
        mesh=mesh,
        in_specs=(
            tokens_spec, P("dp", None, None), P("dp"), tokens_spec,
            rows1, rows1, rows2, rows2, rows1, rows1, rows2, rows2, rows2,
            rows1, rows1, rows2, rows1, rows2, rows1,
        ),
        out_specs=(
            tokens_spec, tokens_spec, P("dp", None, None),
            rows1, rows1, rows2, rows2, rows1, rows1, rows2, rows2, rows2,
            rows1, rows1, rows2, rows1, rows2, rows1,
        ),
        check_vma=False,
    )
```

```python
import functools
import itertools

import jax
import jax.numpy as jnp
from jax import lax
from jax.experimental import pallas as pl
from jax.experimental.pallas import tpu as pltpu
from jax.sharding import PartitionSpec as P

HEADS = 16
AXES = ("dp", "seq")
BF = jnp.bfloat16
F32 = jnp.float32
epsilon = 1e-05
masked_score = -1e30
VMEM_LIMIT = 34 * 1024 * 1024


def device_count():
    return lax.axis_size("dp") * lax.axis_size("seq")


def place():
    index = lax.axis_index("dp") * lax.axis_size("seq") + lax.axis_index("seq")
    return index


def spots(core):
    index = place()
    c = index % 2
    half = c if core == "own" else 1 - c
    return jnp.stack(
        [half, (index // 4) % 2, (index // 2) % 2, (index // 8) % 2, index // 16]
    ).astype(jnp.int32)


def hop(values, change):
    count = device_count()
    pairs = [(i, change(i)) for i in range(count)]
    return lax.ppermute(values, AXES, pairs)


def hop_core(values):
    return hop(values, lambda i: i ^ 1)


def hop_first(values):
    return hop(values, lambda i: i ^ 4 if i % 2 == 0 else i ^ 2)


def hop_second(values):
    return hop(values, lambda i: i ^ 2 if i % 2 == 0 else i ^ 4)


def hop_z0(values):
    return hop(values, lambda i: i ^ 8)


def hop_z1(values, step):
    return hop(values, lambda i: i ^ (16 * step))


def far_count():
    return device_count() // 16


def column_half(values, half):
    width = values.shape[-1] // 2
    return lax.dynamic_slice_in_dim(values, half * width, width, values.ndim - 1)


def after(value, *others):
    return lax.optimization_barrier((value, *others))[0]


class Line:
    def __init__(self):
        self.last = ()

    def __call__(self, function, first, *rest, whole=False):
        if self.last and whole:
            first, *rest = lax.optimization_barrier((first, *rest, *self.last))[: 1 + len(rest)]
        elif self.last:
            first = after(first, *self.last)
        result = function(first, *rest)
        self.last = jax.tree.leaves(result)[:1]
        return result


class Gather:
    def __init__(self, line, shards):
        c = place() % 2

        def split(*parts):
            return [
                jnp.concatenate([column_half(p, half) for p in parts], axis=1)
                for half in (1 - c, c)
            ]

        other, self.mine = line(split, *shards, whole=True)
        self.came = hop_core(other)

    def far(self, line):
        c = place() % 2
        self.sent = line(
            lambda came, mine: jnp.where(
                c == 0, jnp.concatenate([mine, came]), jnp.concatenate([came, mine])
            ),
            self.came,
            self.mine,
        )
        self.came = [hop_z1(self.sent, k) for k in range(1, far_count())]

    def first(self, line):
        self.sent = line(lambda c, s, *o: jnp.stack([s, *o, c]), self.came[-1], self.sent, *self.came[:-1])
        self.came = hop_first(self.sent)

    def near(self, line):
        self.sent = line(lambda c, s: jnp.stack([s, c]), self.came, self.sent)
        self.came = hop_z0(self.sent)

    def second(self, line):
        self.sent = line(lambda c, s: jnp.stack([s, c]), self.came, self.sent)
        self.came = hop_second(self.sent)
        self.sent_other = hop_core(self.sent)

    def pair(self, line):
        self.came = line(lambda v: v, self.came)
        self.came_other = hop_core(self.came)

    def pieces(self):
        return self.came_other, self.sent, self.came, self.sent_other


def fetch(spot_ref, pieces, targets, sems):
    far_other, near_own, far_own, near_other = pieces
    far, rows = near_own.shape[2], near_own.shape[3]
    c, mx, my, mz0, mz1 = (spot_ref[i] for i in range(5))
    started, start = [], 0
    for k, (target, first, both) in enumerate(targets):
        width = both // 2
        copies = []
        for half, sides in ((c, (near_own, far_own)), (1 - c, (near_other, far_other))):
            column = pl.multiple_of(first + half * width, 128)
            for d4, dz0, d2, dz1 in itertools.product(range(2), range(2), range(2), range(far)):
                x = jnp.where(half == 0, d2, d4) ^ mx
                y = jnp.where(half == 0, d4, d2) ^ my
                z = (dz1 ^ mz1) * 2 + (dz0 ^ mz0)
                row = pl.multiple_of(((z * 2 + x) * 2 + y) * rows, rows)
                copies.append(
                    pltpu.make_async_copy(
                        sides[d4].at[dz0, d2, dz1, :, pl.ds(start, width)],
                        target.at[pl.ds(row, rows), pl.ds(column, width)],
                        sems.at[k],
                    )
                )
        for copy in copies:
            copy.start()
        started.append(copies)
        start += width
    return started


def finish(copies):
    for copy in copies:
        copy.wait()


SHORT = pl.CostEstimate(flops=1, bytes_accessed=1, transcendentals=0)
ANY = pl.BlockSpec(memory_space=pl.ANY)
SMEM = pl.BlockSpec(memory_space=pltpu.SMEM)
VMEM = pl.BlockSpec(memory_space=pltpu.VMEM)


def call(kernel, name, outs, in_specs, out_specs, scratch, grid=()):
    return pl.pallas_call(
        kernel,
        out_shape=outs,
        grid=grid,
        in_specs=in_specs,
        out_specs=out_specs,
        scratch_shapes=scratch,
        compiler_params=pltpu.CompilerParams(vmem_limit_bytes=VMEM_LIMIT - 6 * 1024 * 1024),
        cost_estimate=SHORT,
        name=name,
    )


def shaped(shape, dtype):
    return jax.ShapeDtypeStruct(tuple(shape), dtype)


def kdot(left, right):
    return jnp.dot(left, right, preferred_element_type=F32)


def kdot_t(left, right):
    return lax.dot_general(left, right, (((1,), (1,)), ((), ())), preferred_element_type=F32)


def unit_of(values):
    centered = values - jnp.mean(values, axis=-1, keepdims=True)
    inverse = lax.rsqrt(jnp.mean(centered * centered, axis=-1, keepdims=True) + epsilon)
    return centered * inverse, inverse


def unit_back(unit, inverse, grad_unit):
    return inverse * (
        grad_unit
        - jnp.mean(grad_unit, axis=-1, keepdims=True)
        - unit * jnp.mean(grad_unit * unit, axis=-1, keepdims=True)
    )


def project_kernel(
    spot_ref, token_ref, p0, p1, p2, p3, p4, p5, p6, p7,
    a_ref, q_ref, k_ref, v_ref, small_ref, w_ref, w, packed, vectors, sems, out_sem,
):
    _, items, count, d = token_ref.shape
    kept = pltpu.make_async_copy(w, w_ref, out_sem)

    @pl.when(pl.program_id(0) == 0)
    def _():
        half = 3 * d // 2
        one = fetch(spot_ref, (p0, p1, p2, p3), [(w, 0, half)], sems.at[pl.ds(0, 1)])
        two = fetch(
            spot_ref, (p4, p5, p6, p7), [(w, half, half), (packed, 0, 256)], sems.at[pl.ds(1, 2)]
        )
        finish(two[1])
        vectors[...] = packed[...].astype(F32).T
        small_ref[...] = vectors[0:16, :]
        finish(one[0])
        finish(two[0])
        kept.start()

    unit, _ = unit_of(token_ref[...].reshape(items * count, d).astype(F32))
    normed = (unit * vectors[0:1, :] + vectors[1:2, :]).astype(BF)
    a_ref[...] = normed.reshape(a_ref.shape)
    k_ref[...] = kdot(normed, w[:, d : 2 * d]).astype(BF).reshape(k_ref.shape)
    v_ref[...] = kdot(normed, w[:, 2 * d :]).astype(BF).reshape(v_ref.shape)

    @pl.when(pl.program_id(0) == 0)
    def _():
        q_ref[...] = kdot(normed, w[:, :d]).astype(BF).reshape(q_ref.shape)

    @pl.when(pl.program_id(0) == pl.num_programs(0) - 1)
    def _():
        kept.wait()


def project(tokens, pieces):
    blocks, items, count, d = tokens.shape
    block = pl.BlockSpec((1, items, count, d), lambda b: (b, 0, 0, 0))
    own = pl.BlockSpec((1, items, count, d), lambda b: (0, 0, 0, 0))
    big = shaped(tokens.shape, BF)
    return call(
        project_kernel,
        "project",
        [big, shaped((1, items, count, d), BF), big, big, shaped((16, d), F32), shaped((d, 3 * d), BF)],
        [SMEM, block] + [ANY] * 8,
        [block, own, block, block, pl.BlockSpec((16, d), lambda b: (0, 0)), ANY],
        [
            pltpu.VMEM((d, 3 * d), BF),
            pltpu.VMEM((d, 256), BF),
            pltpu.VMEM((256, d), F32),
            pltpu.SemaphoreType.DMA((3,)),
            pltpu.SemaphoreType.DMA,
        ],
        grid=(blocks,),
    )(spots("own"), tokens, *pieces)


def mix_kernel(
    spot_ref, att0_ref, att1_ref, token_ref, small_ref, p0, p1, p2, p3,
    r_ref, a_ref, cq_ref, wso_ref, wcq_ref, wso, wcq, sems, out_sems,
):
    weights = (wso, wcq)
    groups = fetch(spot_ref, (p0, p1, p2, p3), [(w, 0, w.shape[1]) for w in weights], sems)
    kept = [
        pltpu.make_async_copy(w, out, out_sems.at[i])
        for i, (w, out) in enumerate(zip(weights, (wso_ref, wcq_ref)))
    ]
    finish(groups[0])
    kept[0].start()
    half = att0_ref.shape[1]
    residual = token_ref[...].astype(F32) + (
        kdot(att0_ref[...], wso[:half]) + kdot(att1_ref[...], wso[half:])
    )
    r_ref[...] = residual
    unit, _ = unit_of(residual)
    normed = (unit * small_ref[2:3, :] + small_ref[3:4, :]).astype(BF)
    a_ref[...] = normed
    finish(groups[1])
    kept[1].start()
    cq_ref[...] = kdot(normed, wcq[...]).astype(BF)
    finish(kept)


def mix(attended0, attended1, tokens, small, pieces):
    rows, d = tokens.shape
    return call(
        mix_kernel,
        "mix",
        [shaped((rows, d), F32), shaped((rows, d), BF), shaped((rows, d), BF)]
        + [shaped((d, d), BF)] * 2,
        [SMEM, VMEM, VMEM, VMEM, VMEM] + [ANY] * 4,
        [VMEM] * 3 + [ANY] * 2,
        [pltpu.VMEM((d, d), BF)] * 2
        + [pltpu.SemaphoreType.DMA((2,)), pltpu.SemaphoreType.DMA((2,))],
    )(spots("own"), attended0, attended1, tokens, small, *pieces)


def memory_kernel(
    spot_ref, caption_ref, p0, p1, p2, p3, memory_ref, wcm_ref, wco_ref, wcm, wco, sems, out_sems
):
    weights = (wcm, wco)
    groups = fetch(spot_ref, (p0, p1, p2, p3), [(w, 0, w.shape[1]) for w in weights], sems)
    kept = [
        pltpu.make_async_copy(w, out, out_sems.at[i])
        for i, (w, out) in enumerate(zip(weights, (wcm_ref, wco_ref)))
    ]
    finish(groups[0])
    kept[0].start()
    memory_ref[...] = kdot(caption_ref[...], wcm[...]).astype(BF)
    finish(groups[1])
    kept[1].start()
    finish(kept)


def remember(captions, pieces):
    rows, d = captions.shape
    weights = [(d, 2 * d), (d, d)]
    return call(
        memory_kernel,
        "memory",
        [shaped((rows, 2 * d), BF)] + [shaped(w, BF) for w in weights],
        [SMEM, VMEM] + [ANY] * 4,
        [VMEM] + [ANY] * 2,
        [pltpu.VMEM(w, BF) for w in weights]
        + [pltpu.SemaphoreType.DMA((2,)), pltpu.SemaphoreType.DMA((2,))],
    )(spots("own"), captions, *pieces)


def up_kernel(
    spot_ref, att_ref, r1_ref, wco_ref, small_ref, bias_ref, p0, p1, p2, p3,
    r2_ref, a_ref, act_ref, slope_ref, w_ref, w, sems, out_sem,
):
    n = pl.program_id(0)
    width = act_ref.shape[1]
    kept = pltpu.make_async_copy(w, w_ref, out_sem)

    @pl.when(n == 0)
    def _():
        (copies,) = fetch(spot_ref, (p0, p1, p2, p3), [(w, 0, w.shape[1])], sems)
        residual = r1_ref[...] + kdot(att_ref[...], wco_ref[...])
        r2_ref[...] = residual
        unit, _ = unit_of(residual)
        a_ref[...] = (unit * small_ref[4:5, :] + small_ref[5:6, :]).astype(BF)
        finish(copies)
        kept.start()

    part = w[:, pl.ds(pl.multiple_of(n * width, width), width)]
    before = kdot(a_ref[...], part) + bias_ref[...]
    phi = 0.5 + 0.5 * lax.erf(before * (0.5 ** 0.5))
    act_ref[...] = (before * phi).astype(BF)
    slope_ref[...] = (phi + before * (jnp.exp(-0.5 * before * before) * 0.3989422804014327)).astype(BF)

    @pl.when(n == pl.num_programs(0) - 1)
    def _():
        kept.wait()


def up_gelu(attended, residual, cross_out, small, bias, pieces, block=512):
    rows, d = residual.shape
    hidden = bias.shape[1]
    whole = pl.BlockSpec((rows, d), lambda n: (0, 0))
    column = pl.BlockSpec((rows, block), lambda n: (0, n))
    return call(
        up_kernel,
        "up_gelu",
        [shaped((rows, d), F32), shaped((rows, d), BF)]
        + [shaped((rows, hidden), BF)] * 2
        + [shaped((d, hidden), BF)],
        [
            SMEM, whole, whole, pl.BlockSpec((d, d), lambda n: (0, 0)),
            pl.BlockSpec((16, d), lambda n: (0, 0)), pl.BlockSpec((1, block), lambda n: (0, n)),
            ANY, ANY, ANY, ANY,
        ],
        [whole, whole, column, column, ANY],
        [pltpu.VMEM((d, hidden), BF), pltpu.SemaphoreType.DMA((1,)), pltpu.SemaphoreType.DMA],
        grid=(hidden // block,),
    )(spots("own"), attended, residual, cross_out, small, bias, *pieces)


def down_kernel(
    spot_ref, g_ref, slope_ref, act_ref, r2_ref, small_ref, p0, p1, p2, p3,
    out_ref, grad_ref, bias_ref, down_bias_ref, w, total, sems,
):
    n = pl.program_id(0)
    height = act_ref.shape[1]

    @pl.when(n == 0)
    def _():
        (copies,) = fetch(spot_ref, (p0, p1, p2, p3), [(w, 0, w.shape[1])], sems)
        total[...] = r2_ref[...] + small_ref[6:7, :]
        down_bias_ref[...] = jnp.sum(g_ref[...].astype(F32), axis=0, keepdims=True)
        finish(copies)

    part = w[pl.ds(pl.multiple_of(n * height, height), height), :]
    grad = (kdot_t(g_ref[...], part) * slope_ref[...].astype(F32)).astype(BF)
    grad_ref[...] = grad
    bias_ref[...] = jnp.sum(grad.astype(F32), axis=0, keepdims=True)
    total[...] += kdot(act_ref[...], part)

    @pl.when(n == pl.num_programs(0) - 1)
    def _():
        out_ref[...] = total[...].astype(BF)


def down_both(grad, slope, activated, residual, small, pieces, block=512):
    rows, d = residual.shape
    hidden = slope.shape[1]
    whole = pl.BlockSpec((rows, d), lambda n: (0, 0))
    column = pl.BlockSpec((rows, block), lambda n: (0, n))
    return call(
        down_kernel,
        "down",
        [shaped((rows, d), BF), shaped((rows, hidden), BF), shaped((1, hidden), F32), shaped((1, d), F32)],
        [SMEM, whole, column, column, whole, pl.BlockSpec((16, d), lambda n: (0, 0)), ANY, ANY, ANY, ANY],
        [whole, column, pl.BlockSpec((1, block), lambda n: (0, n)), pl.BlockSpec((1, d), lambda n: (0, 0))],
        [pltpu.VMEM((hidden, d), BF), pltpu.VMEM((rows, d), F32), pltpu.SemaphoreType.DMA((1,))],
        grid=(hidden // block,),
    )(spots("own"), grad, slope, activated, residual, small, *pieces)


def feed_back_kernel(
    g_ref, w_ref, r2_ref, cot_ref, small_ref, wco_ref, dr_ref, low_ref, datt_ref, vec_ref, total
):
    n = pl.program_id(0)

    @pl.when(n == 0)
    def _():
        total[...] = jnp.zeros_like(total)

    total[...] += kdot_t(g_ref[...], w_ref[...])

    @pl.when(n == pl.num_programs(0) - 1)
    def _():
        grad = total[...]
        unit, inverse = unit_of(r2_ref[...])
        vec_ref[0:1, :] = jnp.sum(grad * unit, axis=0, keepdims=True)
        vec_ref[1:2, :] = jnp.sum(grad, axis=0, keepdims=True)
        out = cot_ref[...].astype(F32) + unit_back(unit, inverse, grad * small_ref[4:5, :])
        dr_ref[...] = out
        low = out.astype(BF)
        low_ref[...] = low
        datt_ref[...] = kdot_t(low, wco_ref[...]).astype(BF)


def feed_back(grad, up, residual, cotangent, small, cross_out, block=1024):
    rows, d = residual.shape
    hidden = grad.shape[1]
    whole = pl.BlockSpec((rows, d), lambda n: (0, 0))
    return call(
        feed_back_kernel,
        "feed_back",
        [shaped((rows, d), F32), shaped((rows, d), BF), shaped((rows, d), BF), shaped((8, d), F32)],
        [
            pl.BlockSpec((rows, block), lambda n: (0, n)), pl.BlockSpec((d, block), lambda n: (0, n)),
            whole, whole, pl.BlockSpec((16, d), lambda n: (0, 0)), pl.BlockSpec((d, d), lambda n: (0, 0)),
        ],
        [whole, whole, whole, pl.BlockSpec((8, d), lambda n: (0, 0))],
        [pltpu.VMEM((rows, d), F32)],
        grid=(hidden // block,),
    )(grad, up, residual, cotangent, small, cross_out)


def cross_back_kernel(
    g_ref, wcq_ref, r1_ref, dr2_ref, small_ref, wso_ref, dr_ref, low_ref, datt_ref, vec_ref
):
    grad = kdot_t(g_ref[...], wcq_ref[...])
    unit, inverse = unit_of(r1_ref[...])
    vec_ref[0:1, :] = jnp.sum(grad * unit, axis=0, keepdims=True)
    vec_ref[1:2, :] = jnp.sum(grad, axis=0, keepdims=True)
    out = dr2_ref[...] + unit_back(unit, inverse, grad * small_ref[2:3, :])
    dr_ref[...] = out
    low = out.astype(BF)
    low_ref[...] = low
    datt_ref[...] = kdot_t(low, wso_ref[...]).astype(BF)


def cross_back(grad, cross_query, residual, grad_residual, small, self_out):
    rows, d = residual.shape
    return call(
        cross_back_kernel,
        "cross_back",
        [shaped((rows, d), F32), shaped((rows, d), BF), shaped((rows, d), BF), shaped((8, d), F32)],
        [VMEM] * 6,
        [VMEM] * 4,
        [],
    )(grad, cross_query, residual, grad_residual, small, self_out)


def self_back_kernel(
    dq0_ref, dk0_ref, dv0_ref, dq1_ref, dk1_ref, dv1_ref, token_ref, w_ref,
    cross_ref, feed_ref, down_ref, up_ref, *refs,
):
    *da_refs, vec_ref, own = refs
    b = pl.program_id(0)
    _, items, count, d = token_ref.shape
    half = d // 2

    def back(ref, at):
        return kdot_t(ref[...].reshape(items * count, half), w_ref[:, at : at + half])

    own[...] = (back(dk0_ref, d) + back(dk1_ref, d + half)) + (
        back(dv0_ref, 2 * d) + back(dv1_ref, 2 * d + half)
    )

    @pl.when(b == 0)
    def _():
        own[...] += back(dq0_ref, 0) + back(dq1_ref, half)
        vec_ref[0:2, :] = jnp.zeros((2, d), F32)
        vec_ref[2:4, :] = cross_ref[0:2, :]
        vec_ref[4:6, :] = feed_ref[0:2, :]
        vec_ref[6:7, :] = down_ref[...]
        for k in range(up_ref.shape[1] // d):
            vec_ref[7 + k : 8 + k, :] = up_ref[:, k * d : (k + 1) * d]

    grad = own[...]
    for k in range(len(da_refs) // items):

        @pl.when(b == k)
        def _():
            for i in range(items):
                da_refs[k * items + i][...] = grad[i * count : (i + 1) * count].astype(BF)

    unit, _ = unit_of(token_ref[...].reshape(items * count, d).astype(F32))
    vec_ref[0:1, :] += jnp.sum(grad * unit, axis=0, keepdims=True)
    vec_ref[1:2, :] += jnp.sum(grad, axis=0, keepdims=True)


def self_back(grads, tokens, weight, cross, feed, down, up):
    blocks, items, count, d = tokens.shape
    block = pl.BlockSpec((1, items, count, d), lambda b: (b, 0, 0, 0))
    part = pl.BlockSpec((1, items, count, d // 2), lambda b: (b, 0, 0, 0))

    height = 7 + up.shape[1] // d

    def whole(array):
        return pl.BlockSpec(array.shape, lambda b: (0,) * array.ndim)

    return call(
        self_back_kernel,
        "self_back",
        [shaped((count, d), BF)] * (blocks * items) + [shaped((height, d), F32)],
        [whole(grads[0]), part, part, whole(grads[3]), part, part, block]
        + [whole(a) for a in (weight, cross, feed, down, up)],
        [pl.BlockSpec((count, d), lambda b: (0, 0))] * (blocks * items)
        + [pl.BlockSpec((height, d), lambda b: (0, 0))],
        [pltpu.VMEM((items * count, d), F32)],
        grid=(blocks,),
    )(*grads, tokens, weight, cross, feed, down, up)


def wgrad_kernel(kinds, rows, side, spot_ref, *refs):
    half, mx, my, mz0 = (spot_ref[i] for i in range(4))
    scratch = refs[-1]
    outs = refs[-5:-1] if side == "other" else refs[-3:-1]
    at, start = 0, 0
    for kind in kinds:
        if kind == "dot":
            left, right = refs[at], refs[at + 1]
            at += 2
            block = lax.dot_general(
                left[...], right[...], (((0,), (0,)), ((), ())), preferred_element_type=F32
            )
        else:
            block = refs[at][...].astype(F32)
            at += 1
        scratch[:, start : start + block.shape[1]] = block
        start += block.shape[1]
    for d4, dz0, d2 in itertools.product(range(2), range(2), range(2)):
        x = jnp.where(half == 0, d2, d4) ^ mx
        y = jnp.where(half == 0, d4, d2) ^ my
        j = ((dz0 ^ mz0) * 2 + x) * 2 + y
        part = scratch[pl.ds(pl.multiple_of(j * rows, rows), rows), :]
        if side == "other":
            outs[d4 * 2 + dz0][d2, 0] = part.astype(BF)
        else:
            came = refs[at + d4 * 2 + dz0]
            outs[d4][dz0, d2, 0] = (part + came[d2, 0].astype(F32)).astype(BF)


def wgrad(terms, side, came=None):
    far = far_count()
    kinds = tuple("dot" if len(t) == 2 else "raw" for t in terms)
    height = terms[0][0].shape[1] if kinds[0] == "dot" else terms[0][0].shape[0]
    rows = height // (8 * far)
    specs, args, total = [], [], 0
    for term in terms:
        right = term[-1]
        width = right.shape[1] // 2
        if len(term) == 2:
            left = term[0]
            specs.append(pl.BlockSpec((left.shape[0], 8 * rows), lambda z, s: (0, z)))
            specs.append(pl.BlockSpec((right.shape[0], width), lambda z, s: (0, s[0])))
        else:
            specs.append(pl.BlockSpec((8 * rows, width), lambda z, s: (z, s[0])))
        args += list(term)
        total += width
    piece = pl.BlockSpec((2, 1, rows, total), lambda z, s: (0, z ^ s[4], 0, 0))
    part = pl.BlockSpec((2, 2, 1, rows, total), lambda z, s: (0, 0, z ^ s[4], 0, 0))
    if side == "other":
        out_shape, out_specs = [shaped((2, far, rows, total), BF)] * 4, [piece] * 4
    else:
        specs += [piece] * 4
        args += came
        out_shape, out_specs = [shaped((2, 2, far, rows, total), BF)] * 2, [part] * 2
    return pl.pallas_call(
        functools.partial(wgrad_kernel, kinds, rows, side),
        out_shape=out_shape,
        grid_spec=pltpu.PrefetchScalarGridSpec(
            num_scalar_prefetch=1,
            grid=(far,),
            in_specs=specs,
            out_specs=out_specs,
            scratch_shapes=[pltpu.VMEM((8 * rows, total), F32)],
        ),
        compiler_params=pltpu.CompilerParams(vmem_limit_bytes=VMEM_LIMIT),
        cost_estimate=SHORT,
        name="wgrad",
    )(spots(side), *args)


def wide(values):
    return values.astype(F32)


class Scatter:
    def __init__(self, line, terms):
        self.widths = [t[-1].shape[1] // 2 for t in terms]

        self.terms = terms
        sent = line(lambda f: wgrad([(f, *terms[0][1:]), *terms[1:]], "other"), terms[0][0])
        self.came0 = [hop_core(v) for v in sent]

    def second(self, line):
        self.own, sent = line(lambda *c: wgrad(self.terms, "own", c), *self.came0)
        self.came1 = hop_second(sent)

    def near(self, line):
        def add(c1, o):
            return (wide(o[1]) + wide(c1[1])).astype(BF)

        self.came2 = hop_z0(line(add, self.came1, self.own))

    def first(self, line):
        def add(c2, c1, o):
            return (wide(o[0, 1]) + wide(c1[0, 1]) + wide(c2[1])).astype(BF)

        self.came3 = hop_first(line(add, self.came2, self.came1, self.own))

    def far(self, line):
        def add(c3, c2, c1, o):
            kept = wide(o[0, 0]) + wide(c1[0, 0]) + wide(c2[0]) + wide(c3)
            return kept.astype(BF), kept[0]

        low, self.kept = line(add, self.came3, self.came2, self.came1, self.own)
        self.came4 = [hop_z1(low[k], k) for k in range(1, far_count())]

    def close(self, line):
        total = line(lambda c, t, *o: sum(map(wide, o), t + wide(c)), self.came4[-1], self.kept, *self.came4[:-1])
        rows = total.shape[0] // 2
        c = place() % 2
        self.mine = lax.dynamic_slice_in_dim(total, c * rows, rows, 0)
        self.theirs = hop_core(lax.dynamic_slice_in_dim(total, (1 - c) * rows, rows, 0))

    def result(self, line):
        c = place() % 2

        def join(came, mine):
            left = jnp.where(c == 0, mine, came)
            right = jnp.where(c == 0, came, mine)
            results, start = [], 0
            for width in self.widths:
                at = slice(start, start + width)
                results.append(jnp.concatenate([left[:, at], right[:, at]], axis=1))
                start += width
            return results

        return line(join, self.theirs, self.mine)


def pack_small(vectors, bias):
    r = vectors[0].shape[0]
    k = bias.shape[0] // r
    rows = jnp.concatenate([jnp.stack(vectors), bias.reshape(k, r)])
    return jnp.pad(rows.T, ((0, 0), (0, 256 - rows.shape[0])))


def offset_rows(rows):
    k, d = rows.shape
    n = device_count()
    return rows.reshape(k, n, d // n).transpose(1, 0, 2).reshape(1, k * d)


class SmallSum:
    def __init__(self, values):
        self.values = values
        far = 16
        self.distances = [1, 4]
        while far < device_count():
            self.distances.append(far)
            far *= 2
        self.distances += [8, 2]
        self.send()

    def send(self):
        distance = self.distances.pop(0)
        self.came = hop(self.values, lambda i: i ^ distance)

    def step(self, line):
        self.values = line(lambda c, v: c + v, self.came, self.values)
        if self.distances:
            self.send()
            return True
        return False

    def parts(self, line, count):
        while self.step(line):
            pass
        rows = self.values
        n = device_count()
        part = rows.shape[1] // n
        own = lax.dynamic_slice_in_dim(rows[:count], place() * part, part, 1)
        long = rows[count:].reshape(-1)
        share = long.shape[0] // n
        return own, lax.dynamic_slice_in_dim(long, place() * share, share)


def shifts(info_ref, kind, block):
    if kind == "length" or block == 0:
        return None
    me = info_ref[0]
    return jnp.where((me ^ block) < me, 0.0, -masked_score).astype(F32)

def allowed_keys(info_ref, kind, item, span, count):
    shape = (span, count)
    row = lax.broadcasted_iota(jnp.int32, shape, 0)
    if kind == "length":
        return row < info_ref[item]
    return row <= lax.broadcasted_iota(jnp.int32, shape, 1)

def attend_kernel(kind, info_ref, q_ref, k_ref, v_ref, o_ref, lse_ref):
    blocks, _, span, wide_lanes = k_ref.shape
    count = q_ref.shape[2]
    lanes = 128
    head = lanes // 2
    low_lane = lax.broadcasted_iota(jnp.int32, (count, lanes), 1) < head
    allowed = allowed_keys(info_ref, kind, pl.program_id(0), span, count)
    outside = [shifts(info_ref, kind, j) for j in range(blocks)]
    for pair in range(wide_lanes // lanes):
        at = slice(pair * lanes, (pair + 1) * lanes)
        values_t = v_ref[:, :, :, at].reshape(blocks * span, lanes).T
        queries = q_ref[0, 0, :, at] * (head ** -0.5)
        outs = []
        for h in range(2):
            mine = jnp.where(low_lane if h == 0 else ~low_lane, queries, 0).astype(BF)
            scores = [
                lax.dot_general(k_ref[j, 0, :, at], mine, (((1,), (1,)), ((), ())), preferred_element_type=F32)
                for j in range(blocks)
            ]
            scores[0] = jnp.where(allowed, scores[0], masked_score)
            top = jnp.max(scores[0], axis=0, keepdims=True)
            for j in range(1, blocks):
                top = jnp.maximum(top, jnp.max(scores[j], axis=0, keepdims=True) - outside[j])
            soft = [jnp.exp(scores[0] - top)]
            soft += [jnp.exp(scores[j] - (top + outside[j])) for j in range(1, blocks)]
            total = sum(jnp.sum(s, axis=0, keepdims=True) for s in soft)
            lse_ref[0, pair, h : h + 1, :] = top + jnp.log(total)
            low = jnp.concatenate([s.astype(BF) for s in soft], axis=0)
            out = jnp.dot(values_t[h * head : (h + 1) * head], low, preferred_element_type=F32)
            outs.append(out / total)
        o_ref[0, :, at] = jnp.concatenate(outs, axis=0).T.astype(BF)

def attend(kind, info, queries, q_at, keyed, k_at, valued, v_at, group=1, part=(0, 1)):
    blocks, items, span, _ = keyed.shape
    count = queries.shape[2]
    pairs = HEADS // 2 // part[1]
    skip = part[0] * pairs // group
    lanes = 128 * group
    width = pairs * 128
    return pl.pallas_call(
        functools.partial(attend_kernel, kind),
        out_shape=[jax.ShapeDtypeStruct((items, count, width), BF), jax.ShapeDtypeStruct((items, pairs, 2, count), F32)],
        grid_spec=pltpu.PrefetchScalarGridSpec(
            num_scalar_prefetch=1, grid=(items, pairs // group),
            in_specs=[
                pl.BlockSpec((1, 1, count, lanes), lambda i, p, s: (0, i, 0, p + skip + q_at // lanes)),
                pl.BlockSpec((blocks, 1, span, lanes), lambda i, p, s: (0, i, 0, p + skip + k_at // lanes)),
                pl.BlockSpec((blocks, 1, span, lanes), lambda i, p, s: (0, i, 0, p + skip + v_at // lanes)),
            ],
            out_specs=[
                pl.BlockSpec((1, count, lanes), lambda i, p, s: (i, 0, p)),
                pl.BlockSpec((1, group, 2, count), lambda i, p, s: (i, p, 0, 0)),
            ]),
        compiler_params=pltpu.CompilerParams(vmem_limit_bytes=VMEM_LIMIT - 12 * 1024 * 1024),
        cost_estimate=SHORT,
        name="attend",
    )(info, queries, keyed, valued)

def attend_back_kernel(kind, info_ref, q_ref, k_ref, v_ref, o_ref, lse_ref, do_ref, dq_ref, dk_ref, dv_ref):
    blocks, _, span, wide_lanes = k_ref.shape
    count = q_ref.shape[2]
    lanes = 128
    head = lanes // 2
    scaling = head ** -0.5
    low_lane = lax.broadcasted_iota(jnp.int32, (count, lanes), 1) < head
    allowed = allowed_keys(info_ref, kind, pl.program_id(0), span, count)
    outside = [shifts(info_ref, kind, j) for j in range(blocks)]
    for pair in range(wide_lanes // lanes):
        at = slice(pair * lanes, (pair + 1) * lanes)
        keys_t = k_ref[:, :, :, at].reshape(blocks * span, lanes).T
        queries = q_ref[0, 0, :, at] * scaling
        grad = do_ref[0, :, at]
        product_t = (grad.astype(F32) * o_ref[0, :, at].astype(F32)).T
        grad_q, dk, dv = [], [0.0] * blocks, [0.0] * blocks
        for h in range(2):
            lane = low_lane if h == 0 else ~low_lane
            mine = jnp.where(lane, queries, 0).astype(BF)
            grad_mine = jnp.where(lane, grad, 0).astype(BF)
            lse = lse_ref[0, pair, h : h + 1, :]
            delta = jnp.sum(product_t[h * head : (h + 1) * head], axis=0, keepdims=True)
            grads = []
            for j in range(blocks):
                scores = lax.dot_general(k_ref[j, 0, :, at], mine, (((1,), (1,)), ((), ())), preferred_element_type=F32)
                if j == 0:
                    soft = jnp.where(allowed, jnp.exp(scores - lse), 0.0)
                else:
                    soft = jnp.exp(scores - (lse + outside[j]))
                grad_soft = lax.dot_general(v_ref[j, 0, :, at], grad_mine, (((1,), (1,)), ((), ())), preferred_element_type=F32)
                grads.append((soft * (grad_soft - delta)).astype(BF))
                dv[j] += jnp.dot(soft.astype(BF), grad_mine, preferred_element_type=F32)
                dk[j] += jnp.dot(grads[j], mine, preferred_element_type=F32)
            grad_scores = jnp.concatenate(grads, axis=0)
            grad_q.append(jnp.dot(keys_t[h * head : (h + 1) * head], grad_scores, preferred_element_type=F32))
        dq_ref[0, :, at] = (jnp.concatenate(grad_q, axis=0) * scaling).T.astype(BF)
        for j in range(blocks):
            dk_ref[j, 0, :, at] = dk[j].astype(BF)
            dv_ref[j, 0, :, at] = dv[j].astype(BF)

def attend_back(kind, info, queries, q_at, keyed, k_at, valued, v_at, attended, lse, grad, group=1, part=(0, 1)):
    blocks, items, span, _ = keyed.shape
    count = queries.shape[2]
    pairs = HEADS // 2 // part[1]
    skip = part[0] * pairs // group
    lanes = 128 * group
    width = pairs * 128
    row = pl.BlockSpec((1, count, lanes), lambda i, p, s: (i, 0, p + skip))
    out = pl.BlockSpec((1, count, lanes), lambda i, p, s: (i, 0, p))
    key = pl.BlockSpec((blocks, 1, span, lanes), lambda i, p, s: (0, i, 0, p))
    return pl.pallas_call(
        functools.partial(attend_back_kernel, kind),
        out_shape=[jax.ShapeDtypeStruct((items, count, width), BF)] + [jax.ShapeDtypeStruct((blocks, items, span, width), BF)]*2,
        grid_spec=pltpu.PrefetchScalarGridSpec(
            num_scalar_prefetch=1, grid=(items, pairs // group),
            in_specs=[
                pl.BlockSpec((1, 1, count, lanes), lambda i, p, s: (0, i, 0, p + skip + q_at // lanes)),
                pl.BlockSpec((blocks, 1, span, lanes), lambda i, p, s: (0, i, 0, p + skip + k_at // lanes)),
                pl.BlockSpec((blocks, 1, span, lanes), lambda i, p, s: (0, i, 0, p + skip + v_at // lanes)),
                row,
                pl.BlockSpec((1, group, 2, count), lambda i, p, s: (i, p + skip, 0, 0)),
                row,
            ],
            out_specs=[out, key, key]),
        compiler_params=pltpu.CompilerParams(vmem_limit_bytes=VMEM_LIMIT - 12 * 1024 * 1024),
        cost_estimate=SHORT,
        name="attend_back",
    )(info, queries, keyed, valued, attended, lse, grad)

def flat(tensor):
    return tensor.reshape(-1, tensor.shape[-1])


def dot_t(left, right):
    return lax.dot_general(
        left, right, (((left.ndim - 1,), (1,)), ((), ())), preferred_element_type=F32
    )


def hop_seq(values, step):
    size = lax.axis_size("seq")
    return hop(values, lambda i: i // size * size + (i % size ^ step))


def body(
    tokens,
    captions,
    caption_lengths,
    cotangent,
    self_gain,
    self_shift,
    self_in_weight,
    self_out_weight,
    cross_gain,
    cross_shift,
    cross_query_weight,
    cross_memory_weight,
    cross_out_weight,
    feed_gain,
    feed_shift,
    up_weight,
    up_bias,
    down_weight,
    down_bias,
):
    features = tokens.shape[2]
    k_bias = up_weight.shape[1] // features
    half = 3 * features // 2
    line = Line()
    tokens_y = hop_seq(tokens, 2)
    ga = Gather(line, [self_in_weight[:, :half]])
    ga.far(line)
    small = line(
        lambda *v: pack_small(list(v[:-1]), v[-1]),
        self_gain, self_shift, cross_gain, cross_shift, feed_gain, feed_shift, down_bias, up_bias,
        whole=True,
    )
    ge = Gather(line, [self_in_weight[:, half:], small])
    ga.first(line)
    ge.far(line)
    ga.near(line)
    ge.first(line)
    tokens_y = line(lambda v: v, tokens_y)
    tokens_3 = hop_seq(tokens_y, 1)
    gb = Gather(line, [self_out_weight, cross_query_weight])
    ga.second(line)
    ge.near(line)
    gb.far(line)
    gf = Gather(line, [cross_memory_weight, cross_out_weight])
    gc = Gather(line, [up_weight])
    ga.pair(line)
    ge.second(line)
    gb.first(line)
    gf.far(line)
    tokens_1 = hop_seq(tokens, 1)
    all_tokens = line(lambda a, b, c, d: jnp.stack([d, b, c, a]), tokens_3, tokens_1, tokens_y, tokens)
    gd = Gather(line, [down_weight])
    ge.pair(line)
    gf.first(line)
    gb.near(line)
    gc.far(line)
    seq_place = lax.axis_index("seq").astype(jnp.int32)[None]

    normed1, queries, key_rows, value_rows, small_full, self_in = line(
        lambda t: project(t, ga.pieces() + ge.pieces()), all_tokens
    )
    up_offset = offset_rows(small_full[7 : 7 + k_bias])
    gd.far(line)
    gc.first(line)
    gf.near(line)
    gb.second(line)
    halves = []
    for i in range(2):
        halves.append(
            line(
                lambda q: attend("causal", seq_place, q, 0, key_rows, 0, value_rows, 0, 2, (i, 2)),
                queries,
            )
        )
        if i == 0:
            gd.first(line)
            gc.near(line)
            gf.second(line)
            gb.pair(line)
    flat_tokens, flat_captions = flat(tokens), flat(captions)
    residual1, normed2, cross_queries, self_out, cross_query = line(
        lambda b, a: mix(flat(a), flat(b), flat_tokens, small_full, gb.pieces()),
        halves[1][0],
        halves[0][0],
    )
    cross_queries = cross_queries.reshape(1, *tokens.shape)
    gd.near(line)
    gc.second(line)
    gf.pair(line)
    attended1 = jnp.concatenate([h[0] for h in halves], axis=2)
    lse1 = jnp.concatenate([h[1] for h in halves], axis=1)

    memory, cross_memory, cross_out = line(lambda c: remember(c, gf.pieces()), flat_captions)
    memory = memory.reshape(1, *captions.shape[:2], -1)
    attended2, lse2 = line(
        lambda q: attend("length", caption_lengths, q, 0, memory, 0, memory, features, 8),
        cross_queries,
    )
    gd.second(line)
    gc.pair(line)

    residual2, normed3, activated, slope, up = line(
        lambda a: up_gelu(flat(a), residual1, cross_out, small_full, up_offset, gc.pieces()),
        attended2,
    )
    low3 = flat(cotangent)
    s1 = Scatter(line, [(activated, low3)])
    gd.pair(line)

    final, grad_before, grad_up_bias, grad_down_bias = line(
        lambda g: down_both(g, slope, activated, residual2, small_full, gd.pieces()), low3
    )
    s1.second(line)
    s2 = Scatter(line, [(normed3, grad_before)])
    grad_second, low2, grad_attended2, grad_feed = line(
        lambda g: feed_back(g, up, residual2, low3, small_full, cross_out), grad_before
    )
    s2.second(line)

    grad_attended2 = grad_attended2.reshape(tokens.shape)
    grad_cq, grad_mk, grad_mv = line(
        lambda g: attend_back(
            "length", caption_lengths, cross_queries, 0, memory, 0, memory, features,
            attended2, lse2, g, 8,
        ),
        grad_attended2,
    )
    s1.near(line)
    grad_cq = flat(grad_cq)
    grad_first, low1, grad_attended1, grad_cross = line(
        lambda g: cross_back(g, cross_query, residual1, grad_second, small_full, self_out), grad_cq
    )
    grad_memory = line(
        lambda k, v: jnp.concatenate([flat(k), flat(v)], axis=-1), grad_mk, grad_mv
    )
    caption_sum = line(lambda a: dot_t(a, cross_memory).astype(BF), grad_memory)
    caption_came = hop_seq(caption_sum, 1)
    s3 = Scatter(
        line,
        [
            (normed2, grad_cq),
            (flat_captions, grad_memory),
            (flat(attended2), low2),
            (flat(attended1), low1),
        ],
    )

    grad_attended1 = grad_attended1.reshape(tokens.shape)
    flat_normed1 = flat(normed1)

    def heads_back(i):
        return line(
            lambda g: attend_back(
                "causal", seq_place, queries, 0, key_rows, 0, value_rows, 0, attended1, lse1, g, 2,
                (i, 2),
            ),
            grad_attended1,
        )

    caption_sum = line(lambda c, v: (wide(c) + wide(v)).astype(BF), caption_came, caption_sum)
    caption_came = hop_seq(caption_sum, 2)
    s2.near(line)
    grads_a = heads_back(0)
    s1.first(line)
    s3.second(line)
    grads_b = heads_back(1)
    own1 = flat_normed1[: low1.shape[0]]
    s4 = Scatter(
        line,
        [
            (own1 if k == 0 else flat_normed1, flat(g))
            for k, pair in enumerate(zip(grads_a, grads_b))
            for g in pair
        ],
    )
    s1.far(line)
    s2.first(line)
    s3.near(line)
    grad_captions = line(lambda c, v: wide(c) + wide(v), caption_came, caption_sum)
    grad_captions = grad_captions.reshape(captions.shape)
    s4.second(line)
    *grad_blocks, small_grads = line(
        lambda g, *o: self_back(
            (g, *o, *grads_b), all_tokens, self_in, grad_cross, grad_feed, grad_down_bias,
            grad_up_bias,
        ),
        *grads_a,
    )
    items = tokens.shape[0]
    grad_blocks = [grad_blocks[k * items : (k + 1) * items] for k in range(4)]
    small = SmallSum(small_grads)
    grad_threes = [hop_seq(v, 1) for v in grad_blocks[3]]
    grad_ones = [hop_seq(v, 1) for v in grad_blocks[1]]
    s3.first(line)
    s4.near(line)
    small.step(line)
    grad_twos = [
        hop_seq(line(lambda a, b: (wide(a) + wide(b)).astype(BF), came, own), 2)
        for came, own in zip(grad_threes, grad_blocks[2])
    ]
    s2.far(line)
    small.step(line)

    def last_norm(i):
        def run(came, one, own, token, residual):
            grad = wide(own) + wide(one) + wide(came)
            unit, inverse = unit_of(wide(token))
            return residual + unit_back(unit, inverse, grad * small_full[0])

        return line(
            run, grad_twos[i], grad_ones[i], grad_blocks[0][i], tokens[i],
            grad_first.reshape(tokens.shape)[i],
        )

    grad_tokens = [last_norm(0)]
    s3.far(line)
    s4.first(line)
    small.step(line)
    grad_tokens += [last_norm(i) for i in range(1, items)]
    grad_tokens = jnp.stack(grad_tokens)
    s4.far(line)
    s2.close(line)
    s3.close(line)
    s1.close(line)
    small_out, grad_bias = small.parts(line, 7)
    s4.close(line)
    (grad_down,) = s1.result(line)
    (grad_up,) = s2.result(line)
    results3 = s3.result(line)
    grad_cross_query, grad_cross_memory, grad_cross_out, grad_self_out = results3
    grads_4 = s4.result(line)
    return (
        final.reshape(tokens.shape),
        grad_tokens,
        grad_captions,
        small_out[0],
        small_out[1],
        jnp.concatenate(grads_4, axis=1),
        grad_self_out,
        small_out[2],
        small_out[3],
        grad_cross_query,
        grad_cross_memory,
        grad_cross_out,
        small_out[4],
        small_out[5],
        grad_up,
        grad_bias,
        grad_down,
        small_out[6],
    )


def solution(mesh):
    tokens_spec = P("dp", "seq", None)
    rows1, rows2 = P(AXES), P(AXES, None)
    return jax.shard_map(
        body,
        mesh=mesh,
        in_specs=(
            tokens_spec, P("dp", None, None), P("dp"), tokens_spec,
            rows1, rows1, rows2, rows2, rows1, rows1, rows2, rows2, rows2,
            rows1, rows1, rows2, rows1, rows2, rows1,
        ),
        out_specs=(
            tokens_spec, tokens_spec, P("dp", None, None),
            rows1, rows1, rows2, rows2, rows1, rows1, rows2, rows2, rows2,
            rows1, rows1, rows2, rows1, rows2, rows1,
        ),
        check_vma=False,
    )
```
